512 devices in a mesh: col: 16 (over z_lo, x), slab: 32 (over y, z_hi, core).
Axes of the slice: x: 4, y: 4, z: 16 (z_hi: 4, z_lo: 4; z = z_hi * 4 + z_lo), core: 2. Of those that a mesh axis runs over, the one named last changes fastest.
Arguments:
- p_star: float32 [128, 256, 256], P('col', 'slab'), may hold values from 0 to 3
- u_star: float32 [128, 256, 256], P('col', 'slab'), may hold values from -6 to 6
- v_star: float32 [128, 256, 256], P('col', 'slab'), may hold values from -6 to 6
- w_star: float32 [128, 256, 256], P('col', 'slab'), may hold values from -6 to 6
- flags: int32 [128, 256, 256], P('col', 'slab'), may hold values from 0 to 2
- panel_cell: int32 [131072], P(('col', 'slab')), may hold values from 0 to 16383
- panel_section: int32 [131072], P(('col', 'slab')), may hold values from 0 to 127, as said below
- panel_geom: float32 [3, 131072], P(None, ('col', 'slab')), may hold values from -0.12 to 0.12
Outputs:
- pressure: float32 [128, 256, 256], P('col', 'slab')
- vertical_velocity: float32 [128, 256, 256], P('col', 'slab')
- section_loads: float32 [3, 128], P(None, 'slab')
The draws below stay inside these ranges and needn't reach their ends.
Inputs may be any that keep to these rules, and one draw needn't show every extreme that they name: `panel_section`: panel i belongs to the block of device i // 256, devices counted with col slowest; with s that device's slab index, its section lies between 4 * s - 2 and 4 * s + 5.
All inputs are finite; a program needn't handle non-finite values.
Results may differ from the reference program's by a relative error of at most 0.0014.
Values sent between devices are 32-bit elements; how exact they have to be, the bound alone decides.
No kernel may reach another device: no remote copies, remote signals or barrier semaphores. Data moves between devices by JAX's collectives and lax.ppermute only.
A program may use at most 64 MiB of HBM per device.

```python
import jax
import jax.numpy as jnp
from jax import lax

CZ = 8
CX = 8
NY = 256
PANELS_DEV = 256
SEC_DEV = 4
EOS_ITERS = 3
NZ = 128
NX = 256
PANELS = 131072
SECTIONS = 128
N_SLAB = 32


def draw_panel_section(key, part):
    key = jax.random.fold_in(key, 3)
    panel_ids = jnp.arange(PANELS, dtype=jnp.int32)
    position = panel_ids % PANELS_DEV
    owner = panel_ids // PANELS_DEV % (SECTIONS // SEC_DEV)
    offset = jax.random.randint(key, (PANELS,), -2, SEC_DEV + 2, dtype=jnp.int32)
    offset = jnp.where(position == 0, -2, offset)
    offset = jnp.where(position == PANELS_DEV - 1, SEC_DEV + 1, offset)
    return jnp.clip(owner * SEC_DEV + offset, 0, SECTIONS - 1).astype(jnp.int32)


def draw_flags(key, part):
    key = jax.random.fold_in(key, 5)
    rolled = jax.random.randint(key, (NZ, NX, NY), 0, 100, dtype=jnp.int32)
    liquid_or_air = jnp.where(rolled < 97, jnp.int32(1), jnp.int32(2))
    return jnp.where(rolled < 94, jnp.int32(0), liquid_or_air).astype(jnp.int32)


def draw_p_star(key, part):
    key = jax.random.fold_in(key, 7)
    cell_key = jax.random.fold_in(key, 0)
    uniform_cell = jax.random.uniform(cell_key, (NZ, NX, NY), jnp.float32, 0.0, 1.0)
    values = 3.0 * (1.0 - uniform_cell * uniform_cell * uniform_cell)
    return values.astype(jnp.float32)


def with_ends(entries, stream_key, low, largest):
    extent = entries.shape
    spot = [jax.random.randint(jax.random.fold_in(stream_key, axis), (), 0, extent[axis]) for axis in range(len(extent))]
    entries = entries.at[tuple(spot)].set(low)
    longest = extent.index(max(extent))
    spot[longest] = (spot[longest] + 1) % extent[longest]
    return entries.at[tuple(spot)].set(largest)


def levels(own_key, extent, cuts, low, high):
    def one(dim, parts):
        steps = jax.random.uniform(jax.random.fold_in(jax.random.fold_in(own_key, 6), dim), (parts,), jnp.float32, low / len(cuts), high / len(cuts))
        return jnp.repeat(jnp.exp(steps), extent[dim] // parts).reshape((-1,) + (1,) * (len(extent) - dim - 1))

    loudness = one(*cuts[0])
    for cut in cuts[1:]:
        loudness = loudness * one(*cut)
    return loudness


def centred(stream_key, extent, width, most, cuts=(), kind=jnp.bfloat16):
    entries = jax.random.normal(stream_key, extent, jnp.float32) * width
    if len(cuts) > 0:
        entries = levels(stream_key, extent, cuts, -0.22, 0.18) * entries
    return jnp.clip(entries, min=-most, max=most).astype(kind)


def setup_inputs(seed: int = 0) -> dict:
    arg_keys = jax.random.split(jax.random.key(seed), 9)
    return {
        "p_star": draw_p_star(jax.random.fold_in(arg_keys[8], 71), 0),
        "u_star": centred(arg_keys[1], (NZ, NX, NY), 1.0, 6.0, ((0, 16), (1, 32)), jnp.float32),
        "v_star": centred(arg_keys[2], (NZ, NX, NY), 1.0, 6.0, ((0, 16), (1, 32)), jnp.float32),
        "w_star": centred(arg_keys[3], (NZ, NX, NY), 1.0, 6.0, ((0, 16), (1, 32)), jnp.float32),
        "flags": draw_flags(jax.random.fold_in(arg_keys[8], 71), 0),
        "panel_cell": with_ends(jax.random.randint(arg_keys[5], (PANELS,), 0, CZ * CX * NY), jax.random.fold_in(arg_keys[5], 1), 0, (CZ * CX * NY) - 1).astype(jnp.int32),
        "panel_section": draw_panel_section(jax.random.fold_in(arg_keys[8], 71), 0),
        "panel_geom": centred(arg_keys[7], (3, PANELS), 0.02, 0.12, ((1, 512),), jnp.float32),
    }


KAPPA_SCALE = 0.01
AIR_DENSITY = 0.1
GAMMA_HORIZ = 0.001
DIVERGENCE_SCALE = 0.005


def equation_of_state(p_star, flags):
    air_frac = jnp.where(flags == 1, jnp.float32(1.0), jnp.where(flags == 2, jnp.float32(0.5), jnp.float32(0.0)))
    water_density = jnp.ones_like(p_star)
    for newton in range(EOS_ITERS):
        square_term = water_density * water_density
        cube_term = square_term * water_density
        sixth_power = cube_term * cube_term
        seventh_power = sixth_power * water_density
        water_density = water_density - (seventh_power - 1.0 - p_star) / (7.0 * sixth_power)
    shifted = 1.0 + p_star
    air_density = AIR_DENSITY * jnp.power(shifted, 1.0 / 1.4)
    density = air_frac * air_density + (1.0 - air_frac) * water_density
    compress_coef = KAPPA_SCALE * (air_frac / (1.4 * shifted) + (1.0 - air_frac) / (7.0 * shifted))
    return density, compress_coef


def tridiagonal(sub_band, diagonal, super_band, source):
    def forward_step(current, coeffs):
        ratio_prev, shift_prev = current
        sub_row, diag_row, super_row, source_row = coeffs
        pivot_value = diag_row - sub_row * ratio_prev
        ratio_row = super_row / pivot_value
        shift_row = (source_row - sub_row * shift_prev) / pivot_value
        return (ratio_row, shift_row), (ratio_row, shift_row)

    zero_row = jnp.zeros_like(diagonal[0])
    finals, (ratios, shifts) = lax.scan(forward_step, (zero_row, zero_row), (sub_band, diagonal, super_band, source))

    def back_step(following, coeffs):
        ratio_row, shift_row = coeffs
        value_row = shift_row - ratio_row * following
        return value_row, value_row

    last_value, solution = lax.scan(back_step, zero_row, (ratios, shifts), reverse=True)
    return solution


def reference(p_star, u_star, v_star, w_star, flags, panel_cell, panel_section, panel_geom):
    density, compress_coef = equation_of_state(p_star, flags)
    pad_x = jnp.pad(p_star, ((0, 0), (1, 1), (0, 0)))
    pad_y = jnp.pad(p_star, ((0, 0), (0, 0), (1, 1)))
    laplacian = pad_x[:, 2:] + pad_x[:, :-2] + pad_y[:, :, 2:] + pad_y[:, :, :-2] - 4.0 * p_star
    u_pad = jnp.pad(u_star, ((0, 0), (1, 1), (0, 0)))
    v_pad = jnp.pad(v_star, ((0, 0), (0, 0), (1, 1)))
    w_pad = jnp.pad(w_star, ((1, 1), (0, 0), (0, 0)))
    divergence = (u_pad[:, 2:] - u_pad[:, :-2]) * 0.5 + (v_pad[:, :, 2:] - v_pad[:, :, :-2]) * 0.5 + (w_pad[2:] - w_pad[:-2]) * 0.5
    source = compress_coef * p_star + GAMMA_HORIZ * laplacian - DIVERGENCE_SCALE * divergence
    face_coef = 2.0 / (density[:-1] + density[1:])
    zero_plane = jnp.zeros_like(density[:1])
    lower_face = jnp.concatenate([zero_plane, face_coef], 0)
    upper_face = jnp.concatenate([face_coef, zero_plane], 0)
    diagonal = compress_coef + lower_face + upper_face
    pressure = tridiagonal(-lower_face, diagonal, -upper_face, source)
    above = jnp.concatenate([pressure[1:], zero_plane], 0)
    below = jnp.concatenate([zero_plane, pressure[:-1]], 0)
    vertical_velocity = w_star - 0.5 * (upper_face * (above - pressure) + lower_face * (pressure - below))
    panel_ids = jnp.arange(PANELS, dtype=jnp.int32)
    block_id = panel_ids // PANELS_DEV
    col_block = block_id // N_SLAB
    slab_block = block_id % N_SLAB
    depth_idx = panel_cell // (CX * NY)
    across_idx = (panel_cell // NY) % CX
    span_idx = panel_cell % NY
    sampled = pressure[col_block * CZ + depth_idx, slab_block * CX + across_idx, span_idx]
    section_loads = jnp.stack([jax.ops.segment_sum(panel_geom[component] * sampled, panel_section, num_segments=SECTIONS) for component in range(3)])
    return pressure, vertical_velocity, section_loads
```

```python
import functools

import jax
import jax.numpy as jnp
from jax import lax
from jax.experimental import pallas as pl
from jax.experimental.pallas import tpu as pltpu
from jax.sharding import PartitionSpec as P

SEC_DEV = 4
EOS_ITERS = 3
KAPPA_SCALE = 0.01
AIR_DENSITY = 0.1
GAMMA_HORIZ = 0.001
DIVERGENCE_SCALE = 0.005
HALF_DIV = 0.5 * DIVERGENCE_SCALE

CZ = 8
CX = 8
NY = 256
LANES = 128
COLS = 16
PANELS_DEV = 256
REACH = 2
SEND_ROWS = 24
BACK_ROWS = 8

F32 = jnp.float32


def row_iota(shape):
    return lax.broadcasted_iota(jnp.int32, shape, 0)


def lane_iota(shape):
    return lax.broadcasted_iota(jnp.int32, shape, 1)


def level(ref, z):
    return ref[z * CX : (z + 1) * CX, :]


def split_three(x):
    high = x.astype(jnp.bfloat16)
    rest = x - high.astype(F32)
    middle = rest.astype(jnp.bfloat16)
    low = (rest - middle.astype(F32)).astype(jnp.bfloat16)
    return high, middle, low


def pick(fields, onehot, row_mask):
    total = None
    for part in split_three(fields):
        term = jnp.dot(part, onehot, preferred_element_type=F32)
        total = term if total is None else total + term
    return jnp.sum(jnp.where(row_mask, total, 0.0), axis=0, keepdims=True)


def panel_masks(cell):
    onehot = (row_iota((NY, PANELS_DEV)) == (cell & (NY - 1))).astype(F32)
    row_mask = row_iota((CZ * CX, PANELS_DEV)) == (cell >> 8)
    return onehot.astype(jnp.bfloat16), row_mask


def condense(ground, edges):
    first, here, link = ground[0], ground[1], edges[0]
    to_first, to_next, inverse = [], [], []
    for j in range(1, len(ground) - 1):
        edge = edges[j]
        inv = 1.0 / (here + link + edge)
        a, b = link * inv, edge * inv
        first = first + a * here
        here = ground[j + 1] + b * here
        link = link * b
        to_first.append(a)
        to_next.append(b)
        inverse.append(inv)
    return first, here, link, to_first, to_next, inverse


def condense_source(source, to_first, to_next, inverse):
    first, here = source[0], source[1]
    offsets = []
    for j in range(1, len(source) - 1):
        a, b = to_first[j - 1], to_next[j - 1]
        offsets.append(here * inverse[j - 1])
        first = first + a * here
        here = source[j + 1] + b * here
    return first, here, offsets


def expand(first, last, to_first, to_next, offsets):
    values = [last]
    for a, b, offset in zip(reversed(to_first), reversed(to_next), reversed(offsets)):
        values.append(offset + a * first + b * values[-1])
    values.append(first)
    return values[::-1]


def section_rows(terms):
    rows = []
    for term in terms:
        sums = jnp.sum(term, axis=1, keepdims=True)
        on_diagonal = row_iota((8, LANES)) == lane_iota((8, LANES))
        rows.append(jnp.sum(jnp.where(on_diagonal, sums, 0.0), axis=0, keepdims=True))
    return rows


def edge_kernel(p_ref, u_ref, pair_ref, other_ref):
    even = lax.rem(lax.axis_index("slab"), 2) == 0

    def plane(ref, x):
        return ref[:, x, :]

    leading = GAMMA_HORIZ * plane(p_ref, 0) - HALF_DIV * plane(u_ref, 0)
    trailing = GAMMA_HORIZ * plane(p_ref, CX - 1) + HALF_DIV * plane(u_ref, CX - 1)
    pair_ref[...] = jnp.where(even, trailing, leading)
    other_ref[...] = jnp.where(even, leading, trailing)


A_AT, B_AT, I_AT, FACE_AT, PORT_AT = 0, 6, 12, 18, 25
MAT_LEVELS = 30


def matrix_kernel(p_ref, u_ref, v_ref, w_ref, flags_ref, cell_ref, mat_ref, src_ref, panel_ref):
    shape = (CX, NY)
    rows, lanes = row_iota(shape), lane_iota(shape)
    densities, kappas = [], []
    for z in range(CZ):
        p, flags = level(p_ref, z), level(flags_ref, z)
        air = jnp.where(flags == 1, 1.0, jnp.where(flags == 2, 0.5, 0.0)).astype(F32)
        water = jnp.ones_like(p)
        for _ in range(EOS_ITERS):
            square = water * water
            cube = square * water
            sixth = cube * cube
            water = water - (sixth * water - 1.0 - p) / (7.0 * sixth)
        shifted = 1.0 + p
        air_density = AIR_DENSITY * jnp.exp(jnp.log(shifted) * (1.0 / 1.4))
        densities.append(air * air_density + (1.0 - air) * water)
        kappa = KAPPA_SCALE * (air / (1.4 * shifted) + (1.0 - air) / (7.0 * shifted))
        kappas.append(kappa)

        u, v = level(u_ref, z), level(v_ref, z)

        def beside(x, axis, step):
            size = shape[axis]
            moved = pltpu.roll(x, (-step) % size, axis)
            at = rows if axis == 0 else lanes
            return jnp.where(at == (size - 1 if step > 0 else 0), 0.0, moved)

        laplacian = (
            beside(p, 0, 1) + beside(p, 0, -1) + beside(p, 1, 1) + beside(p, 1, -1) - 4.0 * p
        )
        divergence = 0.5 * (beside(u, 0, 1) - beside(u, 0, -1)) + 0.5 * (
            beside(v, 1, 1) - beside(v, 1, -1)
        )
        if z == 0:
            w_difference = level(w_ref, 1)
        elif z == CZ - 1:
            w_difference = -level(w_ref, CZ - 2)
        else:
            w_difference = level(w_ref, z + 1) - level(w_ref, z - 1)
        divergence = divergence + 0.5 * w_difference
        src_ref[z * CX : (z + 1) * CX, :] = (
            kappa * p + GAMMA_HORIZ * laplacian - DIVERGENCE_SCALE * divergence
        )
    faces = [2.0 / (densities[z] + densities[z + 1]) for z in range(CZ - 1)]
    first, last, link, to_first, to_next, inverse = condense(kappas, faces)
    stored = to_first + to_next + inverse + faces + [first, last, link, densities[0], densities[-1]]
    for at, value in enumerate(stored):
        mat_ref[at * CX : (at + 1) * CX, :] = value

    zero, one = jnp.zeros(shape, F32), jnp.ones(shape, F32)
    no_offset = [zero] * (CZ - 2)
    onehot, row_mask = panel_masks(cell_ref[...])
    from_first = expand(one, zero, to_first, to_next, no_offset)
    from_last = expand(zero, one, to_first, to_next, no_offset)
    panel_ref[0:1, :] = pick(jnp.concatenate(from_first, 0), onehot, row_mask)
    panel_ref[1:2, :] = pick(jnp.concatenate(from_last, 0), onehot, row_mask)


def pack_kernel(
    mat_ref, src_ref, pair_ref, other_ref, w_ref, panel_ref, cell_ref, sec_ref, geom_ref,
    send_ref, offset_ref, constant_ref, rows_ref,
):
    slab = lax.axis_index("slab")
    even = lax.rem(slab, 2) == 0
    shape = (CX, NY)
    rows = row_iota(shape)
    received, beyond = pair_ref[...], other_ref[...]
    from_left = jnp.where(even, beyond, received)
    from_right = jnp.where(even, received, beyond)
    source = []
    for z in range(CZ):
        halo = jnp.where(rows == 0, from_left[z : z + 1, :], 0.0) + jnp.where(
            rows == CX - 1, from_right[z : z + 1, :], 0.0
        )
        source.append(level(src_ref, z) + halo)
    to_first = [level(mat_ref, A_AT + j) for j in range(CZ - 2)]
    to_next = [level(mat_ref, B_AT + j) for j in range(CZ - 2)]
    inverse = [level(mat_ref, I_AT + j) for j in range(CZ - 2)]
    first, last, offsets = condense_source(source, to_first, to_next, inverse)
    for j, offset in enumerate(offsets):
        offset_ref[j * CX : (j + 1) * CX, :] = offset

    section = sec_ref[...] - (slab * SEC_DEV - REACH)
    cell = cell_ref[...]
    column = cell & (CX * NY - 1)
    panel_rows = [geom_ref[k : k + 1, :] for k in range(3)]
    panel_rows += [panel_ref[0:1, :], panel_ref[1:2, :]]
    panel_rows += [column.astype(F32), section.astype(F32)]
    rows_ref[...] = jnp.zeros_like(rows_ref)
    for at, row in enumerate(panel_rows):
        for half in range(2):
            rows_ref[1 + 2 * at + half : 2 + 2 * at + half, :] = row[
                :, half * LANES : (half + 1) * LANES
            ]
    for owner in range(COLS):
        send_ref[owner * SEND_ROWS + 8 : owner * SEND_ROWS + 24, :] = rows_ref[...]
    ports = [level(mat_ref, PORT_AT + j) for j in range(3)] + [first, last]
    ports += [level(mat_ref, PORT_AT + 3), level(mat_ref, PORT_AT + 4)]
    ports += [level(w_ref, 0), level(w_ref, CZ - 1)]
    for at, value in enumerate(ports):
        for half in range(2):
            send_ref[pl.ds(half * SEND_ROWS + at, CX, stride=2 * SEND_ROWS), :] = value[
                :, half * LANES : (half + 1) * LANES
            ]

    zero = jnp.zeros(shape, F32)
    constant = expand(zero, zero, to_first, to_next, offsets)
    onehot, row_mask = panel_masks(cell)
    at_panel = pick(jnp.concatenate(constant, 0), onehot, row_mask)
    in_section = row_iota((8, PANELS_DEV)) == section
    terms = [
        jnp.where(in_section, geom_ref[k : k + 1, :] * at_panel, 0.0) for k in range(3)
    ]
    constant_ref[...] = jnp.zeros_like(constant_ref)
    for k, row in enumerate(section_rows(terms)):
        constant_ref[k : k + 1, :] = row


def owner_kernel(recv_ref, constant_ref, back_ref, group_ref, ends_ref, parts_ref, picked_ref):
    def value(at, x):
        return recv_ref[pl.ds(x * SEND_ROWS + at, 4, stride=4 * SEND_ROWS), :]

    per = [[value(at, x) for x in range(4)] for at in range(9)]
    low_k, high_k, link, low_r, high_r, low_d, high_d, low_w, high_w = per
    join = [2.0 / (high_d[x] + low_d[x + 1]) for x in range(3)]
    for x in range(3):
        high_r[x] = high_r[x] - HALF_DIV * low_w[x + 1]
        low_r[x + 1] = low_r[x + 1] + HALF_DIV * high_w[x]
    ground, source, edges = [], [], []
    for x in range(4):
        ground += [low_k[x], high_k[x]]
        source += [low_r[x], high_r[x]]
        edges += [link[x]] + ([join[x]] if x < 3 else [])
    first, last, across, to_first, to_next, inverse = condense(ground, edges)
    first_r, last_r, offsets = condense_source(source, to_first, to_next, inverse)

    stored = [first, last, across, first_r, last_r, low_d[0], high_d[3], low_w[0], high_w[3]]
    for at, x in enumerate(stored):
        group_ref[at * 4 : (at + 1) * 4, :] = x
    per = [[group_ref[at * 4 + z : at * 4 + z + 1, :] for z in range(4)] for at in range(9)]
    low_k, high_k, link, low_r, high_r, low_d, high_d, low_w, high_w = per
    outer = [2.0 / (high_d[z] + low_d[z + 1]) for z in range(3)]
    for z in range(3):
        high_r[z] = high_r[z] - HALF_DIV * low_w[z + 1]
        low_r[z + 1] = low_r[z + 1] + HALF_DIV * high_w[z]
    ground, source, edges = [], [], []
    for z in range(4):
        ground += [low_k[z], high_k[z]]
        source += [low_r[z], high_r[z]]
        edges += [link[z]] + ([outer[z]] if z < 3 else [])
    k_a, k_b, f_ab, a_list, b_list, i_list = condense(ground, edges)
    r_a, r_b, o_list = condense_source(source, a_list, b_list, i_list)
    scale = 1.0 / (k_a * k_b + f_ab * (k_a + k_b))
    p_a = ((k_b + f_ab) * r_a + f_ab * r_b) * scale
    p_b = ((k_a + f_ab) * r_b + f_ab * r_a) * scale
    nodes = expand(p_a, p_b, a_list, b_list, o_list)
    zero_row = jnp.zeros((1, LANES), F32)
    flux = [outer[z] * (nodes[2 * z + 2] - nodes[2 * z + 1]) for z in range(3)]
    for z in range(4):
        ends_ref[z : z + 1, :] = nodes[2 * z]
        ends_ref[4 + z : 5 + z, :] = nodes[2 * z + 1]
        ends_ref[8 + z : 9 + z, :] = flux[z - 1] if z > 0 else zero_row
        ends_ref[12 + z : 13 + z, :] = flux[z] if z < 3 else zero_row

    nodes = expand(ends_ref[0:4, :], ends_ref[4:8, :], to_first, to_next, offsets)
    inner = [join[x] * (nodes[2 * x + 2] - nodes[2 * x + 1]) for x in range(3)]
    below = [ends_ref[8:12, :]] + inner
    above = inner + [ends_ref[12:16, :]]

    def put(ref, rows, at, x, what):
        ref[pl.ds(x * rows + at, 4, stride=4 * rows), :] = what

    for x in range(4):
        put(back_ref, BACK_ROWS, 0, x, nodes[2 * x])
        put(back_ref, BACK_ROWS, 1, x, nodes[2 * x + 1])
        put(back_ref, BACK_ROWS, 2, x, below[x])
        put(back_ref, BACK_ROWS, 3, x, above[x])
        for end in range(2):
            for at, part in enumerate(split_three(nodes[2 * x + end])):
                put(parts_ref, 8, 3 * end + at, x, part.astype(F32))
            put(parts_ref, 8, 6 + end, x, jnp.zeros((4, LANES), F32))

    mine = lax.axis_index("col") * LANES
    want = (row_iota((LANES, LANES)) + mine).astype(F32)
    for block in range(COLS):
        ends = parts_ref[block * 8 : (block + 1) * 8, :].astype(jnp.bfloat16)
        at = block * SEND_ROWS + 9 + 10
        for half in range(2):
            column = recv_ref[at + half : at + half + 1, :]
            onehot = jnp.where(want == column, 1.0, 0.0).astype(jnp.bfloat16)
            got = jnp.dot(ends, onehot, preferred_element_type=F32)
            picked_ref[(half * COLS + block) * 8 : (half * COLS + block + 1) * 8, :] = got
    sums = [[None] * 8 for _ in range(3)]
    for half in range(2):

        def panel(at):
            return recv_ref[pl.ds(9 + 2 * at + half, COLS, stride=SEND_ROWS), :]

        def got(at):
            return picked_ref[pl.ds(half * COLS * 8 + at, COLS, stride=8), :]

        low = got(0) + got(1) + got(2)
        high = got(3) + got(4) + got(5)
        at_panel = panel(3) * low + panel(4) * high
        section = panel(6)
        for k in range(3):
            term = panel(k) * at_panel
            for j in range(8):
                part = jnp.where(section == float(j), term, 0.0)
                part = part[0:8, :] + part[8:16, :]
                sums[k][j] = part if half == 0 else sums[k][j] + part
    terms = [
        jnp.concatenate([jnp.sum(x, axis=0, keepdims=True) for x in sums[k]], 0)
        for k in range(3)
    ]
    rows = section_rows(terms)
    for block in range(COLS):
        for k in range(3):
            at = block * BACK_ROWS + 4 + k
            back_ref[at : at + 1, :] = rows[k] + constant_ref[k : k + 1, :]
        back_ref[block * BACK_ROWS + 7 : block * BACK_ROWS + 8, :] = zero_row


def load_kernel(back_ref, load_ref):
    load_ref[...] = jnp.zeros_like(load_ref)
    for k in range(3):
        rows = back_ref[pl.ds(4 + k, COLS, stride=BACK_ROWS), :]
        load_ref[k : k + 1, :] = jnp.sum(rows, axis=0, keepdims=True)


def field_kernel(back_ref, mat_ref, offset_ref, w_ref, pressure_ref, velocity_ref):
    def end(at):
        halves = [
            back_ref[pl.ds(half * BACK_ROWS + at, CX, stride=2 * BACK_ROWS), :] for half in range(2)
        ]
        return jnp.concatenate(halves, axis=1)

    to_first = [level(mat_ref, A_AT + j) for j in range(CZ - 2)]
    to_next = [level(mat_ref, B_AT + j) for j in range(CZ - 2)]
    offsets = [level(offset_ref, j) for j in range(CZ - 2)]
    pressure = expand(end(0), end(1), to_first, to_next, offsets)
    flux = [end(2)]
    for z in range(CZ - 1):
        flux.append(level(mat_ref, FACE_AT + z) * (pressure[z + 1] - pressure[z]))
    flux.append(end(3))
    for z in range(CZ):
        pressure_ref[z * CX : (z + 1) * CX, :] = pressure[z]
        velocity_ref[z * CX : (z + 1) * CX, :] = level(w_ref, z) - 0.5 * (flux[z + 1] + flux[z])


def section_kernel(load_ref, pair_ref, other_ref, out_ref):
    even = lax.rem(lax.axis_index("slab"), 2) == 0
    received, beyond = pair_ref[...], other_ref[...]
    from_left = jnp.where(even, beyond, received)
    from_right = jnp.where(even, received, beyond)
    lanes = lane_iota((8, LANES))
    total = load_ref[...]
    total = total + jnp.where(lanes < 4, pltpu.roll(from_left, LANES - 4, 1), 0.0)
    total = total + jnp.where(lanes >= 4, pltpu.roll(from_right, 4, 1), 0.0)
    total = pltpu.roll(total, LANES - REACH, 1)
    out_ref[...] = total[0:3, 0:SEC_DEV]


def call(kernel, outs, scratch=(), flops=20000):
    shapes = [jax.ShapeDtypeStruct(shape, F32) for shape in outs]
    return pl.pallas_call(
        kernel,
        out_shape=shapes if len(shapes) > 1 else shapes[0],
        scratch_shapes=[pltpu.VMEM(shape, F32) for shape in scratch],
        compiler_params=pltpu.CompilerParams(vmem_limit_bytes=16 * 1024 * 1024),
        cost_estimate=pl.CostEstimate(flops=flops, bytes_accessed=500000, transcendentals=0),
    )


def per_device(p_star, u_star, v_star, w_star, flags, panel_cell, panel_section, panel_geom):
    flat = (CZ * CX, NY)
    p, u, v, w = (x.reshape(flat) for x in (p_star, u_star, v_star, w_star))
    flags = flags.reshape(flat)
    cell = panel_cell.reshape(1, PANELS_DEV)
    section = panel_section.reshape(1, PANELS_DEV)
    slabs = lax.axis_size("slab")
    pairs = [(i, i ^ 1) for i in range(slabs)]
    others = [(i, i + 1) for i in range(1, slabs - 1, 2)]
    others += [(j, i) for i, j in others]

    to_pair, to_other = call(edge_kernel, [(CZ, NY)] * 2)(p_star, u_star)
    from_pair = lax.ppermute(to_pair, "slab", pairs)
    from_other = lax.ppermute(to_other, "slab", others)
    mat, source, panel = call(
        matrix_kernel, [(MAT_LEVELS * CX, NY), flat, (2, PANELS_DEV)], flops=5000000
    )(p, u, v, w, flags, cell)
    send, offsets, constant = call(
        pack_kernel,
        [(COLS * SEND_ROWS, LANES), ((CZ - 2) * CX, NY), (8, LANES)],
        [(16, LANES)],
    )(mat, source, from_pair, from_other, w, panel, cell, section, panel_geom)
    recv = lax.all_to_all(send, "col", 0, 0, tiled=True)
    back = call(
        owner_kernel,
        [(COLS * BACK_ROWS, LANES)],
        [(40, LANES), (16, LANES), (COLS * 8, LANES), (2 * COLS * 8, LANES)],
    )(recv, constant)
    back = lax.all_to_all(back, "col", 0, 0, tiled=True)
    loads = call(load_kernel, [(8, LANES)])(back)
    loads_pair = lax.ppermute(loads, "slab", pairs)
    loads_other = lax.ppermute(loads, "slab", others)
    pressure, velocity = call(field_kernel, [flat, flat], flops=5000000)(back, mat, offsets, w)
    section_loads = call(section_kernel, [(3, SEC_DEV)])(loads, loads_pair, loads_other)
    return pressure.reshape(p_star.shape), velocity.reshape(p_star.shape), section_loads


def solution(mesh):
    in_specs = (
        P("col", "slab", None),
        P("col", "slab", None),
        P("col", "slab", None),
        P("col", "slab", None),
        P("col", "slab", None),
        P(("col", "slab")),
        P(("col", "slab")),
        P(None, ("col", "slab")),
    )
    out_specs = (P("col", "slab", None), P("col", "slab", None), P(None, "slab"))
    return jax.shard_map(
        per_device, mesh=mesh, in_specs=in_specs, out_specs=out_specs, check_vma=False
    )
```

```python
import functools

import jax
import jax.numpy as jnp
from jax import lax
from jax.experimental import pallas as pl
from jax.experimental.pallas import tpu as pltpu
from jax.sharding import PartitionSpec as P

SEC_DEV = 4
EOS_ITERS = 3
KAPPA_SCALE = 0.01
AIR_DENSITY = 0.1
GAMMA_HORIZ = 0.001
DIVERGENCE_SCALE = 0.005
HALF_DIV = 0.5 * DIVERGENCE_SCALE

CZ = 8
CX = 8
NY = 256
LANES = 128
COLS = 16
PANELS_DEV = 256
REACH = 2
SEND_ROWS = 24
BACK_ROWS = 8

F32 = jnp.float32


def row_iota(shape):
    return lax.broadcasted_iota(jnp.int32, shape, 0)


def lane_iota(shape):
    return lax.broadcasted_iota(jnp.int32, shape, 1)


def level(ref, z):
    return ref[z * CX : (z + 1) * CX, :]


def split_three(x):
    high = x.astype(jnp.bfloat16)
    rest = x - high.astype(F32)
    middle = rest.astype(jnp.bfloat16)
    low = (rest - middle.astype(F32)).astype(jnp.bfloat16)
    return high, middle, low


def pick(fields, onehot, row_mask):
    total = None
    for part in split_three(fields):
        term = jnp.dot(part, onehot, preferred_element_type=F32)
        total = term if total is None else total + term
    return jnp.sum(jnp.where(row_mask, total, 0.0), axis=0, keepdims=True)


def panel_masks(cell):
    onehot = (row_iota((NY, PANELS_DEV)) == (cell & (NY - 1))).astype(F32)
    row_mask = row_iota((CZ * CX, PANELS_DEV)) == (cell >> 8)
    return onehot.astype(jnp.bfloat16), row_mask


def condense(ground, edges):
    first, here, link = ground[0], ground[1], edges[0]
    to_first, to_next, inverse = [], [], []
    for j in range(1, len(ground) - 1):
        edge = edges[j]
        inv = 1.0 / (here + link + edge)
        a, b = link * inv, edge * inv
        first = first + a * here
        here = ground[j + 1] + b * here
        link = link * b
        to_first.append(a)
        to_next.append(b)
        inverse.append(inv)
    return first, here, link, to_first, to_next, inverse


def condense_source(source, to_first, to_next, inverse):
    first, here = source[0], source[1]
    offsets = []
    for j in range(1, len(source) - 1):
        a, b = to_first[j - 1], to_next[j - 1]
        offsets.append(here * inverse[j - 1])
        first = first + a * here
        here = source[j + 1] + b * here
    return first, here, offsets


def expand(first, last, to_first, to_next, offsets):
    values = [last]
    for a, b, offset in zip(reversed(to_first), reversed(to_next), reversed(offsets)):
        values.append(offset + a * first + b * values[-1])
    values.append(first)
    return values[::-1]


def section_rows(terms):
    rows = []
    for term in terms:
        sums = jnp.sum(term, axis=1, keepdims=True)
        on_diagonal = row_iota((8, LANES)) == lane_iota((8, LANES))
        rows.append(jnp.sum(jnp.where(on_diagonal, sums, 0.0), axis=0, keepdims=True))
    return rows


A_AT, B_AT, I_AT, FACE_AT, PORT_AT = 0, 6, 12, 18, 25
MAT_LEVELS = 30


def matrix_kernel(
    p_ref, u_ref, v_ref, w_ref, flags_ref, cell_ref, sec_ref, geom_ref,
    mat_ref, src_ref, panel_ref,
):
    shape = (CX, NY)
    rows, lanes = row_iota(shape), lane_iota(shape)
    densities, kappas = [], []
    for z in range(CZ):
        p, flags = level(p_ref, z), level(flags_ref, z)
        air = jnp.where(flags == 1, 1.0, jnp.where(flags == 2, 0.5, 0.0)).astype(F32)
        water = jnp.ones_like(p)
        for _ in range(EOS_ITERS):
            square = water * water
            cube = square * water
            sixth = cube * cube
            water = water - (sixth * water - 1.0 - p) / (7.0 * sixth)
        shifted = 1.0 + p
        air_density = AIR_DENSITY * jnp.exp(jnp.log(shifted) * (1.0 / 1.4))
        densities.append(air * air_density + (1.0 - air) * water)
        kappa = KAPPA_SCALE * (air / (1.4 * shifted) + (1.0 - air) / (7.0 * shifted))
        kappas.append(kappa)

        u, v = level(u_ref, z), level(v_ref, z)

        def beside(x, axis, step):
            size = shape[axis]
            moved = pltpu.roll(x, (-step) % size, axis)
            at = rows if axis == 0 else lanes
            return jnp.where(at == (size - 1 if step > 0 else 0), 0.0, moved)

        laplacian = (
            beside(p, 0, 1) + beside(p, 0, -1) + beside(p, 1, 1) + beside(p, 1, -1) - 4.0 * p
        )
        divergence = 0.5 * (beside(u, 0, 1) - beside(u, 0, -1)) + 0.5 * (
            beside(v, 1, 1) - beside(v, 1, -1)
        )
        if z == 0:
            w_difference = level(w_ref, 1)
        elif z == CZ - 1:
            w_difference = -level(w_ref, CZ - 2)
        else:
            w_difference = level(w_ref, z + 1) - level(w_ref, z - 1)
        divergence = divergence + 0.5 * w_difference
        src_ref[z * CX : (z + 1) * CX, :] = (
            kappa * p + GAMMA_HORIZ * laplacian - DIVERGENCE_SCALE * divergence
        )
    faces = [2.0 / (densities[z] + densities[z + 1]) for z in range(CZ - 1)]
    first, last, link, to_first, to_next, inverse = condense(kappas, faces)
    stored = to_first + to_next + inverse + faces + [first, last, link, densities[0], densities[-1]]
    for at, value in enumerate(stored):
        mat_ref[at * CX : (at + 1) * CX, :] = value

    zero, one = jnp.zeros(shape, F32), jnp.ones(shape, F32)
    no_offset = [zero] * (CZ - 2)
    onehot, row_mask = panel_masks(cell_ref[...])
    from_first = expand(one, zero, to_first, to_next, no_offset)
    from_last = expand(zero, one, to_first, to_next, no_offset)
    section = sec_ref[...] - (lax.axis_index("slab") * SEC_DEV - REACH)
    column = cell_ref[...] & (CX * NY - 1)
    panel_rows = [geom_ref[k : k + 1, :] for k in range(3)]
    panel_rows.append(pick(jnp.concatenate(from_first, 0), onehot, row_mask))
    panel_rows.append(pick(jnp.concatenate(from_last, 0), onehot, row_mask))
    panel_rows += [column.astype(F32), section.astype(F32)]
    panel_ref[...] = jnp.zeros_like(panel_ref)
    for at, row in enumerate(panel_rows):
        for half in range(2):
            panel_ref[1 + 2 * at + half : 2 + 2 * at + half, :] = row[
                :, half * LANES : (half + 1) * LANES
            ]


def pack_kernel(
    mat_ref, src_ref, pair_ref, other_ref, w_ref, panel_ref, cell_ref,
    send_ref, offset_ref, constant_ref,
):
    even = lax.rem(lax.axis_index("slab"), 2) == 0
    shape = (CX, NY)
    rows = row_iota(shape)
    received, beyond = pair_ref[...], other_ref[...]
    from_left = jnp.where(even, beyond, received)
    from_right = jnp.where(even, received, beyond)
    source = []
    for z in range(CZ):
        halo = jnp.where(rows == 0, from_left[z : z + 1, :], 0.0) + jnp.where(
            rows == CX - 1, from_right[z : z + 1, :], 0.0
        )
        source.append(level(src_ref, z) + halo)
    to_first = [level(mat_ref, A_AT + j) for j in range(CZ - 2)]
    to_next = [level(mat_ref, B_AT + j) for j in range(CZ - 2)]
    inverse = [level(mat_ref, I_AT + j) for j in range(CZ - 2)]
    first, last, offsets = condense_source(source, to_first, to_next, inverse)
    for j, offset in enumerate(offsets):
        offset_ref[j * CX : (j + 1) * CX, :] = offset

    for owner in range(COLS):
        send_ref[owner * SEND_ROWS + 8 : owner * SEND_ROWS + 24, :] = panel_ref[...]
    ports = [level(mat_ref, PORT_AT + j) for j in range(3)] + [first, last]
    ports += [level(mat_ref, PORT_AT + 3), level(mat_ref, PORT_AT + 4)]
    ports += [level(w_ref, 0), level(w_ref, CZ - 1)]
    for at, value in enumerate(ports):
        for half in range(2):
            send_ref[pl.ds(half * SEND_ROWS + at, CX, stride=2 * SEND_ROWS), :] = value[
                :, half * LANES : (half + 1) * LANES
            ]

    zero = jnp.zeros(shape, F32)
    constant = expand(zero, zero, to_first, to_next, offsets)
    onehot, row_mask = panel_masks(cell_ref[...])
    at_panel = pick(jnp.concatenate(constant, 0), onehot, row_mask)
    terms = [0.0, 0.0, 0.0]
    for half in range(2):
        lanes = slice(half * LANES, (half + 1) * LANES)
        in_section = row_iota((8, LANES)).astype(F32) == panel_ref[13 + half : 14 + half, :]
        for k in range(3):
            row = panel_ref[1 + 2 * k + half : 2 + 2 * k + half, :] * at_panel[:, lanes]
            terms[k] = terms[k] + jnp.where(in_section, row, 0.0)
    constant_ref[...] = jnp.zeros_like(constant_ref)
    for k, row in enumerate(section_rows(terms)):
        constant_ref[k : k + 1, :] = row


def owner_kernel(recv_ref, constant_ref, back_ref, group_ref, ends_ref, parts_ref, picked_ref):
    def value(at, x):
        return recv_ref[pl.ds(x * SEND_ROWS + at, 4, stride=4 * SEND_ROWS), :]

    per = [[value(at, x) for x in range(4)] for at in range(9)]
    low_k, high_k, link, low_r, high_r, low_d, high_d, low_w, high_w = per
    join = [2.0 / (high_d[x] + low_d[x + 1]) for x in range(3)]
    for x in range(3):
        high_r[x] = high_r[x] - HALF_DIV * low_w[x + 1]
        low_r[x + 1] = low_r[x + 1] + HALF_DIV * high_w[x]
    ground, source, edges = [], [], []
    for x in range(4):
        ground += [low_k[x], high_k[x]]
        source += [low_r[x], high_r[x]]
        edges += [link[x]] + ([join[x]] if x < 3 else [])
    first, last, across, to_first, to_next, inverse = condense(ground, edges)
    first_r, last_r, offsets = condense_source(source, to_first, to_next, inverse)

    stored = [first, last, across, first_r, last_r, low_d[0], high_d[3], low_w[0], high_w[3]]
    for at, x in enumerate(stored):
        group_ref[at * 4 : (at + 1) * 4, :] = x
    per = [[group_ref[at * 4 + z : at * 4 + z + 1, :] for z in range(4)] for at in range(9)]
    low_k, high_k, link, low_r, high_r, low_d, high_d, low_w, high_w = per
    outer = [2.0 / (high_d[z] + low_d[z + 1]) for z in range(3)]
    for z in range(3):
        high_r[z] = high_r[z] - HALF_DIV * low_w[z + 1]
        low_r[z + 1] = low_r[z + 1] + HALF_DIV * high_w[z]
    ground, source, edges = [], [], []
    for z in range(4):
        ground += [low_k[z], high_k[z]]
        source += [low_r[z], high_r[z]]
        edges += [link[z]] + ([outer[z]] if z < 3 else [])
    k_a, k_b, f_ab, a_list, b_list, i_list = condense(ground, edges)
    r_a, r_b, o_list = condense_source(source, a_list, b_list, i_list)
    scale = 1.0 / (k_a * k_b + f_ab * (k_a + k_b))
    p_a = ((k_b + f_ab) * r_a + f_ab * r_b) * scale
    p_b = ((k_a + f_ab) * r_b + f_ab * r_a) * scale
    nodes = expand(p_a, p_b, a_list, b_list, o_list)
    zero_row = jnp.zeros((1, LANES), F32)
    flux = [outer[z] * (nodes[2 * z + 2] - nodes[2 * z + 1]) for z in range(3)]
    for z in range(4):
        ends_ref[z : z + 1, :] = nodes[2 * z]
        ends_ref[4 + z : 5 + z, :] = nodes[2 * z + 1]
        ends_ref[8 + z : 9 + z, :] = flux[z - 1] if z > 0 else zero_row
        ends_ref[12 + z : 13 + z, :] = flux[z] if z < 3 else zero_row

    nodes = expand(ends_ref[0:4, :], ends_ref[4:8, :], to_first, to_next, offsets)
    inner = [join[x] * (nodes[2 * x + 2] - nodes[2 * x + 1]) for x in range(3)]
    below = [ends_ref[8:12, :]] + inner
    above = inner + [ends_ref[12:16, :]]

    def put(ref, rows, at, x, what):
        ref[pl.ds(x * rows + at, 4, stride=4 * rows), :] = what

    for x in range(4):
        put(back_ref, BACK_ROWS, 0, x, nodes[2 * x])
        put(back_ref, BACK_ROWS, 1, x, nodes[2 * x + 1])
        put(back_ref, BACK_ROWS, 2, x, below[x])
        put(back_ref, BACK_ROWS, 3, x, above[x])
        for end in range(2):
            for at, part in enumerate(split_three(nodes[2 * x + end])):
                put(parts_ref, 8, 3 * end + at, x, part.astype(F32))
            put(parts_ref, 8, 6 + end, x, jnp.zeros((4, LANES), F32))

    mine = lax.axis_index("col") * LANES
    want = (row_iota((LANES, LANES)) + mine).astype(F32)
    for block in range(COLS):
        ends = parts_ref[block * 8 : (block + 1) * 8, :].astype(jnp.bfloat16)
        at = block * SEND_ROWS + 9 + 10
        for half in range(2):
            column = recv_ref[at + half : at + half + 1, :]
            onehot = jnp.where(want == column, 1.0, 0.0).astype(jnp.bfloat16)
            got = jnp.dot(ends, onehot, preferred_element_type=F32)
            picked_ref[(half * COLS + block) * 8 : (half * COLS + block + 1) * 8, :] = got
    sums = [[None] * 8 for _ in range(3)]
    for half in range(2):

        def panel(at):
            return recv_ref[pl.ds(9 + 2 * at + half, COLS, stride=SEND_ROWS), :]

        def got(at):
            return picked_ref[pl.ds(half * COLS * 8 + at, COLS, stride=8), :]

        low = got(0) + got(1) + got(2)
        high = got(3) + got(4) + got(5)
        at_panel = panel(3) * low + panel(4) * high
        section = panel(6)
        for k in range(3):
            term = panel(k) * at_panel
            for j in range(8):
                part = jnp.where(section == float(j), term, 0.0)
                part = part[0:8, :] + part[8:16, :]
                sums[k][j] = part if half == 0 else sums[k][j] + part
    terms = [
        jnp.concatenate([jnp.sum(x, axis=0, keepdims=True) for x in sums[k]], 0)
        for k in range(3)
    ]
    rows = section_rows(terms)
    for block in range(COLS):
        for k in range(3):
            at = block * BACK_ROWS + 4 + k
            back_ref[at : at + 1, :] = rows[k] + constant_ref[k : k + 1, :]
        back_ref[block * BACK_ROWS + 7 : block * BACK_ROWS + 8, :] = zero_row


def load_kernel(back_ref, load_ref):
    load_ref[...] = jnp.zeros_like(load_ref)
    for k in range(3):
        rows = back_ref[pl.ds(4 + k, COLS, stride=BACK_ROWS), :]
        load_ref[k : k + 1, :] = jnp.sum(rows, axis=0, keepdims=True)


def field_kernel(back_ref, mat_ref, offset_ref, w_ref, pressure_ref, velocity_ref):
    def end(at):
        halves = [
            back_ref[pl.ds(half * BACK_ROWS + at, CX, stride=2 * BACK_ROWS), :] for half in range(2)
        ]
        return jnp.concatenate(halves, axis=1)

    to_first = [level(mat_ref, A_AT + j) for j in range(CZ - 2)]
    to_next = [level(mat_ref, B_AT + j) for j in range(CZ - 2)]
    offsets = [level(offset_ref, j) for j in range(CZ - 2)]
    pressure = expand(end(0), end(1), to_first, to_next, offsets)
    flux = [end(2)]
    for z in range(CZ - 1):
        flux.append(level(mat_ref, FACE_AT + z) * (pressure[z + 1] - pressure[z]))
    flux.append(end(3))
    for z in range(CZ):
        pressure_ref[z * CX : (z + 1) * CX, :] = pressure[z]
        velocity_ref[z * CX : (z + 1) * CX, :] = level(w_ref, z) - 0.5 * (flux[z + 1] + flux[z])


def section_kernel(load_ref, pair_ref, other_ref, out_ref):
    even = lax.rem(lax.axis_index("slab"), 2) == 0
    received, beyond = pair_ref[...], other_ref[...]
    from_left = jnp.where(even, beyond, received)
    from_right = jnp.where(even, received, beyond)
    lanes = lane_iota((8, LANES))
    total = load_ref[...]
    total = total + jnp.where(lanes < 4, pltpu.roll(from_left, LANES - 4, 1), 0.0)
    total = total + jnp.where(lanes >= 4, pltpu.roll(from_right, 4, 1), 0.0)
    total = pltpu.roll(total, LANES - REACH, 1)
    out_ref[...] = total[0:3, 0:SEC_DEV]


def call(kernel, outs, scratch=(), flops=20000):
    shapes = [jax.ShapeDtypeStruct(shape, F32) for shape in outs]
    return pl.pallas_call(
        kernel,
        out_shape=shapes if len(shapes) > 1 else shapes[0],
        scratch_shapes=[pltpu.VMEM(shape, F32) for shape in scratch],
        compiler_params=pltpu.CompilerParams(vmem_limit_bytes=16 * 1024 * 1024),
        cost_estimate=pl.CostEstimate(flops=flops, bytes_accessed=500000, transcendentals=0),
    )


def per_device(p_star, u_star, v_star, w_star, flags, panel_cell, panel_section, panel_geom):
    flat = (CZ * CX, NY)
    p, u, v, w = (x.reshape(flat) for x in (p_star, u_star, v_star, w_star))
    flags = flags.reshape(flat)
    cell = panel_cell.reshape(1, PANELS_DEV)
    section = panel_section.reshape(1, PANELS_DEV)
    slabs = lax.axis_size("slab")
    pairs = [(i, i ^ 1) for i in range(slabs)]
    others = [(i, i + 1) for i in range(1, slabs - 1, 2)]
    others += [(j, i) for i, j in others]

    even = lax.rem(lax.axis_index("slab"), 2) == 0
    leading = GAMMA_HORIZ * p_star[:, 0, :] - HALF_DIV * u_star[:, 0, :]
    trailing = GAMMA_HORIZ * p_star[:, CX - 1, :] + HALF_DIV * u_star[:, CX - 1, :]
    to_pair = jnp.where(even, trailing, leading)
    to_other = jnp.where(even, leading, trailing)
    from_other = lax.ppermute(to_other, "slab", others)
    from_pair = lax.ppermute(to_pair, "slab", pairs)
    mat, source, panel = call(
        matrix_kernel, [(MAT_LEVELS * CX, NY), flat, (16, LANES)], flops=5000000
    )(p, u, v, w, flags, cell, section, panel_geom)
    send, offsets, constant = call(
        pack_kernel,
        [(COLS * SEND_ROWS, LANES), ((CZ - 2) * CX, NY), (8, LANES)],
    )(mat, source, from_pair, from_other, w, panel, cell)
    recv = lax.all_to_all(send, "col", 0, 0, tiled=True)
    back = call(
        owner_kernel,
        [(COLS * BACK_ROWS, LANES)],
        [(40, LANES), (16, LANES), (COLS * 8, LANES), (2 * COLS * 8, LANES)],
    )(recv, constant)
    back = lax.all_to_all(back, "col", 0, 0, tiled=True)
    loads = call(load_kernel, [(8, LANES)])(back)
    loads_pair = lax.ppermute(loads, "slab", pairs)
    loads_other = lax.ppermute(loads, "slab", others)
    pressure, velocity = call(field_kernel, [flat, flat], flops=5000000)(back, mat, offsets, w)
    section_loads = call(section_kernel, [(3, SEC_DEV)])(loads, loads_pair, loads_other)
    return pressure.reshape(p_star.shape), velocity.reshape(p_star.shape), section_loads


def solution(mesh):
    in_specs = (
        P("col", "slab", None),
        P("col", "slab", None),
        P("col", "slab", None),
        P("col", "slab", None),
        P("col", "slab", None),
        P(("col", "slab")),
        P(("col", "slab")),
        P(None, ("col", "slab")),
    )
    out_specs = (P("col", "slab", None), P("col", "slab", None), P(None, "slab"))
    return jax.shard_map(
        per_device, mesh=mesh, in_specs=in_specs, out_specs=out_specs, check_vma=False
    )
```

```python
import functools

import jax
import jax.numpy as jnp
from jax import lax
from jax.experimental import pallas as pl
from jax.experimental.pallas import tpu as pltpu
from jax.sharding import PartitionSpec as P

SEC_DEV = 4
EOS_ITERS = 3
KAPPA_SCALE = 0.01
AIR_DENSITY = 0.1
GAMMA_HORIZ = 0.001
DIVERGENCE_SCALE = 0.005
HALF_DIV = 0.5 * DIVERGENCE_SCALE

CZ = 8
CX = 8
NY = 256
LANES = 128
COLS = 16
PANELS_DEV = 256
REACH = 2
SEND_ROWS = 24
BACK_ROWS = 8

F32 = jnp.float32


def row_iota(shape):
    return lax.broadcasted_iota(jnp.int32, shape, 0)


def lane_iota(shape):
    return lax.broadcasted_iota(jnp.int32, shape, 1)


def level(ref, z):
    return ref[z * CX : (z + 1) * CX, :]


def split_three(x):
    high = x.astype(jnp.bfloat16)
    rest = x - high.astype(F32)
    middle = rest.astype(jnp.bfloat16)
    low = (rest - middle.astype(F32)).astype(jnp.bfloat16)
    return high, middle, low


def pick(fields, onehot, row_mask):
    total = None
    for part in split_three(fields):
        term = jnp.dot(part, onehot, preferred_element_type=F32)
        total = term if total is None else total + term
    return jnp.sum(jnp.where(row_mask, total, 0.0), axis=0, keepdims=True)


def panel_masks(cell):
    onehot = (row_iota((NY, PANELS_DEV)) == (cell & (NY - 1))).astype(F32)
    row_mask = row_iota((CZ * CX, PANELS_DEV)) == (cell >> 8)
    return onehot.astype(jnp.bfloat16), row_mask


def condense(ground, edges):
    first, here, link = ground[0], ground[1], edges[0]
    to_first, to_next, inverse = [], [], []
    for j in range(1, len(ground) - 1):
        edge = edges[j]
        inv = 1.0 / (here + link + edge)
        a, b = link * inv, edge * inv
        first = first + a * here
        here = ground[j + 1] + b * here
        link = link * b
        to_first.append(a)
        to_next.append(b)
        inverse.append(inv)
    return first, here, link, to_first, to_next, inverse


def condense_source(source, to_first, to_next, inverse):
    first, here = source[0], source[1]
    offsets = []
    for j in range(1, len(source) - 1):
        a, b = to_first[j - 1], to_next[j - 1]
        offsets.append(here * inverse[j - 1])
        first = first + a * here
        here = source[j + 1] + b * here
    return first, here, offsets


def expand(first, last, to_first, to_next, offsets):
    values = [last]
    for a, b, offset in zip(reversed(to_first), reversed(to_next), reversed(offsets)):
        values.append(offset + a * first + b * values[-1])
    values.append(first)
    return values[::-1]


def section_rows(terms):
    rows = []
    for term in terms:
        sums = jnp.sum(term, axis=1, keepdims=True)
        on_diagonal = row_iota((8, LANES)) == lane_iota((8, LANES))
        rows.append(jnp.sum(jnp.where(on_diagonal, sums, 0.0), axis=0, keepdims=True))
    return rows


def choose_kernel(leading_ref, trailing_ref, plane_ref):
    even = lax.rem(lax.axis_index("slab"), 2) == 0
    for z in range(CZ):
        plane_ref[z : z + 1, :] = jnp.where(even, leading_ref[z], trailing_ref[z])


A_AT, B_AT, I_AT, FACE_AT, PORT_AT = 0, 6, 12, 18, 25
MAT_LEVELS = 30


def matrix_kernel(
    p_ref, u_ref, v_ref, w_ref, flags_ref, cell_ref, sec_ref, geom_ref,
    mat_ref, src_ref, panel_ref, plane_ref,
):
    even = lax.rem(lax.axis_index("slab"), 2) == 0
    for z in range(CZ):
        p, u = level(p_ref, z), level(u_ref, z)
        plane_ref[z : z + 1, :] = jnp.where(
            even,
            GAMMA_HORIZ * p[CX - 1 :, :] + HALF_DIV * u[CX - 1 :, :],
            GAMMA_HORIZ * p[:1, :] - HALF_DIV * u[:1, :],
        )
    shape = (CX, NY)
    rows, lanes = row_iota(shape), lane_iota(shape)
    densities, kappas = [], []
    for z in range(CZ):
        p, flags = level(p_ref, z), level(flags_ref, z)
        air = jnp.where(flags == 1, 1.0, jnp.where(flags == 2, 0.5, 0.0)).astype(F32)
        water = jnp.ones_like(p)
        for _ in range(EOS_ITERS):
            square = water * water
            cube = square * water
            sixth = cube * cube
            water = water - (sixth * water - 1.0 - p) / (7.0 * sixth)
        shifted = 1.0 + p
        air_density = AIR_DENSITY * jnp.exp(jnp.log(shifted) * (1.0 / 1.4))
        densities.append(air * air_density + (1.0 - air) * water)
        kappa = KAPPA_SCALE * (air / (1.4 * shifted) + (1.0 - air) / (7.0 * shifted))
        kappas.append(kappa)

        u, v = level(u_ref, z), level(v_ref, z)

        def beside(x, axis, step):
            size = shape[axis]
            moved = pltpu.roll(x, (-step) % size, axis)
            at = rows if axis == 0 else lanes
            return jnp.where(at == (size - 1 if step > 0 else 0), 0.0, moved)

        laplacian = (
            beside(p, 0, 1) + beside(p, 0, -1) + beside(p, 1, 1) + beside(p, 1, -1) - 4.0 * p
        )
        divergence = 0.5 * (beside(u, 0, 1) - beside(u, 0, -1)) + 0.5 * (
            beside(v, 1, 1) - beside(v, 1, -1)
        )
        if z == 0:
            w_difference = level(w_ref, 1)
        elif z == CZ - 1:
            w_difference = -level(w_ref, CZ - 2)
        else:
            w_difference = level(w_ref, z + 1) - level(w_ref, z - 1)
        divergence = divergence + 0.5 * w_difference
        src_ref[z * CX : (z + 1) * CX, :] = (
            kappa * p + GAMMA_HORIZ * laplacian - DIVERGENCE_SCALE * divergence
        )
    faces = [2.0 / (densities[z] + densities[z + 1]) for z in range(CZ - 1)]
    first, last, link, to_first, to_next, inverse = condense(kappas, faces)
    stored = to_first + to_next + inverse + faces + [first, last, link, densities[0], densities[-1]]
    for at, value in enumerate(stored):
        mat_ref[at * CX : (at + 1) * CX, :] = value

    zero, one = jnp.zeros(shape, F32), jnp.ones(shape, F32)
    no_offset = [zero] * (CZ - 2)
    onehot, row_mask = panel_masks(cell_ref[...])
    from_first = expand(one, zero, to_first, to_next, no_offset)
    from_last = expand(zero, one, to_first, to_next, no_offset)
    section = sec_ref[...] - (lax.axis_index("slab") * SEC_DEV - REACH)
    column = cell_ref[...] & (CX * NY - 1)
    panel_rows = [geom_ref[k : k + 1, :] for k in range(3)]
    panel_rows.append(pick(jnp.concatenate(from_first, 0), onehot, row_mask))
    panel_rows.append(pick(jnp.concatenate(from_last, 0), onehot, row_mask))
    panel_rows += [column.astype(F32), section.astype(F32)]
    panel_ref[...] = jnp.zeros_like(panel_ref)
    for at, row in enumerate(panel_rows):
        for half in range(2):
            panel_ref[1 + 2 * at + half : 2 + 2 * at + half, :] = row[
                :, half * LANES : (half + 1) * LANES
            ]


def pack_kernel(
    mat_ref, src_ref, pair_ref, other_ref, w_ref, panel_ref, cell_ref,
    send_ref, offset_ref, constant_ref,
):
    even = lax.rem(lax.axis_index("slab"), 2) == 0
    shape = (CX, NY)
    rows = row_iota(shape)
    received, beyond = pair_ref[...], other_ref[...]
    from_left = jnp.where(even, beyond, received)
    from_right = jnp.where(even, received, beyond)
    source = []
    for z in range(CZ):
        halo = jnp.where(rows == 0, from_left[z : z + 1, :], 0.0) + jnp.where(
            rows == CX - 1, from_right[z : z + 1, :], 0.0
        )
        source.append(level(src_ref, z) + halo)
    to_first = [level(mat_ref, A_AT + j) for j in range(CZ - 2)]
    to_next = [level(mat_ref, B_AT + j) for j in range(CZ - 2)]
    inverse = [level(mat_ref, I_AT + j) for j in range(CZ - 2)]
    first, last, offsets = condense_source(source, to_first, to_next, inverse)
    for j, offset in enumerate(offsets):
        offset_ref[j * CX : (j + 1) * CX, :] = offset

    for owner in range(COLS):
        send_ref[owner * SEND_ROWS + 8 : owner * SEND_ROWS + 24, :] = panel_ref[...]
    ports = [level(mat_ref, PORT_AT + j) for j in range(3)] + [first, last]
    ports += [level(mat_ref, PORT_AT + 3), level(mat_ref, PORT_AT + 4)]
    ports += [level(w_ref, 0), level(w_ref, CZ - 1)]
    for at, value in enumerate(ports):
        for half in range(2):
            send_ref[pl.ds(half * SEND_ROWS + at, CX, stride=2 * SEND_ROWS), :] = value[
                :, half * LANES : (half + 1) * LANES
            ]

    zero = jnp.zeros(shape, F32)
    constant = expand(zero, zero, to_first, to_next, offsets)
    onehot, row_mask = panel_masks(cell_ref[...])
    at_panel = pick(jnp.concatenate(constant, 0), onehot, row_mask)
    terms = [0.0, 0.0, 0.0]
    for half in range(2):
        lanes = slice(half * LANES, (half + 1) * LANES)
        in_section = row_iota((8, LANES)).astype(F32) == panel_ref[13 + half : 14 + half, :]
        for k in range(3):
            row = panel_ref[1 + 2 * k + half : 2 + 2 * k + half, :] * at_panel[:, lanes]
            terms[k] = terms[k] + jnp.where(in_section, row, 0.0)
    constant_ref[...] = jnp.zeros_like(constant_ref)
    for k, row in enumerate(section_rows(terms)):
        constant_ref[k : k + 1, :] = row


def owner_kernel(recv_ref, constant_ref, back_ref, group_ref, ends_ref, parts_ref, picked_ref):
    def value(at, x):
        return recv_ref[pl.ds(x * SEND_ROWS + at, 4, stride=4 * SEND_ROWS), :]

    per = [[value(at, x) for x in range(4)] for at in range(9)]
    low_k, high_k, link, low_r, high_r, low_d, high_d, low_w, high_w = per
    join = [2.0 / (high_d[x] + low_d[x + 1]) for x in range(3)]
    for x in range(3):
        high_r[x] = high_r[x] - HALF_DIV * low_w[x + 1]
        low_r[x + 1] = low_r[x + 1] + HALF_DIV * high_w[x]
    ground, source, edges = [], [], []
    for x in range(4):
        ground += [low_k[x], high_k[x]]
        source += [low_r[x], high_r[x]]
        edges += [link[x]] + ([join[x]] if x < 3 else [])
    first, last, across, to_first, to_next, inverse = condense(ground, edges)
    first_r, last_r, offsets = condense_source(source, to_first, to_next, inverse)

    stored = [first, last, across, first_r, last_r, low_d[0], high_d[3], low_w[0], high_w[3]]
    for at, x in enumerate(stored):
        group_ref[at * 4 : (at + 1) * 4, :] = x
    per = [[group_ref[at * 4 + z : at * 4 + z + 1, :] for z in range(4)] for at in range(9)]
    low_k, high_k, link, low_r, high_r, low_d, high_d, low_w, high_w = per
    outer = [2.0 / (high_d[z] + low_d[z + 1]) for z in range(3)]
    for z in range(3):
        high_r[z] = high_r[z] - HALF_DIV * low_w[z + 1]
        low_r[z + 1] = low_r[z + 1] + HALF_DIV * high_w[z]
    ground, source, edges = [], [], []
    for z in range(4):
        ground += [low_k[z], high_k[z]]
        source += [low_r[z], high_r[z]]
        edges += [link[z]] + ([outer[z]] if z < 3 else [])
    k_a, k_b, f_ab, a_list, b_list, i_list = condense(ground, edges)
    r_a, r_b, o_list = condense_source(source, a_list, b_list, i_list)
    scale = 1.0 / (k_a * k_b + f_ab * (k_a + k_b))
    p_a = ((k_b + f_ab) * r_a + f_ab * r_b) * scale
    p_b = ((k_a + f_ab) * r_b + f_ab * r_a) * scale
    nodes = expand(p_a, p_b, a_list, b_list, o_list)
    zero_row = jnp.zeros((1, LANES), F32)
    flux = [outer[z] * (nodes[2 * z + 2] - nodes[2 * z + 1]) for z in range(3)]
    for z in range(4):
        ends_ref[z : z + 1, :] = nodes[2 * z]
        ends_ref[4 + z : 5 + z, :] = nodes[2 * z + 1]
        ends_ref[8 + z : 9 + z, :] = flux[z - 1] if z > 0 else zero_row
        ends_ref[12 + z : 13 + z, :] = flux[z] if z < 3 else zero_row

    nodes = expand(ends_ref[0:4, :], ends_ref[4:8, :], to_first, to_next, offsets)
    inner = [join[x] * (nodes[2 * x + 2] - nodes[2 * x + 1]) for x in range(3)]
    below = [ends_ref[8:12, :]] + inner
    above = inner + [ends_ref[12:16, :]]

    def put(ref, rows, at, x, what):
        ref[pl.ds(x * rows + at, 4, stride=4 * rows), :] = what

    for x in range(4):
        put(back_ref, BACK_ROWS, 0, x, nodes[2 * x])
        put(back_ref, BACK_ROWS, 1, x, nodes[2 * x + 1])
        put(back_ref, BACK_ROWS, 2, x, below[x])
        put(back_ref, BACK_ROWS, 3, x, above[x])
        for end in range(2):
            for at, part in enumerate(split_three(nodes[2 * x + end])):
                put(parts_ref, 8, 3 * end + at, x, part.astype(F32))
            put(parts_ref, 8, 6 + end, x, jnp.zeros((4, LANES), F32))

    mine = lax.axis_index("col") * LANES
    want = (row_iota((LANES, LANES)) + mine).astype(F32)
    for block in range(COLS):
        ends = parts_ref[block * 8 : (block + 1) * 8, :].astype(jnp.bfloat16)
        at = block * SEND_ROWS + 9 + 10
        for half in range(2):
            column = recv_ref[at + half : at + half + 1, :]
            onehot = jnp.where(want == column, 1.0, 0.0).astype(jnp.bfloat16)
            got = jnp.dot(ends, onehot, preferred_element_type=F32)
            picked_ref[(half * COLS + block) * 8 : (half * COLS + block + 1) * 8, :] = got
    sums = [[None] * 8 for _ in range(3)]
    for half in range(2):

        def panel(at):
            return recv_ref[pl.ds(9 + 2 * at + half, COLS, stride=SEND_ROWS), :]

        def got(at):
            return picked_ref[pl.ds(half * COLS * 8 + at, COLS, stride=8), :]

        low = got(0) + got(1) + got(2)
        high = got(3) + got(4) + got(5)
        at_panel = panel(3) * low + panel(4) * high
        section = panel(6)
        for k in range(3):
            term = panel(k) * at_panel
            for j in range(8):
                part = jnp.where(section == float(j), term, 0.0)
                part = part[0:8, :] + part[8:16, :]
                sums[k][j] = part if half == 0 else sums[k][j] + part
    terms = [
        jnp.concatenate([jnp.sum(x, axis=0, keepdims=True) for x in sums[k]], 0)
        for k in range(3)
    ]
    rows = section_rows(terms)
    for block in range(COLS):
        for k in range(3):
            at = block * BACK_ROWS + 4 + k
            back_ref[at : at + 1, :] = rows[k] + constant_ref[k : k + 1, :]
        back_ref[block * BACK_ROWS + 7 : block * BACK_ROWS + 8, :] = zero_row


def load_kernel(back_ref, load_ref):
    load_ref[...] = jnp.zeros_like(load_ref)
    for k in range(3):
        rows = back_ref[pl.ds(4 + k, COLS, stride=BACK_ROWS), :]
        load_ref[k : k + 1, :] = jnp.sum(rows, axis=0, keepdims=True)


def field_kernel(back_ref, mat_ref, offset_ref, w_ref, pressure_ref, velocity_ref):
    def end(at):
        halves = [
            back_ref[pl.ds(half * BACK_ROWS + at, CX, stride=2 * BACK_ROWS), :] for half in range(2)
        ]
        return jnp.concatenate(halves, axis=1)

    to_first = [level(mat_ref, A_AT + j) for j in range(CZ - 2)]
    to_next = [level(mat_ref, B_AT + j) for j in range(CZ - 2)]
    offsets = [level(offset_ref, j) for j in range(CZ - 2)]
    pressure = expand(end(0), end(1), to_first, to_next, offsets)
    flux = [end(2)]
    for z in range(CZ - 1):
        flux.append(level(mat_ref, FACE_AT + z) * (pressure[z + 1] - pressure[z]))
    flux.append(end(3))
    for z in range(CZ):
        pressure_ref[z * CX : (z + 1) * CX, :] = pressure[z]
        velocity_ref[z * CX : (z + 1) * CX, :] = level(w_ref, z) - 0.5 * (flux[z + 1] + flux[z])


def section_kernel(load_ref, pair_ref, other_ref, out_ref):
    even = lax.rem(lax.axis_index("slab"), 2) == 0
    received, beyond = pair_ref[...], other_ref[...]
    from_left = jnp.where(even, beyond, received)
    from_right = jnp.where(even, received, beyond)
    lanes = lane_iota((8, LANES))
    total = load_ref[...]
    total = total + jnp.where(lanes < 4, pltpu.roll(from_left, LANES - 4, 1), 0.0)
    total = total + jnp.where(lanes >= 4, pltpu.roll(from_right, 4, 1), 0.0)
    total = pltpu.roll(total, LANES - REACH, 1)
    out_ref[...] = total[0:3, 0:SEC_DEV]


def call(kernel, outs, scratch=(), flops=20000):
    shapes = [jax.ShapeDtypeStruct(shape, F32) for shape in outs]
    return pl.pallas_call(
        kernel,
        out_shape=shapes if len(shapes) > 1 else shapes[0],
        scratch_shapes=[pltpu.VMEM(shape, F32) for shape in scratch],
        compiler_params=pltpu.CompilerParams(vmem_limit_bytes=16 * 1024 * 1024),
        cost_estimate=pl.CostEstimate(flops=flops, bytes_accessed=500000, transcendentals=0),
    )


def per_device(p_star, u_star, v_star, w_star, flags, panel_cell, panel_section, panel_geom):
    flat = (CZ * CX, NY)
    p, u, v, w = (x.reshape(flat) for x in (p_star, u_star, v_star, w_star))
    flags = flags.reshape(flat)
    cell = panel_cell.reshape(1, PANELS_DEV)
    section = panel_section.reshape(1, PANELS_DEV)
    slabs = lax.axis_size("slab")
    pairs = [(i, i ^ 1) for i in range(slabs)]
    others = [(i, i + 1) for i in range(1, slabs - 1, 2)]
    others += [(j, i) for i, j in others]

    leading = GAMMA_HORIZ * p_star[:, :1, :] - HALF_DIV * u_star[:, :1, :]
    trailing = GAMMA_HORIZ * p_star[:, CX - 1 :, :] + HALF_DIV * u_star[:, CX - 1 :, :]
    to_other = call(choose_kernel, [(CZ, NY)], flops=2000000000)(leading, trailing)
    from_other = lax.ppermute(to_other, "slab", others)
    mat, source, panel, plane = call(
        matrix_kernel, [(MAT_LEVELS * CX, NY), flat, (16, LANES), (CZ, NY)], flops=5000000
    )(p, u, v, w, flags, cell, section, panel_geom)
    from_pair = lax.ppermute(plane, "slab", pairs)
    send, offsets, constant = call(
        pack_kernel,
        [(COLS * SEND_ROWS, LANES), ((CZ - 2) * CX, NY), (8, LANES)],
    )(mat, source, from_pair, from_other, w, panel, cell)
    recv = lax.all_to_all(send, "col", 0, 0, tiled=True)
    back = call(
        owner_kernel,
        [(COLS * BACK_ROWS, LANES)],
        [(40, LANES), (16, LANES), (COLS * 8, LANES), (2 * COLS * 8, LANES)],
    )(recv, constant)
    back = lax.all_to_all(back, "col", 0, 0, tiled=True)
    loads = call(load_kernel, [(8, LANES)])(back)
    loads_other = lax.ppermute(loads, "slab", others)
    loads_pair = lax.ppermute(loads, "slab", pairs)
    pressure, velocity = call(field_kernel, [flat, flat], flops=5000000)(back, mat, offsets, w)
    section_loads = call(section_kernel, [(3, SEC_DEV)])(loads, loads_pair, loads_other)
    return pressure.reshape(p_star.shape), velocity.reshape(p_star.shape), section_loads


def solution(mesh):
    in_specs = (
        P("col", "slab", None),
        P("col", "slab", None),
        P("col", "slab", None),
        P("col", "slab", None),
        P("col", "slab", None),
        P(("col", "slab")),
        P(("col", "slab")),
        P(None, ("col", "slab")),
    )
    out_specs = (P("col", "slab", None), P("col", "slab", None), P(None, "slab"))
    return jax.shard_map(
        per_device, mesh=mesh, in_specs=in_specs, out_specs=out_specs, check_vma=False
    )
```

```python
import functools

import jax
import jax.numpy as jnp
from jax import lax
from jax.experimental import pallas as pl
from jax.experimental.pallas import tpu as pltpu
from jax.sharding import PartitionSpec as P

SEC_DEV = 4
EOS_ITERS = 3
KAPPA_SCALE = 0.01
AIR_DENSITY = 0.1
GAMMA_HORIZ = 0.001
DIVERGENCE_SCALE = 0.005
HALF_DIV = 0.5 * DIVERGENCE_SCALE

CZ = 8
CX = 8
NY = 256
LANES = 128
COLS = 16
PANELS_DEV = 256
REACH = 2
OWNERS = 8
SEND_ROWS = 32
BACK_ROWS = 16
GEOM_ROW, FIRST_ROW, LAST_ROW, COLUMN_ROW, META_ROW = 18, 24, 26, 28, 30

F32 = jnp.float32


def row_iota(shape):
    return lax.broadcasted_iota(jnp.int32, shape, 0)


def lane_iota(shape):
    return lax.broadcasted_iota(jnp.int32, shape, 1)


def level(ref, z):
    return ref[z * CX : (z + 1) * CX, :]


def split_three(x):
    high = x.astype(jnp.bfloat16)
    rest = x - high.astype(F32)
    middle = rest.astype(jnp.bfloat16)
    low = (rest - middle.astype(F32)).astype(jnp.bfloat16)
    return high, middle, low


def pick(fields, onehot, row_mask):
    total = None
    for part in split_three(fields):
        term = jnp.dot(part, onehot, preferred_element_type=F32)
        total = term if total is None else total + term
    return jnp.sum(jnp.where(row_mask, total, 0.0), axis=0, keepdims=True)


def panel_masks(cell):
    onehot = (row_iota((NY, PANELS_DEV)) == (cell & (NY - 1))).astype(F32)
    row_mask = row_iota((CZ * CX, PANELS_DEV)) == (cell >> 8)
    return onehot.astype(jnp.bfloat16), row_mask


def condense(ground, edges):
    first, here, link = ground[0], ground[1], edges[0]
    to_first, to_next, inverse = [], [], []
    for j in range(1, len(ground) - 1):
        edge = edges[j]
        inv = 1.0 / (here + link + edge)
        a, b = link * inv, edge * inv
        first = first + a * here
        here = ground[j + 1] + b * here
        link = link * b
        to_first.append(a)
        to_next.append(b)
        inverse.append(inv)
    return first, here, link, to_first, to_next, inverse


def condense_source(source, to_first, to_next, inverse):
    first, here = source[0], source[1]
    offsets = []
    for j in range(1, len(source) - 1):
        a, b = to_first[j - 1], to_next[j - 1]
        offsets.append(here * inverse[j - 1])
        first = first + a * here
        here = source[j + 1] + b * here
    return first, here, offsets


def expand(first, last, to_first, to_next, offsets):
    values = [last]
    for a, b, offset in zip(reversed(to_first), reversed(to_next), reversed(offsets)):
        values.append(offset + a * first + b * values[-1])
    values.append(first)
    return values[::-1]


def to_row(column):
    on_diagonal = row_iota((8, LANES)) == lane_iota((8, LANES))
    return jnp.sum(jnp.where(on_diagonal, column, 0.0), axis=0, keepdims=True)


def section_rows(terms):
    return [to_row(jnp.sum(term, axis=1, keepdims=True)) for term in terms]


def sort_panels(section, rows):
    square = (PANELS_DEV, PANELS_DEV)
    key = section * PANELS_DEV + lane_iota((1, PANELS_DEV))
    key = key.astype(F32)
    on_diagonal = row_iota(square) == lane_iota(square)
    key_column = jnp.sum(jnp.where(on_diagonal, key, 0.0), axis=1, keepdims=True)
    rank = jnp.sum(jnp.where(key < key_column, 1.0, 0.0), axis=1, keepdims=True)
    order = jnp.where(lane_iota(square).astype(F32) == rank, 1.0, 0.0).astype(jnp.bfloat16)
    total = None
    for part in split_three(rows):
        term = jnp.dot(part, order, preferred_element_type=F32)
        total = term if total is None else total + term
    return total


def choose_kernel(leading_ref, trailing_ref, plane_ref):
    even = lax.rem(lax.axis_index("slab"), 2) == 0
    for z in range(CZ):
        plane_ref[z : z + 1, :] = jnp.where(even, leading_ref[z], trailing_ref[z])


A_AT, B_AT, I_AT, FACE_AT, PORT_AT = 0, 6, 12, 18, 25
MAT_LEVELS = 30


def matrix_kernel(
    p_ref, u_ref, v_ref, w_ref, flags_ref, cell_ref, sec_ref, geom_ref,
    mat_ref, src_ref, panel_ref, bound_ref, sorted_ref, plane_ref,
):
    even = lax.rem(lax.axis_index("slab"), 2) == 0
    for z in range(CZ):
        p, u = level(p_ref, z), level(u_ref, z)
        plane_ref[z : z + 1, :] = jnp.where(
            even,
            GAMMA_HORIZ * p[CX - 1 :, :] + HALF_DIV * u[CX - 1 :, :],
            GAMMA_HORIZ * p[:1, :] - HALF_DIV * u[:1, :],
        )
    shape = (CX, NY)
    rows, lanes = row_iota(shape), lane_iota(shape)
    densities, kappas = [], []
    for z in range(CZ):
        p, flags = level(p_ref, z), level(flags_ref, z)
        air = jnp.where(flags == 1, 1.0, jnp.where(flags == 2, 0.5, 0.0)).astype(F32)
        water = jnp.ones_like(p)
        for _ in range(EOS_ITERS):
            square = water * water
            cube = square * water
            sixth = cube * cube
            water = water - (sixth * water - 1.0 - p) / (7.0 * sixth)
        shifted = 1.0 + p
        air_density = AIR_DENSITY * jnp.exp(jnp.log(shifted) * (1.0 / 1.4))
        densities.append(air * air_density + (1.0 - air) * water)
        kappa = KAPPA_SCALE * (air / (1.4 * shifted) + (1.0 - air) / (7.0 * shifted))
        kappas.append(kappa)

        u, v = level(u_ref, z), level(v_ref, z)

        def beside(x, axis, step):
            size = shape[axis]
            moved = pltpu.roll(x, (-step) % size, axis)
            at = rows if axis == 0 else lanes
            return jnp.where(at == (size - 1 if step > 0 else 0), 0.0, moved)

        laplacian = (
            beside(p, 0, 1) + beside(p, 0, -1) + beside(p, 1, 1) + beside(p, 1, -1) - 4.0 * p
        )
        divergence = 0.5 * (beside(u, 0, 1) - beside(u, 0, -1)) + 0.5 * (
            beside(v, 1, 1) - beside(v, 1, -1)
        )
        if z == 0:
            w_difference = level(w_ref, 1)
        elif z == CZ - 1:
            w_difference = -level(w_ref, CZ - 2)
        else:
            w_difference = level(w_ref, z + 1) - level(w_ref, z - 1)
        divergence = divergence + 0.5 * w_difference
        src_ref[z * CX : (z + 1) * CX, :] = (
            kappa * p + GAMMA_HORIZ * laplacian - DIVERGENCE_SCALE * divergence
        )
    faces = [2.0 / (densities[z] + densities[z + 1]) for z in range(CZ - 1)]
    first, last, link, to_first, to_next, inverse = condense(kappas, faces)
    stored = to_first + to_next + inverse + faces + [first, last, link, densities[0], densities[-1]]
    for at, value in enumerate(stored):
        mat_ref[at * CX : (at + 1) * CX, :] = value

    zero, one = jnp.zeros(shape, F32), jnp.ones(shape, F32)
    no_offset = [zero] * (CZ - 2)
    section = sec_ref[...] - (lax.axis_index("slab") * SEC_DEV - REACH)
    rows = [geom_ref[k : k + 1, :] for k in range(3)] + [cell_ref[...].astype(F32)]
    rows = sort_panels(section, jnp.concatenate(rows + [jnp.zeros((4, PANELS_DEV), F32)], 0))
    sorted_ref[...] = rows
    at_section = row_iota((8, PANELS_DEV))
    starts = jnp.sum(jnp.where(section < at_section, 1.0, 0.0), axis=1, keepdims=True)
    stops = jnp.sum(jnp.where(section <= at_section, 1.0, 0.0), axis=1, keepdims=True)
    bound_ref[0:8, :] = jnp.broadcast_to(starts, (8, LANES))
    bound_ref[8:16, :] = jnp.broadcast_to(stops, (8, LANES))

    cell = rows[3:4, :].astype(jnp.int32)
    onehot, row_mask = panel_masks(cell)
    from_first = expand(one, zero, to_first, to_next, no_offset)
    from_last = expand(zero, one, to_first, to_next, no_offset)
    panel_rows = [rows[k : k + 1, :] for k in range(3)]
    panel_rows.append(pick(jnp.concatenate(from_first, 0), onehot, row_mask))
    panel_rows.append(pick(jnp.concatenate(from_last, 0), onehot, row_mask))
    panel_rows.append((cell & (CX * NY - 1)).astype(F32))
    panel_ref[...] = jnp.zeros_like(panel_ref)
    for at, row in enumerate(panel_rows):
        for half in range(2):
            panel_ref[2 + 2 * at + half : 3 + 2 * at + half, :] = row[
                :, half * LANES : (half + 1) * LANES
            ]
    panel_ref[META_ROW - 16 : META_ROW - 15, :] = to_row(starts)


def pack_kernel(
    mat_ref, src_ref, pair_ref, other_ref, w_ref, panel_ref, bound_ref, sorted_ref,
    send_ref, offset_ref,
):
    even = lax.rem(lax.axis_index("slab"), 2) == 0
    shape = (CX, NY)
    rows = row_iota(shape)
    received, beyond = pair_ref[...], other_ref[...]
    from_left = jnp.where(even, beyond, received)
    from_right = jnp.where(even, received, beyond)
    source = []
    for z in range(CZ):
        halo = jnp.where(rows == 0, from_left[z : z + 1, :], 0.0) + jnp.where(
            rows == CX - 1, from_right[z : z + 1, :], 0.0
        )
        source.append(level(src_ref, z) + halo)
    to_first = [level(mat_ref, A_AT + j) for j in range(CZ - 2)]
    to_next = [level(mat_ref, B_AT + j) for j in range(CZ - 2)]
    inverse = [level(mat_ref, I_AT + j) for j in range(CZ - 2)]
    first, last, offsets = condense_source(source, to_first, to_next, inverse)
    for j, offset in enumerate(offsets):
        offset_ref[j * CX : (j + 1) * CX, :] = offset

    zero = jnp.zeros(shape, F32)
    constant = expand(zero, zero, to_first, to_next, offsets)
    onehot, row_mask = panel_masks(sorted_ref[3:4, :].astype(jnp.int32))
    at_panel = pick(jnp.concatenate(constant, 0), onehot, row_mask)
    terms = [0.0, 0.0, 0.0]
    for half in range(2):
        lanes = slice(half * LANES, (half + 1) * LANES)
        place = (lane_iota((8, LANES)) + half * LANES).astype(F32)
        in_section = (place >= bound_ref[0:8, :]) & (place < bound_ref[8:16, :])
        for k in range(3):
            row = sorted_ref[k : k + 1, lanes] * at_panel[:, lanes]
            terms[k] = terms[k] + jnp.where(in_section, row, 0.0)
    meta = panel_ref[META_ROW - 16 : META_ROW - 15, :]
    for k, row in enumerate(section_rows(terms)):
        meta = meta + pltpu.roll(row, 8 * (k + 1), 1)

    for device in range(COLS):
        send_ref[device * SEND_ROWS + 16 : (device + 1) * SEND_ROWS, :] = panel_ref[...]
    for device in range(COLS):
        at = device * SEND_ROWS + META_ROW
        send_ref[at : at + 1, :] = meta
    ports = [level(mat_ref, PORT_AT + j) for j in range(3)] + [first, last]
    ports += [level(mat_ref, PORT_AT + 3), level(mat_ref, PORT_AT + 4)]
    ports += [level(w_ref, 0), level(w_ref, CZ - 1)]
    for at, value in enumerate(ports):
        for half in range(2):
            row = half * 8 + at if at < 8 else 16 + half
            for group in range(0, COLS, OWNERS):
                send_ref[pl.ds(group * SEND_ROWS + row, OWNERS, stride=SEND_ROWS), :] = value[
                    :, half * LANES : (half + 1) * LANES
                ]


def solve_columns(half, recv_ref, group_ref, ends_ref, all_ref, parts_ref):
    def value(at, x):
        row = half * 8 + at if at < 8 else 16 + half
        return recv_ref[pl.ds(x * SEND_ROWS + row, 4, stride=4 * SEND_ROWS), :]

    per = [[value(at, x) for x in range(4)] for at in range(9)]
    low_k, high_k, link, low_r, high_r, low_d, high_d, low_w, high_w = per
    join = [2.0 / (high_d[x] + low_d[x + 1]) for x in range(3)]
    for x in range(3):
        high_r[x] = high_r[x] - HALF_DIV * low_w[x + 1]
        low_r[x + 1] = low_r[x + 1] + HALF_DIV * high_w[x]
    ground, source, edges = [], [], []
    for x in range(4):
        ground += [low_k[x], high_k[x]]
        source += [low_r[x], high_r[x]]
        edges += [link[x]] + ([join[x]] if x < 3 else [])
    first, last, across, to_first, to_next, inverse = condense(ground, edges)
    first_r, last_r, offsets = condense_source(source, to_first, to_next, inverse)

    stored = [first, last, across, first_r, last_r, low_d[0], high_d[3], low_w[0], high_w[3]]
    for at, x in enumerate(stored):
        group_ref[half, at * 4 : (at + 1) * 4, :] = x
    per = [[group_ref[half, at * 4 + z : at * 4 + z + 1, :] for z in range(4)] for at in range(9)]
    low_k, high_k, link, low_r, high_r, low_d, high_d, low_w, high_w = per
    outer = [2.0 / (high_d[z] + low_d[z + 1]) for z in range(3)]
    for z in range(3):
        high_r[z] = high_r[z] - HALF_DIV * low_w[z + 1]
        low_r[z + 1] = low_r[z + 1] + HALF_DIV * high_w[z]
    ground, source, edges = [], [], []
    for z in range(4):
        ground += [low_k[z], high_k[z]]
        source += [low_r[z], high_r[z]]
        edges += [link[z]] + ([outer[z]] if z < 3 else [])
    k_a, k_b, f_ab, a_list, b_list, i_list = condense(ground, edges)
    r_a, r_b, o_list = condense_source(source, a_list, b_list, i_list)
    scale = 1.0 / (k_a * k_b + f_ab * (k_a + k_b))
    p_a = ((k_b + f_ab) * r_a + f_ab * r_b) * scale
    p_b = ((k_a + f_ab) * r_b + f_ab * r_a) * scale
    nodes = expand(p_a, p_b, a_list, b_list, o_list)
    zero_row = jnp.zeros((1, LANES), F32)
    flux = [outer[z] * (nodes[2 * z + 2] - nodes[2 * z + 1]) for z in range(3)]
    for z in range(4):
        ends_ref[half, z : z + 1, :] = nodes[2 * z]
        ends_ref[half, 4 + z : 5 + z, :] = nodes[2 * z + 1]
        ends_ref[half, 8 + z : 9 + z, :] = flux[z - 1] if z > 0 else zero_row
        ends_ref[half, 12 + z : 13 + z, :] = flux[z] if z < 3 else zero_row

    nodes = expand(ends_ref[half, 0:4, :], ends_ref[half, 4:8, :], to_first, to_next, offsets)
    inner = [join[x] * (nodes[2 * x + 2] - nodes[2 * x + 1]) for x in range(3)]
    below = [ends_ref[half, 8:12, :]] + inner
    above = inner + [ends_ref[half, 12:16, :]]

    def put(ref, rows, at, x, what):
        ref[pl.ds(x * rows + at, 4, stride=4 * rows), :] = what

    for x in range(4):
        for at, what in enumerate([nodes[2 * x], nodes[2 * x + 1], below[x], above[x]]):
            put(all_ref, BACK_ROWS, half * 4 + at, x, what)
        for end in range(2):
            for at, part in enumerate(split_three(nodes[2 * x + end])):
                put(parts_ref, 16, half * 8 + 3 * end + at, x, part.astype(F32))
            put(parts_ref, 16, half * 8 + 6 + end, x, jnp.zeros((4, LANES), F32))


def owner_kernel(
    recv_ref, back_ref, group_ref, ends_ref, all_ref, parts_ref, place_ref, picked_ref
):
    for half in range(2):
        solve_columns(half, recv_ref, group_ref, ends_ref, all_ref, parts_ref)

    column_device = lax.axis_index("col")
    mine = lax.rem(column_device, OWNERS) * NY

    def panel(row):
        return recv_ref[pl.ds(row, COLS, stride=SEND_ROWS), :]

    inside, upper = [], []
    for half in range(2):
        place = panel(COLUMN_ROW + half).astype(jnp.int32) - mine
        inside.append((place >= 0) & (place < NY))
        upper.append(place >= LANES)
        place_ref[half * COLS : (half + 1) * COLS, :] = (place & (LANES - 1)).astype(F32)
    want = row_iota((LANES, LANES)).astype(F32)
    for block in range(COLS):
        ends = parts_ref[block * 16 : (block + 1) * 16, :].astype(jnp.bfloat16)
        for half in range(2):
            at = half * COLS + block
            onehot = jnp.where(want == place_ref[at : at + 1, :], 1.0, 0.0).astype(jnp.bfloat16)
            got = jnp.dot(ends, onehot, preferred_element_type=F32)
            picked_ref[at * 16 : (at + 1) * 16, :] = got
    meta = panel(META_ROW)
    starts = [meta[:, j : j + 1] for j in range(8)] + [float(PANELS_DEV)]
    sums = [[None] * 8 for _ in range(3)]
    for half in range(2):

        def got(at):
            return picked_ref[pl.ds(half * COLS * 16 + at, COLS, stride=16), :]

        low = [got(8 * h) + got(8 * h + 1) + got(8 * h + 2) for h in range(2)]
        high = [got(8 * h + 3) + got(8 * h + 4) + got(8 * h + 5) for h in range(2)]
        low = jnp.where(upper[half], low[1], low[0])
        high = jnp.where(upper[half], high[1], high[0])
        at_panel = panel(FIRST_ROW + half) * low + panel(LAST_ROW + half) * high
        at_panel = jnp.where(inside[half], at_panel, 0.0)
        place = (lane_iota((COLS, LANES)) + half * LANES).astype(F32)
        reached = [place >= start for start in starts]
        terms = [panel(GEOM_ROW + 2 * k + half) * at_panel for k in range(3)]
        for j in range(8):
            in_section = reached[j] & jnp.logical_not(reached[j + 1])
            for k in range(3):
                part = jnp.where(in_section, terms[k], 0.0)
                part = part[0:8, :] + part[8:16, :]
                sums[k][j] = part if half == 0 else sums[k][j] + part
    terms = [
        jnp.concatenate([jnp.sum(x, axis=0, keepdims=True) for x in sums[k]], 0)
        for k in range(3)
    ]
    constant = jnp.sum(meta, axis=0, keepdims=True)
    lanes = lane_iota((1, LANES))
    own = lax.rem(column_device, OWNERS) == 0
    rows = section_rows(terms)
    for k in range(3):
        moved = pltpu.roll(constant, LANES - 8 * (k + 1), 1)
        rows[k] = rows[k] + jnp.where((lanes < 8) & own, moved, 0.0)
    for block in range(COLS):
        at = block * BACK_ROWS + 8
        for k in range(3):
            all_ref[at + k : at + k + 1, :] = rows[k]
        all_ref[at + 3 : at + 8, :] = jnp.zeros((5, LANES), F32)
    mine = pl.multiple_of((column_device // OWNERS) * (OWNERS * BACK_ROWS), OWNERS * BACK_ROWS)
    back_ref[...] = all_ref[pl.ds(mine, OWNERS * BACK_ROWS), :]


def load_kernel(back_ref, load_ref):
    load_ref[...] = jnp.zeros_like(load_ref)
    for k in range(3):
        rows = back_ref[pl.ds(8 + k, OWNERS, stride=BACK_ROWS), :]
        load_ref[k : k + 1, :] = jnp.sum(rows, axis=0, keepdims=True)


def field_kernel(back_ref, mat_ref, offset_ref, w_ref, pressure_ref, velocity_ref):
    def end(at):
        halves = [back_ref[pl.ds(half * 4 + at, CX, stride=BACK_ROWS), :] for half in range(2)]
        return jnp.concatenate(halves, axis=1)

    to_first = [level(mat_ref, A_AT + j) for j in range(CZ - 2)]
    to_next = [level(mat_ref, B_AT + j) for j in range(CZ - 2)]
    offsets = [level(offset_ref, j) for j in range(CZ - 2)]
    pressure = expand(end(0), end(1), to_first, to_next, offsets)
    flux = [end(2)]
    for z in range(CZ - 1):
        flux.append(level(mat_ref, FACE_AT + z) * (pressure[z + 1] - pressure[z]))
    flux.append(end(3))
    for z in range(CZ):
        pressure_ref[z * CX : (z + 1) * CX, :] = pressure[z]
        velocity_ref[z * CX : (z + 1) * CX, :] = level(w_ref, z) - 0.5 * (flux[z + 1] + flux[z])


def section_kernel(load_ref, pair_ref, other_ref, out_ref):
    even = lax.rem(lax.axis_index("slab"), 2) == 0
    received, beyond = pair_ref[...], other_ref[...]
    from_left = jnp.where(even, beyond, received)
    from_right = jnp.where(even, received, beyond)
    lanes = lane_iota((8, LANES))
    total = load_ref[...]
    total = total + jnp.where(lanes < 4, pltpu.roll(from_left, LANES - 4, 1), 0.0)
    total = total + jnp.where(lanes >= 4, pltpu.roll(from_right, 4, 1), 0.0)
    total = pltpu.roll(total, LANES - REACH, 1)
    out_ref[...] = total[0:3, 0:SEC_DEV]


def call(kernel, outs, scratch=(), flops=20000):
    shapes = [jax.ShapeDtypeStruct(shape, F32) for shape in outs]
    return pl.pallas_call(
        kernel,
        out_shape=shapes if len(shapes) > 1 else shapes[0],
        scratch_shapes=[pltpu.VMEM(shape, F32) for shape in scratch],
        compiler_params=pltpu.CompilerParams(vmem_limit_bytes=16 * 1024 * 1024),
        cost_estimate=pl.CostEstimate(flops=flops, bytes_accessed=500000, transcendentals=0),
    )


def per_device(p_star, u_star, v_star, w_star, flags, panel_cell, panel_section, panel_geom):
    flat = (CZ * CX, NY)
    p, u, v, w = (x.reshape(flat) for x in (p_star, u_star, v_star, w_star))
    flags = flags.reshape(flat)
    cell = panel_cell.reshape(1, PANELS_DEV)
    section = panel_section.reshape(1, PANELS_DEV)
    slabs = lax.axis_size("slab")
    pairs = [(i, i ^ 1) for i in range(slabs)]
    others = [(i, i + 1) for i in range(1, slabs - 1, 2)]
    others += [(j, i) for i, j in others]

    leading = GAMMA_HORIZ * p_star[:, :1, :] - HALF_DIV * u_star[:, :1, :]
    trailing = GAMMA_HORIZ * p_star[:, CX - 1 :, :] + HALF_DIV * u_star[:, CX - 1 :, :]
    to_other = call(choose_kernel, [(CZ, NY)], flops=2000000000)(leading, trailing)
    from_other = lax.ppermute(to_other, "slab", others)
    mat, source, panel, bounds, ordered, plane = call(
        matrix_kernel,
        [(MAT_LEVELS * CX, NY), flat, (16, LANES), (16, LANES), (8, PANELS_DEV), (CZ, NY)],
        flops=5000000,
    )(p, u, v, w, flags, cell, section, panel_geom)
    from_pair = lax.ppermute(plane, "slab", pairs)
    send, offsets = call(pack_kernel, [(COLS * SEND_ROWS, LANES), ((CZ - 2) * CX, NY)])(
        mat, source, from_pair, from_other, w, panel, bounds, ordered
    )
    recv = lax.all_to_all(send, "col", 0, 0, tiled=True)
    back = call(
        owner_kernel,
        [(OWNERS * BACK_ROWS, LANES)],
        [
            (2, 40, LANES),
            (2, 16, LANES),
            (COLS * BACK_ROWS, LANES),
            (COLS * 16, LANES),
            (2 * COLS, LANES),
            (2 * COLS * 16, LANES),
        ],
    )(recv)
    sets = [list(range(at, at + OWNERS)) for at in range(0, COLS, OWNERS)]
    back = lax.all_to_all(back, "col", 0, 0, axis_index_groups=sets, tiled=True)
    loads = call(load_kernel, [(8, LANES)])(back)
    loads_other = lax.ppermute(loads, "slab", others)
    loads_pair = lax.ppermute(loads, "slab", pairs)
    pressure, velocity = call(field_kernel, [flat, flat], flops=5000000)(back, mat, offsets, w)
    section_loads = call(section_kernel, [(3, SEC_DEV)])(loads, loads_pair, loads_other)
    return pressure.reshape(p_star.shape), velocity.reshape(p_star.shape), section_loads


def solution(mesh):
    in_specs = (
        P("col", "slab", None),
        P("col", "slab", None),
        P("col", "slab", None),
        P("col", "slab", None),
        P("col", "slab", None),
        P(("col", "slab")),
        P(("col", "slab")),
        P(None, ("col", "slab")),
    )
    out_specs = (P("col", "slab", None), P("col", "slab", None), P(None, "slab"))
    return jax.shard_map(
        per_device, mesh=mesh, in_specs=in_specs, out_specs=out_specs, check_vma=False
    )
```

```python
import functools

import jax
import jax.numpy as jnp
from jax import lax
from jax.experimental import pallas as pl
from jax.experimental.pallas import tpu as pltpu
from jax.sharding import PartitionSpec as P

SEC_DEV = 4
EOS_ITERS = 3
KAPPA_SCALE = 0.01
AIR_DENSITY = 0.1
GAMMA_HORIZ = 0.001
DIVERGENCE_SCALE = 0.005
HALF_DIV = 0.5 * DIVERGENCE_SCALE

CZ = 8
CX = 8
NY = 256
LANES = 128
COLS = 16
PANELS_DEV = 256
REACH = 2
OWNERS = 8
SEND_ROWS = 32
BACK_ROWS = 16
GEOM_ROW, FIRST_ROW, LAST_ROW, COLUMN_ROW, META_ROW = 18, 24, 26, 28, 30

F32 = jnp.float32


def row_iota(shape):
    return lax.broadcasted_iota(jnp.int32, shape, 0)


def lane_iota(shape):
    return lax.broadcasted_iota(jnp.int32, shape, 1)


def level(ref, z):
    return ref[z * CX : (z + 1) * CX, :]


def split_three(x):
    high = x.astype(jnp.bfloat16)
    rest = x - high.astype(F32)
    middle = rest.astype(jnp.bfloat16)
    low = (rest - middle.astype(F32)).astype(jnp.bfloat16)
    return high, middle, low


def exact_dot(x, onehot):
    rows = x.shape[0]
    parts = jnp.concatenate(split_three(x), 0)
    got = jnp.dot(parts, onehot, preferred_element_type=F32)
    return got[:rows] + got[rows : 2 * rows] + got[2 * rows :]


def pick(fields, onehot, row_mask):
    total = exact_dot(fields, onehot)
    return jnp.sum(jnp.where(row_mask, total, 0.0), axis=0, keepdims=True)


def panel_masks(cell):
    onehot = (row_iota((NY, PANELS_DEV)) == (cell & (NY - 1))).astype(F32)
    row_mask = row_iota((CZ * CX, PANELS_DEV)) == (cell >> 8)
    return onehot.astype(jnp.bfloat16), row_mask


def halving(count):
    nodes, order = list(range(count)), []
    while len(nodes) > 2:
        gone = range(1, len(nodes) - 1, 2)
        order += [(nodes[i], nodes[i - 1], nodes[i + 1]) for i in gone]
        nodes = [node for i, node in enumerate(nodes) if i not in gone]
    return order


def condense(ground, edges):
    count = len(ground)
    ground = list(ground)
    edges = {(i, i + 1): edge for i, edge in enumerate(edges)}
    to_low, to_high, inverse = ([None] * (count - 2) for _ in range(3))
    for node, low, high in halving(count):
        inv = 1.0 / (ground[node] + edges[low, node] + edges[node, high])
        a, b = edges[low, node] * inv, edges[node, high] * inv
        to_low[node - 1], to_high[node - 1], inverse[node - 1] = a, b, inv
        ground[low] = ground[low] + a * ground[node]
        ground[high] = ground[high] + b * ground[node]
        edges[low, high] = edges[low, node] * b
    return ground[0], ground[-1], edges[0, count - 1], to_low, to_high, inverse


def condense_source(source, to_low, to_high, inverse):
    source = list(source)
    for node, low, high in halving(len(source)):
        source[low] = source[low] + to_low[node - 1] * source[node]
        source[high] = source[high] + to_high[node - 1] * source[node]
    offsets = [x * inv for x, inv in zip(source[1:-1], inverse)]
    return source[0], source[-1], offsets


def expand(first, last, to_low, to_high, offsets):
    values = [first] + [None] * len(offsets) + [last]
    for node, low, high in reversed(halving(len(values))):
        inflow = to_low[node - 1] * values[low] + to_high[node - 1] * values[high]
        values[node] = inflow if offsets[node - 1] is None else offsets[node - 1] + inflow
    return values


def to_row(column):
    on_diagonal = row_iota((8, LANES)) == lane_iota((8, LANES))
    return jnp.sum(jnp.where(on_diagonal, column, 0.0), axis=0, keepdims=True)


def section_rows(terms):
    return [to_row(jnp.sum(term, axis=1, keepdims=True)) for term in terms]


def sort_panels(section, rows):
    square = (PANELS_DEV, PANELS_DEV)
    key = section * PANELS_DEV + lane_iota((1, PANELS_DEV))
    key = key.astype(F32)
    on_diagonal = row_iota(square) == lane_iota(square)
    key_column = jnp.sum(jnp.where(on_diagonal, key, 0.0), axis=1, keepdims=True)
    rank = jnp.sum(jnp.where(key < key_column, 1.0, 0.0), axis=1, keepdims=True)
    order = jnp.where(lane_iota(square).astype(F32) == rank, 1.0, 0.0).astype(jnp.bfloat16)
    return exact_dot(rows, order)


def fetch_kernel(*refs):
    sources, targets, other_ref, pair_ref, sems = refs[:8], refs[8:16], *refs[16:]
    fetches = [
        pltpu.make_async_copy(source, target, sems.at[i])
        for i, (source, target) in enumerate(zip(sources, targets))
    ]
    for fetch in fetches:
        fetch.start()
    p_ref, u_ref = targets[:2]
    even = lax.rem(lax.axis_index("slab"), 2) == 0
    for fetch in fetches:
        fetch.wait()
    for z in range(CZ):
        first, last = z * CX, (z + 1) * CX - 1
        leading = GAMMA_HORIZ * p_ref[first : first + 1, :] - HALF_DIV * u_ref[first : first + 1, :]
        trailing = GAMMA_HORIZ * p_ref[last : last + 1, :] + HALF_DIV * u_ref[last : last + 1, :]
        other_ref[z : z + 1, :] = jnp.where(even, leading, trailing)
        pair_ref[z : z + 1, :] = jnp.where(even, trailing, leading)


A_AT, B_AT, I_AT, FACE_AT, PORT_AT = 0, 6, 12, 18, 25
MAT_LEVELS = 30


def matrix_kernel(
    p_ref, u_ref, v_ref, w_ref, flags_ref, cell_ref, sec_ref, geom_ref,
    mat_ref, src_ref, panel_ref, bound_ref, sorted_ref,
):
    shape = (CX, NY)
    rows, lanes = row_iota(shape), lane_iota(shape)
    densities, kappas = [], []
    for z in range(CZ):
        p, flags = level(p_ref, z), level(flags_ref, z)
        air = jnp.where(flags == 1, 1.0, jnp.where(flags == 2, 0.5, 0.0)).astype(F32)
        water = jnp.ones_like(p)
        for _ in range(EOS_ITERS):
            square = water * water
            cube = square * water
            sixth = cube * cube
            water = water - (sixth * water - 1.0 - p) / (7.0 * sixth)
        shifted = 1.0 + p
        air_density = AIR_DENSITY * jnp.exp(jnp.log(shifted) * (1.0 / 1.4))
        densities.append(air * air_density + (1.0 - air) * water)
        kappa = KAPPA_SCALE * (air / (1.4 * shifted) + (1.0 - air) / (7.0 * shifted))
        kappas.append(kappa)

        u, v = level(u_ref, z), level(v_ref, z)

        def beside(x, axis, step):
            size = shape[axis]
            moved = pltpu.roll(x, (-step) % size, axis)
            at = rows if axis == 0 else lanes
            return jnp.where(at == (size - 1 if step > 0 else 0), 0.0, moved)

        laplacian = (
            beside(p, 0, 1) + beside(p, 0, -1) + beside(p, 1, 1) + beside(p, 1, -1) - 4.0 * p
        )
        divergence = 0.5 * (beside(u, 0, 1) - beside(u, 0, -1)) + 0.5 * (
            beside(v, 1, 1) - beside(v, 1, -1)
        )
        if z == 0:
            w_difference = level(w_ref, 1)
        elif z == CZ - 1:
            w_difference = -level(w_ref, CZ - 2)
        else:
            w_difference = level(w_ref, z + 1) - level(w_ref, z - 1)
        divergence = divergence + 0.5 * w_difference
        src_ref[z * CX : (z + 1) * CX, :] = (
            kappa * p + GAMMA_HORIZ * laplacian - DIVERGENCE_SCALE * divergence
        )
    faces = [2.0 / (densities[z] + densities[z + 1]) for z in range(CZ - 1)]
    first, last, link, to_low, to_high, inverse = condense(kappas, faces)
    stored = to_low + to_high + inverse + faces + [first, last, link, densities[0], densities[-1]]
    for at, value in enumerate(stored):
        mat_ref[at * CX : (at + 1) * CX, :] = value

    zero, one = jnp.zeros(shape, F32), jnp.ones(shape, F32)
    no_offset = [None] * (CZ - 2)
    section = sec_ref[...] - (lax.axis_index("slab") * SEC_DEV - REACH)
    rows = [geom_ref[k : k + 1, :] for k in range(3)] + [cell_ref[...].astype(F32)]
    rows = sort_panels(section, jnp.concatenate(rows + [jnp.zeros((4, PANELS_DEV), F32)], 0))
    sorted_ref[...] = rows
    at_section = row_iota((8, PANELS_DEV))
    starts = jnp.sum(jnp.where(section < at_section, 1.0, 0.0), axis=1, keepdims=True)
    stops = jnp.sum(jnp.where(section <= at_section, 1.0, 0.0), axis=1, keepdims=True)
    bound_ref[0:8, :] = jnp.broadcast_to(starts, (8, LANES))
    bound_ref[8:16, :] = jnp.broadcast_to(stops, (8, LANES))

    cell = rows[3:4, :].astype(jnp.int32)
    onehot, row_mask = panel_masks(cell)
    from_first = expand(one, zero, to_low, to_high, no_offset)
    from_last = expand(zero, one, to_low, to_high, no_offset)
    panel_rows = [rows[k : k + 1, :] for k in range(3)]
    panel_rows.append(pick(jnp.concatenate(from_first, 0), onehot, row_mask))
    panel_rows.append(pick(jnp.concatenate(from_last, 0), onehot, row_mask))
    panel_rows.append((cell & (CX * NY - 1)).astype(F32))
    panel_ref[...] = jnp.zeros_like(panel_ref)
    for at, row in enumerate(panel_rows):
        for half in range(2):
            panel_ref[2 + 2 * at + half : 3 + 2 * at + half, :] = row[
                :, half * LANES : (half + 1) * LANES
            ]
    panel_ref[META_ROW - 16 : META_ROW - 15, :] = to_row(starts)


def pack_kernel(
    mat_ref, src_ref, other_ref, pair_ref, w_ref, panel_ref, bound_ref, sorted_ref,
    send_ref, offset_ref,
):
    even = lax.rem(lax.axis_index("slab"), 2) == 0
    shape = (CX, NY)
    rows = row_iota(shape)
    received, beyond = pair_ref[...], other_ref[...]
    from_left = jnp.where(even, beyond, received)
    from_right = jnp.where(even, received, beyond)
    source = []
    for z in range(CZ):
        halo = jnp.where(rows == 0, from_left[z : z + 1, :], 0.0) + jnp.where(
            rows == CX - 1, from_right[z : z + 1, :], 0.0
        )
        source.append(level(src_ref, z) + halo)
    to_low = [level(mat_ref, A_AT + j) for j in range(CZ - 2)]
    to_high = [level(mat_ref, B_AT + j) for j in range(CZ - 2)]
    inverse = [level(mat_ref, I_AT + j) for j in range(CZ - 2)]
    first, last, offsets = condense_source(source, to_low, to_high, inverse)
    for j, offset in enumerate(offsets):
        offset_ref[j * CX : (j + 1) * CX, :] = offset

    zero = jnp.zeros(shape, F32)
    constant = expand(zero, zero, to_low, to_high, offsets)
    onehot, row_mask = panel_masks(sorted_ref[3:4, :].astype(jnp.int32))
    at_panel = pick(jnp.concatenate(constant, 0), onehot, row_mask)
    terms = [0.0, 0.0, 0.0]
    for half in range(2):
        lanes = slice(half * LANES, (half + 1) * LANES)
        place = (lane_iota((8, LANES)) + half * LANES).astype(F32)
        in_section = (place >= bound_ref[0:8, :]) & (place < bound_ref[8:16, :])
        for k in range(3):
            row = sorted_ref[k : k + 1, lanes] * at_panel[:, lanes]
            terms[k] = terms[k] + jnp.where(in_section, row, 0.0)
    meta = panel_ref[META_ROW - 16 : META_ROW - 15, :]
    for k, row in enumerate(section_rows(terms)):
        meta = meta + pltpu.roll(row, 8 * (k + 1), 1)

    for device in range(COLS):
        send_ref[device * SEND_ROWS + 16 : (device + 1) * SEND_ROWS, :] = panel_ref[...]
    for device in range(COLS):
        at = device * SEND_ROWS + META_ROW
        send_ref[at : at + 1, :] = meta
    ports = [level(mat_ref, PORT_AT + j) for j in range(3)] + [first, last]
    ports += [level(mat_ref, PORT_AT + 3), level(mat_ref, PORT_AT + 4)]
    ports += [level(w_ref, 0), level(w_ref, CZ - 1)]
    for at, value in enumerate(ports):
        for half in range(2):
            row = half * 8 + at if at < 8 else 16 + half
            for group in range(0, COLS, OWNERS):
                send_ref[pl.ds(group * SEND_ROWS + row, OWNERS, stride=SEND_ROWS), :] = value[
                    :, half * LANES : (half + 1) * LANES
                ]


def solve_columns(half, recv_ref, group_ref, ends_ref, all_ref, parts_ref):
    def value(at, x):
        row = half * 8 + at if at < 8 else 16 + half
        return recv_ref[pl.ds(x * SEND_ROWS + row, 4, stride=4 * SEND_ROWS), :]

    per = [[value(at, x) for x in range(4)] for at in range(9)]
    low_k, high_k, link, low_r, high_r, low_d, high_d, low_w, high_w = per
    join = [2.0 / (high_d[x] + low_d[x + 1]) for x in range(3)]
    for x in range(3):
        high_r[x] = high_r[x] - HALF_DIV * low_w[x + 1]
        low_r[x + 1] = low_r[x + 1] + HALF_DIV * high_w[x]
    ground, source, edges = [], [], []
    for x in range(4):
        ground += [low_k[x], high_k[x]]
        source += [low_r[x], high_r[x]]
        edges += [link[x]] + ([join[x]] if x < 3 else [])
    first, last, across, to_low, to_high, inverse = condense(ground, edges)
    first_r, last_r, offsets = condense_source(source, to_low, to_high, inverse)

    stored = [first, last, across, first_r, last_r, low_d[0], high_d[3], low_w[0], high_w[3]]
    for at, x in enumerate(stored):
        group_ref[half, at * 4 : (at + 1) * 4, :] = x
    per = [[group_ref[half, at * 4 + z : at * 4 + z + 1, :] for z in range(4)] for at in range(9)]
    low_k, high_k, link, low_r, high_r, low_d, high_d, low_w, high_w = per
    outer = [2.0 / (high_d[z] + low_d[z + 1]) for z in range(3)]
    for z in range(3):
        high_r[z] = high_r[z] - HALF_DIV * low_w[z + 1]
        low_r[z + 1] = low_r[z + 1] + HALF_DIV * high_w[z]
    ground, source, edges = [], [], []
    for z in range(4):
        ground += [low_k[z], high_k[z]]
        source += [low_r[z], high_r[z]]
        edges += [link[z]] + ([outer[z]] if z < 3 else [])
    k_a, k_b, f_ab, *factors = condense(ground, edges)
    r_a, r_b, outer_offsets = condense_source(source, *factors)
    scale = 1.0 / (k_a * k_b + f_ab * (k_a + k_b))
    p_a = ((k_b + f_ab) * r_a + f_ab * r_b) * scale
    p_b = ((k_a + f_ab) * r_b + f_ab * r_a) * scale
    nodes = expand(p_a, p_b, *factors[:2], outer_offsets)
    zero_row = jnp.zeros((1, LANES), F32)
    flux = [outer[z] * (nodes[2 * z + 2] - nodes[2 * z + 1]) for z in range(3)]
    for z in range(4):
        ends_ref[half, z : z + 1, :] = nodes[2 * z]
        ends_ref[half, 4 + z : 5 + z, :] = nodes[2 * z + 1]
        ends_ref[half, 8 + z : 9 + z, :] = flux[z - 1] if z > 0 else zero_row
        ends_ref[half, 12 + z : 13 + z, :] = flux[z] if z < 3 else zero_row

    nodes = expand(ends_ref[half, 0:4, :], ends_ref[half, 4:8, :], to_low, to_high, offsets)
    inner = [join[x] * (nodes[2 * x + 2] - nodes[2 * x + 1]) for x in range(3)]
    below = [ends_ref[half, 8:12, :]] + inner
    above = inner + [ends_ref[half, 12:16, :]]

    def put(ref, rows, at, x, what):
        ref[pl.ds(x * rows + at, 4, stride=4 * rows), :] = what

    for x in range(4):
        for at, what in enumerate([nodes[2 * x], nodes[2 * x + 1], below[x], above[x]]):
            put(all_ref, BACK_ROWS, half * 4 + at, x, what)
        for end in range(2):
            for at, part in enumerate(split_three(nodes[2 * x + end])):
                put(parts_ref, 16, half * 8 + 3 * end + at, x, part.astype(F32))
            put(parts_ref, 16, half * 8 + 6 + end, x, jnp.zeros((4, LANES), F32))


def owner_kernel(
    recv_ref, back_ref, group_ref, ends_ref, all_ref, parts_ref, place_ref, picked_ref
):
    for half in range(2):
        solve_columns(half, recv_ref, group_ref, ends_ref, all_ref, parts_ref)

    column_device = lax.axis_index("col")
    mine = lax.rem(column_device, OWNERS) * NY

    def panel(row):
        return recv_ref[pl.ds(row, COLS, stride=SEND_ROWS), :]

    inside, upper = [], []
    for half in range(2):
        place = panel(COLUMN_ROW + half).astype(jnp.int32) - mine
        inside.append((place >= 0) & (place < NY))
        upper.append(place >= LANES)
        place_ref[half * COLS : (half + 1) * COLS, :] = (place & (LANES - 1)).astype(F32)
    want = row_iota((LANES, LANES)).astype(F32).astype(jnp.bfloat16)
    for block in range(COLS):
        ends = parts_ref[block * 16 : (block + 1) * 16, :].astype(jnp.bfloat16)
        onehots = []
        for half in range(2):
            at = half * COLS + block
            place = place_ref[at : at + 1, :].astype(jnp.bfloat16)
            onehots.append(jnp.where(want == place, jnp.bfloat16(1.0), jnp.bfloat16(0.0)))
        got = jnp.dot(ends, jnp.concatenate(onehots, 1), preferred_element_type=F32)
        for half in range(2):
            at = half * COLS + block
            picked_ref[at * 16 : (at + 1) * 16, :] = got[:, half * LANES : (half + 1) * LANES]
    meta = panel(META_ROW)
    starts = [meta[:, j : j + 1] for j in range(8)] + [float(PANELS_DEV)]
    sums = [[None] * 8 for _ in range(3)]
    for half in range(2):

        def got(at):
            return picked_ref[pl.ds(half * COLS * 16 + at, COLS, stride=16), :]

        low = [got(8 * h) + got(8 * h + 1) + got(8 * h + 2) for h in range(2)]
        high = [got(8 * h + 3) + got(8 * h + 4) + got(8 * h + 5) for h in range(2)]
        low = jnp.where(upper[half], low[1], low[0])
        high = jnp.where(upper[half], high[1], high[0])
        at_panel = panel(FIRST_ROW + half) * low + panel(LAST_ROW + half) * high
        at_panel = jnp.where(inside[half], at_panel, 0.0)
        place = (lane_iota((COLS, LANES)) + half * LANES).astype(F32)
        reached = [place >= start for start in starts]
        terms = [panel(GEOM_ROW + 2 * k + half) * at_panel for k in range(3)]
        for j in range(8):
            in_section = reached[j] & jnp.logical_not(reached[j + 1])
            for k in range(3):
                part = jnp.where(in_section, terms[k], 0.0)
                part = part[0:8, :] + part[8:16, :]
                sums[k][j] = part if half == 0 else sums[k][j] + part
    terms = [
        jnp.concatenate([jnp.sum(x, axis=0, keepdims=True) for x in sums[k]], 0)
        for k in range(3)
    ]
    constant = jnp.sum(meta, axis=0, keepdims=True)
    lanes = lane_iota((1, LANES))
    own = lax.rem(column_device, OWNERS) == 0
    rows = section_rows(terms)
    for k in range(3):
        moved = pltpu.roll(constant, LANES - 8 * (k + 1), 1)
        rows[k] = rows[k] + jnp.where((lanes < 8) & own, moved, 0.0)
    for block in range(COLS):
        at = block * BACK_ROWS + 8
        for k in range(3):
            all_ref[at + k : at + k + 1, :] = rows[k]
        all_ref[at + 3 : at + 8, :] = jnp.zeros((5, LANES), F32)
    mine = pl.multiple_of((column_device // OWNERS) * (OWNERS * BACK_ROWS), OWNERS * BACK_ROWS)
    back_ref[...] = all_ref[pl.ds(mine, OWNERS * BACK_ROWS), :]


def load_kernel(back_ref, load_ref):
    load_ref[...] = jnp.zeros_like(load_ref)
    for k in range(3):
        rows = back_ref[pl.ds(8 + k, OWNERS, stride=BACK_ROWS), :]
        load_ref[k : k + 1, :] = jnp.sum(rows, axis=0, keepdims=True)


def field_kernel(back_ref, mat_ref, offset_ref, w_ref, pressure_ref, velocity_ref):
    def end(at):
        halves = [back_ref[pl.ds(half * 4 + at, CX, stride=BACK_ROWS), :] for half in range(2)]
        return jnp.concatenate(halves, axis=1)

    to_low = [level(mat_ref, A_AT + j) for j in range(CZ - 2)]
    to_high = [level(mat_ref, B_AT + j) for j in range(CZ - 2)]
    offsets = [level(offset_ref, j) for j in range(CZ - 2)]
    pressure = expand(end(0), end(1), to_low, to_high, offsets)
    flux = [end(2)]
    for z in range(CZ - 1):
        flux.append(level(mat_ref, FACE_AT + z) * (pressure[z + 1] - pressure[z]))
    flux.append(end(3))
    for z in range(CZ):
        pressure_ref[z * CX : (z + 1) * CX, :] = pressure[z]
        velocity_ref[z * CX : (z + 1) * CX, :] = level(w_ref, z) - 0.5 * (flux[z + 1] + flux[z])


def section_kernel(load_ref, pair_ref, other_ref, out_ref):
    even = lax.rem(lax.axis_index("slab"), 2) == 0
    received, beyond = pair_ref[...], other_ref[...]
    from_left = jnp.where(even, beyond, received)
    from_right = jnp.where(even, received, beyond)
    lanes = lane_iota((8, LANES))
    total = load_ref[...]
    total = total + jnp.where(lanes < 4, pltpu.roll(from_left, LANES - 4, 1), 0.0)
    total = total + jnp.where(lanes >= 4, pltpu.roll(from_right, 4, 1), 0.0)
    total = pltpu.roll(total, LANES - REACH, 1)
    out_ref[...] = total[0:3, 0:SEC_DEV]


def call(kernel, outs, scratch=(), flops=20000):
    shapes = [jax.ShapeDtypeStruct(shape, F32) for shape in outs]
    return pl.pallas_call(
        kernel,
        out_shape=shapes if len(shapes) > 1 else shapes[0],
        scratch_shapes=[pltpu.VMEM(shape, F32) for shape in scratch],
        compiler_params=pltpu.CompilerParams(vmem_limit_bytes=16 * 1024 * 1024),
        cost_estimate=pl.CostEstimate(flops=flops, bytes_accessed=500000, transcendentals=0),
    )


def per_device(p_star, u_star, v_star, w_star, flags, panel_cell, panel_section, panel_geom):
    flat = (CZ * CX, NY)
    p, u, v, w = (x.reshape(flat) for x in (p_star, u_star, v_star, w_star))
    flags = flags.reshape(flat)
    cell = panel_cell.reshape(1, PANELS_DEV)
    section = panel_section.reshape(1, PANELS_DEV)
    slabs = lax.axis_size("slab")
    pairs = [(i, i ^ 1) for i in range(slabs)]
    others = [(i, i + 1) for i in range(1, slabs - 1, 2)]
    others += [(j, i) for i, j in others]

    inputs = [p, u, v, w, flags, cell, section, panel_geom]
    *inputs, to_other, to_pair = pl.pallas_call(
        fetch_kernel,
        out_shape=[jax.ShapeDtypeStruct(x.shape, x.dtype) for x in inputs]
        + [jax.ShapeDtypeStruct((CZ, NY), F32)] * 2,
        in_specs=[pl.BlockSpec(memory_space=pltpu.HBM)] * 8,
        scratch_shapes=[pltpu.SemaphoreType.DMA((8,))],
        compiler_params=pltpu.CompilerParams(vmem_limit_bytes=16 * 1024 * 1024),
        cost_estimate=pl.CostEstimate(flops=20000, bytes_accessed=500000, transcendentals=0),
    )(*[pltpu.with_memory_space_constraint(x, pltpu.HBM) for x in inputs])
    p, u, v, w, flags, cell, section, panel_geom = inputs
    from_other = lax.ppermute(to_other, "slab", others)
    from_pair = lax.ppermute(to_pair, "slab", pairs)
    mat, source, panel, bounds, ordered = call(
        matrix_kernel,
        [(MAT_LEVELS * CX, NY), flat, (16, LANES), (16, LANES), (8, PANELS_DEV)],
        flops=5000000,
    )(p, u, v, w, flags, cell, section, panel_geom)
    send, offsets = call(pack_kernel, [(COLS * SEND_ROWS, LANES), ((CZ - 2) * CX, NY)])(
        mat, source, from_other, from_pair, w, panel, bounds, ordered
    )
    recv = lax.all_to_all(send, "col", 0, 0, tiled=True)
    back = call(
        owner_kernel,
        [(OWNERS * BACK_ROWS, LANES)],
        [
            (2, 40, LANES),
            (2, 16, LANES),
            (COLS * BACK_ROWS, LANES),
            (COLS * 16, LANES),
            (2 * COLS, LANES),
            (2 * COLS * 16, LANES),
        ],
    )(recv)
    sets = [list(range(at, at + OWNERS)) for at in range(0, COLS, OWNERS)]
    back = lax.all_to_all(back, "col", 0, 0, axis_index_groups=sets, tiled=True)
    loads = call(load_kernel, [(8, LANES)])(back)
    loads_other = lax.ppermute(loads, "slab", others)
    loads_pair = lax.ppermute(loads, "slab", pairs)
    pressure, velocity = call(field_kernel, [flat, flat], flops=5000000)(back, mat, offsets, w)
    section_loads = call(section_kernel, [(3, SEC_DEV)])(loads, loads_pair, loads_other)
    return pressure.reshape(p_star.shape), velocity.reshape(p_star.shape), section_loads


def solution(mesh):
    in_specs = (
        P("col", "slab", None),
        P("col", "slab", None),
        P("col", "slab", None),
        P("col", "slab", None),
        P("col", "slab", None),
        P(("col", "slab")),
        P(("col", "slab")),
        P(None, ("col", "slab")),
    )
    out_specs = (P("col", "slab", None), P("col", "slab", None), P(None, "slab"))
    return jax.shard_map(
        per_device, mesh=mesh, in_specs=in_specs, out_specs=out_specs, check_vma=False
    )
```

```python
import functools

import jax
import jax.numpy as jnp
from jax import lax
from jax.experimental import pallas as pl
from jax.experimental.pallas import tpu as pltpu
from jax.sharding import PartitionSpec as P

SEC_DEV = 4
EOS_ITERS = 3
KAPPA_SCALE = 0.01
AIR_DENSITY = 0.1
GAMMA_HORIZ = 0.001
DIVERGENCE_SCALE = 0.005
HALF_DIV = 0.5 * DIVERGENCE_SCALE

CZ = 8
CX = 8
NY = 256
LANES = 128
COLS = 16
PANELS_DEV = 256
REACH = 2
OWNERS = 8
SEND_ROWS = 32
BACK_ROWS = 16
GEOM_ROW, FIRST_ROW, LAST_ROW, COLUMN_ROW, META_ROW = 18, 24, 26, 28, 30

F32 = jnp.float32


def row_iota(shape):
    return lax.broadcasted_iota(jnp.int32, shape, 0)


def lane_iota(shape):
    return lax.broadcasted_iota(jnp.int32, shape, 1)


def level(ref, z):
    return ref[z * CX : (z + 1) * CX, :]


def split_three(x):
    high = x.astype(jnp.bfloat16)
    rest = x - high.astype(F32)
    middle = rest.astype(jnp.bfloat16)
    low = (rest - middle.astype(F32)).astype(jnp.bfloat16)
    return high, middle, low


def exact_dot(x, onehot):
    rows = x.shape[0]
    parts = jnp.concatenate(split_three(x), 0)
    got = jnp.dot(parts, onehot, preferred_element_type=F32)
    return got[:rows] + got[rows : 2 * rows] + got[2 * rows :]


def pick(fields, onehot, row_mask):
    total = exact_dot(fields, onehot)
    return jnp.sum(jnp.where(row_mask, total, 0.0), axis=0, keepdims=True)


def panel_masks(cell):
    onehot = (row_iota((NY, PANELS_DEV)) == (cell & (NY - 1))).astype(F32)
    row_mask = row_iota((CZ * CX, PANELS_DEV)) == (cell >> 8)
    return onehot.astype(jnp.bfloat16), row_mask


def halving(count):
    nodes, order = list(range(count)), []
    while len(nodes) > 2:
        gone = range(1, len(nodes) - 1, 2)
        order += [(nodes[i], nodes[i - 1], nodes[i + 1]) for i in gone]
        nodes = [node for i, node in enumerate(nodes) if i not in gone]
    return order


def condense(ground, edges):
    count = len(ground)
    ground = list(ground)
    edges = {(i, i + 1): edge for i, edge in enumerate(edges)}
    to_low, to_high, inverse = ([None] * (count - 2) for _ in range(3))
    for node, low, high in halving(count):
        inv = 1.0 / (ground[node] + edges[low, node] + edges[node, high])
        a, b = edges[low, node] * inv, edges[node, high] * inv
        to_low[node - 1], to_high[node - 1], inverse[node - 1] = a, b, inv
        ground[low] = ground[low] + a * ground[node]
        ground[high] = ground[high] + b * ground[node]
        edges[low, high] = edges[low, node] * b
    return ground[0], ground[-1], edges[0, count - 1], to_low, to_high, inverse


def condense_source(source, to_low, to_high, inverse):
    source = list(source)
    for node, low, high in halving(len(source)):
        source[low] = source[low] + to_low[node - 1] * source[node]
        source[high] = source[high] + to_high[node - 1] * source[node]
    offsets = [x * inv for x, inv in zip(source[1:-1], inverse)]
    return source[0], source[-1], offsets


def expand(first, last, to_low, to_high, offsets):
    values = [first] + [None] * len(offsets) + [last]
    for node, low, high in reversed(halving(len(values))):
        inflow = to_low[node - 1] * values[low] + to_high[node - 1] * values[high]
        values[node] = inflow if offsets[node - 1] is None else offsets[node - 1] + inflow
    return values


def to_row(column):
    on_diagonal = row_iota((8, LANES)) == lane_iota((8, LANES))
    return jnp.sum(jnp.where(on_diagonal, column, 0.0), axis=0, keepdims=True)


def section_rows(terms):
    return [to_row(jnp.sum(term, axis=1, keepdims=True)) for term in terms]


def sort_panels(section, rows):
    square = (PANELS_DEV, PANELS_DEV)
    key = section * PANELS_DEV + lane_iota((1, PANELS_DEV))
    key = key.astype(F32)
    on_diagonal = row_iota(square) == lane_iota(square)
    key_column = jnp.sum(jnp.where(on_diagonal, key, 0.0), axis=1, keepdims=True)
    rank = jnp.sum(jnp.where(key < key_column, 1.0, 0.0), axis=1, keepdims=True)
    order = jnp.where(lane_iota(square).astype(F32) == rank, 1.0, 0.0).astype(jnp.bfloat16)
    return exact_dot(rows, order)


def fetch_kernel(*refs):
    sources, targets, other_ref, pair_ref, sems = refs[:8], refs[8:16], *refs[16:]
    fetches = [
        pltpu.make_async_copy(source, target, sems.at[i])
        for i, (source, target) in enumerate(zip(sources, targets))
    ]
    for fetch in fetches:
        fetch.start()
    p_ref, u_ref = targets[:2]
    even = lax.rem(lax.axis_index("slab"), 2) == 0
    for fetch in fetches:
        fetch.wait()
    for z in range(CZ):
        first, last = z * CX, (z + 1) * CX - 1
        leading = GAMMA_HORIZ * p_ref[first : first + 1, :] - HALF_DIV * u_ref[first : first + 1, :]
        trailing = GAMMA_HORIZ * p_ref[last : last + 1, :] + HALF_DIV * u_ref[last : last + 1, :]
        other_ref[z : z + 1, :] = jnp.where(even, leading, trailing)
        pair_ref[z : z + 1, :] = jnp.where(even, trailing, leading)


A_AT, B_AT, I_AT, FACE_AT, PORT_AT = 0, 6, 12, 18, 25
MAT_LEVELS = 30


def matrix_kernel(
    p_ref, u_ref, v_ref, w_ref, flags_ref, cell_ref, sec_ref, geom_ref,
    mat_ref, src_ref, panel_ref, bound_ref, sorted_ref,
):
    shape = (CX, NY)
    rows, lanes = row_iota(shape), lane_iota(shape)
    densities, kappas = [], []
    for z in range(CZ):
        p, flags = level(p_ref, z), level(flags_ref, z)
        air = jnp.where(flags == 1, 1.0, jnp.where(flags == 2, 0.5, 0.0)).astype(F32)
        water = jnp.ones_like(p)
        for _ in range(EOS_ITERS):
            square = water * water
            cube = square * water
            sixth = cube * cube
            water = water - (sixth * water - 1.0 - p) / (7.0 * sixth)
        shifted = 1.0 + p
        air_density = AIR_DENSITY * jnp.exp(jnp.log(shifted) * (1.0 / 1.4))
        densities.append(air * air_density + (1.0 - air) * water)
        kappa = KAPPA_SCALE * (air / (1.4 * shifted) + (1.0 - air) / (7.0 * shifted))
        kappas.append(kappa)

        u, v = level(u_ref, z), level(v_ref, z)

        def beside(x, axis, step):
            size = shape[axis]
            moved = pltpu.roll(x, (-step) % size, axis)
            at = rows if axis == 0 else lanes
            return jnp.where(at == (size - 1 if step > 0 else 0), 0.0, moved)

        laplacian = (
            beside(p, 0, 1) + beside(p, 0, -1) + beside(p, 1, 1) + beside(p, 1, -1) - 4.0 * p
        )
        divergence = 0.5 * (beside(u, 0, 1) - beside(u, 0, -1)) + 0.5 * (
            beside(v, 1, 1) - beside(v, 1, -1)
        )
        if z == 0:
            w_difference = level(w_ref, 1)
        elif z == CZ - 1:
            w_difference = -level(w_ref, CZ - 2)
        else:
            w_difference = level(w_ref, z + 1) - level(w_ref, z - 1)
        divergence = divergence + 0.5 * w_difference
        src_ref[z * CX : (z + 1) * CX, :] = (
            kappa * p + GAMMA_HORIZ * laplacian - DIVERGENCE_SCALE * divergence
        )
    faces = [2.0 / (densities[z] + densities[z + 1]) for z in range(CZ - 1)]
    first, last, link, to_low, to_high, inverse = condense(kappas, faces)
    stored = to_low + to_high + inverse + faces + [first, last, link, densities[0], densities[-1]]
    for at, value in enumerate(stored):
        mat_ref[at * CX : (at + 1) * CX, :] = value

    zero, one = jnp.zeros(shape, F32), jnp.ones(shape, F32)
    no_offset = [None] * (CZ - 2)
    section = sec_ref[...] - (lax.axis_index("slab") * SEC_DEV - REACH)
    rows = [geom_ref[k : k + 1, :] for k in range(3)] + [cell_ref[...].astype(F32)]
    rows = sort_panels(section, jnp.concatenate(rows + [jnp.zeros((4, PANELS_DEV), F32)], 0))
    sorted_ref[...] = rows
    at_section = row_iota((8, PANELS_DEV))
    starts = jnp.sum(jnp.where(section < at_section, 1.0, 0.0), axis=1, keepdims=True)
    stops = jnp.sum(jnp.where(section <= at_section, 1.0, 0.0), axis=1, keepdims=True)
    bound_ref[0:8, :] = jnp.broadcast_to(starts, (8, LANES))
    bound_ref[8:16, :] = jnp.broadcast_to(stops, (8, LANES))

    cell = rows[3:4, :].astype(jnp.int32)
    onehot, row_mask = panel_masks(cell)
    from_first = expand(one, zero, to_low, to_high, no_offset)
    from_last = expand(zero, one, to_low, to_high, no_offset)
    panel_rows = [rows[k : k + 1, :] for k in range(3)]
    panel_rows.append(pick(jnp.concatenate(from_first, 0), onehot, row_mask))
    panel_rows.append(pick(jnp.concatenate(from_last, 0), onehot, row_mask))
    panel_rows.append((cell & (CX * NY - 1)).astype(F32))
    panel_ref[...] = jnp.zeros_like(panel_ref)
    for at, row in enumerate(panel_rows):
        for half in range(2):
            panel_ref[2 + 2 * at + half : 3 + 2 * at + half, :] = row[
                :, half * LANES : (half + 1) * LANES
            ]
    panel_ref[META_ROW - 16 : META_ROW - 15, :] = to_row(starts)


def pack_kernel(
    mat_ref, src_ref, other_ref, pair_ref, w_ref, panel_ref, bound_ref, sorted_ref,
    send_ref, offset_ref,
):
    core = lax.rem(lax.axis_index("slab"), 2)
    even = core == 0
    shape = (CX, NY)
    rows = row_iota(shape)
    received, beyond = pair_ref[1 - core], other_ref[...]
    from_left = jnp.where(even, beyond, received)
    from_right = jnp.where(even, received, beyond)
    source = []
    for z in range(CZ):
        halo = jnp.where(rows == 0, from_left[z : z + 1, :], 0.0) + jnp.where(
            rows == CX - 1, from_right[z : z + 1, :], 0.0
        )
        source.append(level(src_ref, z) + halo)
    to_low = [level(mat_ref, A_AT + j) for j in range(CZ - 2)]
    to_high = [level(mat_ref, B_AT + j) for j in range(CZ - 2)]
    inverse = [level(mat_ref, I_AT + j) for j in range(CZ - 2)]
    first, last, offsets = condense_source(source, to_low, to_high, inverse)
    for j, offset in enumerate(offsets):
        offset_ref[j * CX : (j + 1) * CX, :] = offset

    zero = jnp.zeros(shape, F32)
    constant = expand(zero, zero, to_low, to_high, offsets)
    onehot, row_mask = panel_masks(sorted_ref[3:4, :].astype(jnp.int32))
    at_panel = pick(jnp.concatenate(constant, 0), onehot, row_mask)
    terms = [0.0, 0.0, 0.0]
    for half in range(2):
        lanes = slice(half * LANES, (half + 1) * LANES)
        place = (lane_iota((8, LANES)) + half * LANES).astype(F32)
        in_section = (place >= bound_ref[0:8, :]) & (place < bound_ref[8:16, :])
        for k in range(3):
            row = sorted_ref[k : k + 1, lanes] * at_panel[:, lanes]
            terms[k] = terms[k] + jnp.where(in_section, row, 0.0)
    meta = panel_ref[META_ROW - 16 : META_ROW - 15, :]
    for k, row in enumerate(section_rows(terms)):
        meta = meta + pltpu.roll(row, 8 * (k + 1), 1)

    for device in range(COLS):
        send_ref[device * SEND_ROWS + 16 : (device + 1) * SEND_ROWS, :] = panel_ref[...]
    for device in range(COLS):
        at = device * SEND_ROWS + META_ROW
        send_ref[at : at + 1, :] = meta
    ports = [level(mat_ref, PORT_AT + j) for j in range(3)] + [first, last]
    ports += [level(mat_ref, PORT_AT + 3), level(mat_ref, PORT_AT + 4)]
    ports += [level(w_ref, 0), level(w_ref, CZ - 1)]
    for at, value in enumerate(ports):
        for half in range(2):
            row = half * 8 + at if at < 8 else 16 + half
            for group in range(0, COLS, OWNERS):
                send_ref[pl.ds(group * SEND_ROWS + row, OWNERS, stride=SEND_ROWS), :] = value[
                    :, half * LANES : (half + 1) * LANES
                ]


def solve_columns(half, recv_ref, group_ref, ends_ref, all_ref, parts_ref):
    def value(at, x):
        row = half * 8 + at if at < 8 else 16 + half
        return recv_ref[pl.ds(x * SEND_ROWS + row, 4, stride=4 * SEND_ROWS), :]

    per = [[value(at, x) for x in range(4)] for at in range(9)]
    low_k, high_k, link, low_r, high_r, low_d, high_d, low_w, high_w = per
    join = [2.0 / (high_d[x] + low_d[x + 1]) for x in range(3)]
    for x in range(3):
        high_r[x] = high_r[x] - HALF_DIV * low_w[x + 1]
        low_r[x + 1] = low_r[x + 1] + HALF_DIV * high_w[x]
    ground, source, edges = [], [], []
    for x in range(4):
        ground += [low_k[x], high_k[x]]
        source += [low_r[x], high_r[x]]
        edges += [link[x]] + ([join[x]] if x < 3 else [])
    first, last, across, to_low, to_high, inverse = condense(ground, edges)
    first_r, last_r, offsets = condense_source(source, to_low, to_high, inverse)

    stored = [first, last, across, first_r, last_r, low_d[0], high_d[3], low_w[0], high_w[3]]
    for at, x in enumerate(stored):
        group_ref[half, at * 4 : (at + 1) * 4, :] = x
    per = [[group_ref[half, at * 4 + z : at * 4 + z + 1, :] for z in range(4)] for at in range(9)]
    low_k, high_k, link, low_r, high_r, low_d, high_d, low_w, high_w = per
    outer = [2.0 / (high_d[z] + low_d[z + 1]) for z in range(3)]
    for z in range(3):
        high_r[z] = high_r[z] - HALF_DIV * low_w[z + 1]
        low_r[z + 1] = low_r[z + 1] + HALF_DIV * high_w[z]
    ground, source, edges = [], [], []
    for z in range(4):
        ground += [low_k[z], high_k[z]]
        source += [low_r[z], high_r[z]]
        edges += [link[z]] + ([outer[z]] if z < 3 else [])
    k_a, k_b, f_ab, *factors = condense(ground, edges)
    r_a, r_b, outer_offsets = condense_source(source, *factors)
    scale = 1.0 / (k_a * k_b + f_ab * (k_a + k_b))
    p_a = ((k_b + f_ab) * r_a + f_ab * r_b) * scale
    p_b = ((k_a + f_ab) * r_b + f_ab * r_a) * scale
    nodes = expand(p_a, p_b, *factors[:2], outer_offsets)
    zero_row = jnp.zeros((1, LANES), F32)
    flux = [outer[z] * (nodes[2 * z + 2] - nodes[2 * z + 1]) for z in range(3)]
    for z in range(4):
        ends_ref[half, z : z + 1, :] = nodes[2 * z]
        ends_ref[half, 4 + z : 5 + z, :] = nodes[2 * z + 1]
        ends_ref[half, 8 + z : 9 + z, :] = flux[z - 1] if z > 0 else zero_row
        ends_ref[half, 12 + z : 13 + z, :] = flux[z] if z < 3 else zero_row

    nodes = expand(ends_ref[half, 0:4, :], ends_ref[half, 4:8, :], to_low, to_high, offsets)
    inner = [join[x] * (nodes[2 * x + 2] - nodes[2 * x + 1]) for x in range(3)]
    below = [ends_ref[half, 8:12, :]] + inner
    above = inner + [ends_ref[half, 12:16, :]]

    def put(ref, rows, at, x, what):
        ref[pl.ds(x * rows + at, 4, stride=4 * rows), :] = what

    for x in range(4):
        for at, what in enumerate([nodes[2 * x], nodes[2 * x + 1], below[x], above[x]]):
            put(all_ref, BACK_ROWS, half * 4 + at, x, what)
        for end in range(2):
            for at, part in enumerate(split_three(nodes[2 * x + end])):
                put(parts_ref, 16, half * 8 + 3 * end + at, x, part.astype(F32))
            put(parts_ref, 16, half * 8 + 6 + end, x, jnp.zeros((4, LANES), F32))


def owner_kernel(
    recv_ref, back_ref, group_ref, ends_ref, all_ref, parts_ref, place_ref, picked_ref
):
    for half in range(2):
        solve_columns(half, recv_ref, group_ref, ends_ref, all_ref, parts_ref)

    column_device = lax.axis_index("col")
    mine = lax.rem(column_device, OWNERS) * NY

    def panel(row):
        return recv_ref[pl.ds(row, COLS, stride=SEND_ROWS), :]

    inside, upper = [], []
    for half in range(2):
        place = panel(COLUMN_ROW + half).astype(jnp.int32) - mine
        inside.append((place >= 0) & (place < NY))
        upper.append(place >= LANES)
        place_ref[half * COLS : (half + 1) * COLS, :] = (place & (LANES - 1)).astype(F32)
    want = row_iota((LANES, LANES)).astype(F32).astype(jnp.bfloat16)
    for block in range(COLS):
        ends = parts_ref[block * 16 : (block + 1) * 16, :].astype(jnp.bfloat16)
        onehots = []
        for half in range(2):
            at = half * COLS + block
            place = place_ref[at : at + 1, :].astype(jnp.bfloat16)
            onehots.append(jnp.where(want == place, jnp.bfloat16(1.0), jnp.bfloat16(0.0)))
        got = jnp.dot(ends, jnp.concatenate(onehots, 1), preferred_element_type=F32)
        for half in range(2):
            at = half * COLS + block
            picked_ref[at * 16 : (at + 1) * 16, :] = got[:, half * LANES : (half + 1) * LANES]
    meta = panel(META_ROW)
    starts = [meta[:, j : j + 1] for j in range(8)] + [float(PANELS_DEV)]
    sums = [[None] * 8 for _ in range(3)]
    for half in range(2):

        def got(at):
            return picked_ref[pl.ds(half * COLS * 16 + at, COLS, stride=16), :]

        low = [got(8 * h) + got(8 * h + 1) + got(8 * h + 2) for h in range(2)]
        high = [got(8 * h + 3) + got(8 * h + 4) + got(8 * h + 5) for h in range(2)]
        low = jnp.where(upper[half], low[1], low[0])
        high = jnp.where(upper[half], high[1], high[0])
        at_panel = panel(FIRST_ROW + half) * low + panel(LAST_ROW + half) * high
        at_panel = jnp.where(inside[half], at_panel, 0.0)
        place = (lane_iota((COLS, LANES)) + half * LANES).astype(F32)
        reached = [place >= start for start in starts]
        terms = [panel(GEOM_ROW + 2 * k + half) * at_panel for k in range(3)]
        for j in range(8):
            in_section = reached[j] & jnp.logical_not(reached[j + 1])
            for k in range(3):
                part = jnp.where(in_section, terms[k], 0.0)
                part = part[0:8, :] + part[8:16, :]
                sums[k][j] = part if half == 0 else sums[k][j] + part
    terms = [
        jnp.concatenate([jnp.sum(x, axis=0, keepdims=True) for x in sums[k]], 0)
        for k in range(3)
    ]
    constant = jnp.sum(meta, axis=0, keepdims=True)
    lanes = lane_iota((1, LANES))
    own = lax.rem(column_device, OWNERS) == 0
    rows = section_rows(terms)
    for k in range(3):
        moved = pltpu.roll(constant, LANES - 8 * (k + 1), 1)
        rows[k] = rows[k] + jnp.where((lanes < 8) & own, moved, 0.0)
    for block in range(COLS):
        at = block * BACK_ROWS + 8
        for k in range(3):
            all_ref[at + k : at + k + 1, :] = rows[k]
        all_ref[at + 3 : at + 8, :] = jnp.zeros((5, LANES), F32)
    mine = pl.multiple_of((column_device // OWNERS) * (OWNERS * BACK_ROWS), OWNERS * BACK_ROWS)
    back_ref[...] = all_ref[pl.ds(mine, OWNERS * BACK_ROWS), :]


def load_kernel(back_ref, load_ref):
    load_ref[...] = jnp.zeros_like(load_ref)
    for k in range(3):
        rows = back_ref[pl.ds(8 + k, OWNERS, stride=BACK_ROWS), :]
        load_ref[k : k + 1, :] = jnp.sum(rows, axis=0, keepdims=True)


def field_kernel(back_ref, mat_ref, offset_ref, w_ref, pressure_ref, velocity_ref):
    def end(at):
        halves = [back_ref[pl.ds(half * 4 + at, CX, stride=BACK_ROWS), :] for half in range(2)]
        return jnp.concatenate(halves, axis=1)

    to_low = [level(mat_ref, A_AT + j) for j in range(CZ - 2)]
    to_high = [level(mat_ref, B_AT + j) for j in range(CZ - 2)]
    offsets = [level(offset_ref, j) for j in range(CZ - 2)]
    pressure = expand(end(0), end(1), to_low, to_high, offsets)
    flux = [end(2)]
    for z in range(CZ - 1):
        flux.append(level(mat_ref, FACE_AT + z) * (pressure[z + 1] - pressure[z]))
    flux.append(end(3))
    for z in range(CZ):
        pressure_ref[z * CX : (z + 1) * CX, :] = pressure[z]
        velocity_ref[z * CX : (z + 1) * CX, :] = level(w_ref, z) - 0.5 * (flux[z + 1] + flux[z])


def section_kernel(load_ref, pair_ref, other_ref, out_ref):
    core = lax.rem(lax.axis_index("slab"), 2)
    even = core == 0
    received, beyond = pair_ref[1 - core], other_ref[...]
    from_left = jnp.where(even, beyond, received)
    from_right = jnp.where(even, received, beyond)
    lanes = lane_iota((8, LANES))
    total = load_ref[...]
    total = total + jnp.where(lanes < 4, pltpu.roll(from_left, LANES - 4, 1), 0.0)
    total = total + jnp.where(lanes >= 4, pltpu.roll(from_right, 4, 1), 0.0)
    total = pltpu.roll(total, LANES - REACH, 1)
    out_ref[...] = total[0:3, 0:SEC_DEV]


def call(kernel, outs, scratch=(), flops=20000):
    shapes = [jax.ShapeDtypeStruct(shape, F32) for shape in outs]
    return pl.pallas_call(
        kernel,
        out_shape=shapes if len(shapes) > 1 else shapes[0],
        scratch_shapes=[pltpu.VMEM(shape, F32) for shape in scratch],
        compiler_params=pltpu.CompilerParams(vmem_limit_bytes=16 * 1024 * 1024),
        cost_estimate=pl.CostEstimate(flops=flops, bytes_accessed=500000, transcendentals=0),
    )


def per_device(p_star, u_star, v_star, w_star, flags, panel_cell, panel_section, panel_geom):
    flat = (CZ * CX, NY)
    p, u, v, w = (x.reshape(flat) for x in (p_star, u_star, v_star, w_star))
    flags = flags.reshape(flat)
    cell = panel_cell.reshape(1, PANELS_DEV)
    section = panel_section.reshape(1, PANELS_DEV)
    slabs = lax.axis_size("slab")
    cores = [[i, i + 1] for i in range(0, slabs, 2)]
    others = [(i, i + 1) for i in range(1, slabs - 1, 2)]
    others += [(j, i) for i, j in others]

    inputs = [p, u, v, w, flags, cell, section, panel_geom]
    *inputs, to_other, to_pair = pl.pallas_call(
        fetch_kernel,
        out_shape=[jax.ShapeDtypeStruct(x.shape, x.dtype) for x in inputs]
        + [jax.ShapeDtypeStruct((CZ, NY), F32)] * 2,
        in_specs=[pl.BlockSpec(memory_space=pltpu.HBM)] * 8,
        scratch_shapes=[pltpu.SemaphoreType.DMA((8,))],
        compiler_params=pltpu.CompilerParams(vmem_limit_bytes=16 * 1024 * 1024),
        cost_estimate=pl.CostEstimate(flops=20000, bytes_accessed=500000, transcendentals=0),
    )(*[pltpu.with_memory_space_constraint(x, pltpu.HBM) for x in inputs])
    p, u, v, w, flags, cell, section, panel_geom = inputs
    from_other = lax.ppermute(to_other, "slab", others)
    from_pair = lax.all_gather(to_pair, "slab", axis_index_groups=cores)
    mat, source, panel, bounds, ordered = call(
        matrix_kernel,
        [(MAT_LEVELS * CX, NY), flat, (16, LANES), (16, LANES), (8, PANELS_DEV)],
        flops=5000000,
    )(p, u, v, w, flags, cell, section, panel_geom)
    send, offsets = call(pack_kernel, [(COLS * SEND_ROWS, LANES), ((CZ - 2) * CX, NY)])(
        mat, source, from_other, from_pair, w, panel, bounds, ordered
    )
    recv = lax.all_to_all(send, "col", 0, 0, tiled=True)
    back = call(
        owner_kernel,
        [(OWNERS * BACK_ROWS, LANES)],
        [
            (2, 40, LANES),
            (2, 16, LANES),
            (COLS * BACK_ROWS, LANES),
            (COLS * 16, LANES),
            (2 * COLS, LANES),
            (2 * COLS * 16, LANES),
        ],
    )(recv)
    sets = [list(range(at, at + OWNERS)) for at in range(0, COLS, OWNERS)]
    back = lax.all_to_all(back, "col", 0, 0, axis_index_groups=sets, tiled=True)
    loads = call(load_kernel, [(8, LANES)])(back)
    loads_other = lax.ppermute(loads, "slab", others)
    loads_pair = lax.all_gather(loads, "slab", axis_index_groups=cores)
    pressure, velocity = call(field_kernel, [flat, flat], flops=5000000)(back, mat, offsets, w)
    section_loads = call(section_kernel, [(3, SEC_DEV)])(loads, loads_pair, loads_other)
    return pressure.reshape(p_star.shape), velocity.reshape(p_star.shape), section_loads


def solution(mesh):
    in_specs = (
        P("col", "slab", None),
        P("col", "slab", None),
        P("col", "slab", None),
        P("col", "slab", None),
        P("col", "slab", None),
        P(("col", "slab")),
        P(("col", "slab")),
        P(None, ("col", "slab")),
    )
    out_specs = (P("col", "slab", None), P("col", "slab", None), P(None, "slab"))
    return jax.shard_map(
        per_device, mesh=mesh, in_specs=in_specs, out_specs=out_specs, check_vma=False
    )
```

```python
import functools

import jax
import jax.numpy as jnp
from jax import lax
from jax.experimental import pallas as pl
from jax.experimental.pallas import tpu as pltpu
from jax.sharding import PartitionSpec as P

SEC_DEV = 4
EOS_ITERS = 3
KAPPA_SCALE = 0.01
AIR_DENSITY = 0.1
GAMMA_HORIZ = 0.001
DIVERGENCE_SCALE = 0.005
HALF_DIV = 0.5 * DIVERGENCE_SCALE

CZ = 8
CX = 8
NY = 256
LANES = 128
COLS = 16
PANELS_DEV = 256
REACH = 2
OWNERS = 8
SEND_ROWS = 29
BACK_ROWS = 9
GEOM_ROW, SHARE_ROW, COLUMN_ROW, META_ROW = 18, 24, 26, 28

F32 = jnp.float32


def row_iota(shape):
    return lax.broadcasted_iota(jnp.int32, shape, 0)


def lane_iota(shape):
    return lax.broadcasted_iota(jnp.int32, shape, 1)


def level(ref, z):
    return ref[z * CX : (z + 1) * CX, :]


def split_three(x):
    high = x.astype(jnp.bfloat16)
    rest = x - high.astype(F32)
    middle = rest.astype(jnp.bfloat16)
    low = (rest - middle.astype(F32)).astype(jnp.bfloat16)
    return high, middle, low


def exact_dot(x, onehot):
    rows = x.shape[0]
    parts = jnp.concatenate(split_three(x), 0)
    got = jnp.dot(parts, onehot, preferred_element_type=F32)
    return got[:rows] + got[rows : 2 * rows] + got[2 * rows :]


def pick(fields, onehot, row_mask):
    total = exact_dot(fields, onehot)
    return jnp.sum(jnp.where(row_mask, total, 0.0), axis=0, keepdims=True)


def panel_masks(cell):
    onehot = (row_iota((NY, PANELS_DEV)) == (cell & (NY - 1))).astype(F32)
    row_mask = row_iota((CZ * CX, PANELS_DEV)) == (cell >> 8)
    return onehot.astype(jnp.bfloat16), row_mask


def halving(count):
    nodes, order = list(range(count)), []
    while len(nodes) > 2:
        gone = range(1, len(nodes) - 1, 2)
        order += [(nodes[i], nodes[i - 1], nodes[i + 1]) for i in gone]
        nodes = [node for i, node in enumerate(nodes) if i not in gone]
    return order


def condense(ground, edges):
    count = len(ground)
    ground = list(ground)
    edges = {(i, i + 1): edge for i, edge in enumerate(edges)}
    to_low, to_high, inverse = ([None] * (count - 2) for _ in range(3))
    for node, low, high in halving(count):
        inv = 1.0 / (ground[node] + edges[low, node] + edges[node, high])
        a, b = edges[low, node] * inv, edges[node, high] * inv
        to_low[node - 1], to_high[node - 1], inverse[node - 1] = a, b, inv
        ground[low] = ground[low] + a * ground[node]
        ground[high] = ground[high] + b * ground[node]
        edges[low, high] = edges[low, node] * b
    return ground[0], ground[-1], edges[0, count - 1], to_low, to_high, inverse


def condense_source(source, to_low, to_high, inverse):
    source = list(source)
    for node, low, high in halving(len(source)):
        source[low] = source[low] + to_low[node - 1] * source[node]
        source[high] = source[high] + to_high[node - 1] * source[node]
    offsets = [x * inv for x, inv in zip(source[1:-1], inverse)]
    return source[0], source[-1], offsets


def expand(first, last, to_low, to_high, offsets):
    values = [first] + [None] * len(offsets) + [last]
    for node, low, high in reversed(halving(len(values))):
        inflow = to_low[node - 1] * values[low] + to_high[node - 1] * values[high]
        values[node] = inflow if offsets[node - 1] is None else offsets[node - 1] + inflow
    return values


def to_row(column):
    on_diagonal = row_iota((8, LANES)) == lane_iota((8, LANES))
    return jnp.sum(jnp.where(on_diagonal, column, 0.0), axis=0, keepdims=True)


def section_rows(terms):
    return [to_row(jnp.sum(term, axis=1, keepdims=True)) for term in terms]


def sort_panels(section, rows):
    square = (PANELS_DEV, PANELS_DEV)
    key = section * PANELS_DEV + lane_iota((1, PANELS_DEV))
    key = key.astype(F32)
    on_diagonal = row_iota(square) == lane_iota(square)
    key_column = jnp.sum(jnp.where(on_diagonal, key, 0.0), axis=1, keepdims=True)
    rank = jnp.sum(jnp.where(key < key_column, 1.0, 0.0), axis=1, keepdims=True)
    order = jnp.where(lane_iota(square).astype(F32) == rank, 1.0, 0.0).astype(jnp.bfloat16)
    return exact_dot(rows, order)


def fetch_kernel(*refs):
    sources, targets = refs[:8], refs[8:13] + refs[17:20]
    other_ref, pair_ref, bound_ref, sorted_ref = refs[13:17]
    p_ref, u_ref = targets[:2]
    cell_ref, sec_ref, geom_ref = targets[5:]
    fetches = [
        pltpu.make_async_copy(source, target, refs[20].at[i])
        for i, (source, target) in enumerate(zip(sources, targets))
    ]
    for fetch in fetches[5:] + fetches[:5]:
        fetch.start()
    slab = lax.axis_index("slab")
    even = lax.rem(slab, 2) == 0
    for fetch in fetches[5:]:
        fetch.wait()
    section = sec_ref[...] - (slab * SEC_DEV - REACH)
    rows = [geom_ref[k : k + 1, :] for k in range(3)] + [cell_ref[...].astype(F32)]
    rows = jnp.concatenate(rows + [jnp.zeros((4, PANELS_DEV), F32)], 0)
    sorted_ref[...] = sort_panels(section, rows)
    at_section = row_iota((8, PANELS_DEV))
    for at, before in enumerate((section < at_section, section <= at_section)):
        count = jnp.sum(jnp.where(before, 1.0, 0.0), axis=1, keepdims=True)
        bound_ref[at * 8 : (at + 1) * 8, :] = jnp.broadcast_to(count, (8, LANES))
    for fetch in fetches[:5]:
        fetch.wait()
    for z in range(CZ):
        first, last = z * CX, (z + 1) * CX - 1
        leading = GAMMA_HORIZ * p_ref[first : first + 1, :] - HALF_DIV * u_ref[first : first + 1, :]
        trailing = GAMMA_HORIZ * p_ref[last : last + 1, :] + HALF_DIV * u_ref[last : last + 1, :]
        other_ref[z : z + 1, :] = jnp.where(even, leading, trailing)
        pair_ref[z : z + 1, :] = jnp.where(even, trailing, leading)


A_AT, B_AT, I_AT, FACE_AT, PORT_AT = 0, 6, 12, 18, 25
MAT_LEVELS = 30


def matrix_kernel(
    p_ref, u_ref, v_ref, w_ref, flags_ref, bound_ref, sorted_ref, mat_ref, src_ref, panel_ref
):
    shape = (CX, NY)
    rows, lanes = row_iota(shape), lane_iota(shape)
    densities, kappas = [], []
    for z in range(CZ):
        p, flags = level(p_ref, z), level(flags_ref, z)
        air = jnp.where(flags == 1, 1.0, jnp.where(flags == 2, 0.5, 0.0)).astype(F32)
        water = jnp.ones_like(p)
        for _ in range(EOS_ITERS):
            square = water * water
            cube = square * water
            sixth = cube * cube
            water = water - (sixth * water - 1.0 - p) / (7.0 * sixth)
        shifted = 1.0 + p
        air_density = AIR_DENSITY * jnp.exp(jnp.log(shifted) * (1.0 / 1.4))
        densities.append(air * air_density + (1.0 - air) * water)
        kappa = KAPPA_SCALE * (air / (1.4 * shifted) + (1.0 - air) / (7.0 * shifted))
        kappas.append(kappa)

        u, v = level(u_ref, z), level(v_ref, z)

        def beside(x, axis, step):
            size = shape[axis]
            moved = pltpu.roll(x, (-step) % size, axis)
            at = rows if axis == 0 else lanes
            return jnp.where(at == (size - 1 if step > 0 else 0), 0.0, moved)

        laplacian = (
            beside(p, 0, 1) + beside(p, 0, -1) + beside(p, 1, 1) + beside(p, 1, -1) - 4.0 * p
        )
        divergence = 0.5 * (beside(u, 0, 1) - beside(u, 0, -1)) + 0.5 * (
            beside(v, 1, 1) - beside(v, 1, -1)
        )
        if z == 0:
            w_difference = level(w_ref, 1)
        elif z == CZ - 1:
            w_difference = -level(w_ref, CZ - 2)
        else:
            w_difference = level(w_ref, z + 1) - level(w_ref, z - 1)
        divergence = divergence + 0.5 * w_difference
        src_ref[z * CX : (z + 1) * CX, :] = (
            kappa * p + GAMMA_HORIZ * laplacian - DIVERGENCE_SCALE * divergence
        )
    faces = [2.0 / (densities[z] + densities[z + 1]) for z in range(CZ - 1)]
    first, last, link, to_low, to_high, inverse = condense(kappas, faces)
    stored = to_low + to_high + inverse + faces + [first, last, link, densities[0], densities[-1]]
    for at, value in enumerate(stored):
        mat_ref[at * CX : (at + 1) * CX, :] = value

    zero, one = jnp.zeros(shape, F32), jnp.ones(shape, F32)
    no_offset = [None] * (CZ - 2)
    rows = sorted_ref[...]
    cell = rows[3:4, :].astype(jnp.int32)
    onehot, row_mask = panel_masks(cell)
    from_first = expand(one, zero, to_low, to_high, no_offset)
    from_last = expand(zero, one, to_low, to_high, no_offset)
    at_first = pick(jnp.concatenate(from_first, 0), onehot, row_mask)
    at_last = pick(jnp.concatenate(from_last, 0), onehot, row_mask)
    panel_rows = [rows[k : k + 1, :] * (at_first + at_last) for k in range(3)]
    panel_rows.append(at_first / (at_first + at_last))
    panel_rows.append((cell & (CX * NY - 1)).astype(F32))
    panel_ref[...] = jnp.zeros_like(panel_ref)
    for at, row in enumerate(panel_rows):
        for half in range(2):
            panel_ref[2 * at + half : 2 * at + half + 1, :] = row[
                :, half * LANES : (half + 1) * LANES
            ]
    panel_ref[META_ROW - GEOM_ROW : META_ROW - GEOM_ROW + 1, :] = to_row(bound_ref[0:8, 0:1])


def pack_kernel(
    mat_ref, src_ref, other_ref, pair_ref, w_ref, panel_ref, bound_ref, sorted_ref,
    send_ref, offset_ref,
):
    core = lax.rem(lax.axis_index("slab"), 2)
    even = core == 0
    shape = (CX, NY)
    rows = row_iota(shape)
    received, beyond = pair_ref[1 - core], other_ref[...]
    from_left = jnp.where(even, beyond, received)
    from_right = jnp.where(even, received, beyond)
    source = []
    for z in range(CZ):
        halo = jnp.where(rows == 0, from_left[z : z + 1, :], 0.0) + jnp.where(
            rows == CX - 1, from_right[z : z + 1, :], 0.0
        )
        source.append(level(src_ref, z) + halo)
    to_low = [level(mat_ref, A_AT + j) for j in range(CZ - 2)]
    to_high = [level(mat_ref, B_AT + j) for j in range(CZ - 2)]
    inverse = [level(mat_ref, I_AT + j) for j in range(CZ - 2)]
    first, last, offsets = condense_source(source, to_low, to_high, inverse)
    for j, offset in enumerate(offsets):
        offset_ref[j * CX : (j + 1) * CX, :] = offset

    zero = jnp.zeros(shape, F32)
    constant = expand(zero, zero, to_low, to_high, offsets)
    onehot, row_mask = panel_masks(sorted_ref[3:4, :].astype(jnp.int32))
    at_panel = pick(jnp.concatenate(constant, 0), onehot, row_mask)
    terms = [0.0, 0.0, 0.0]
    for half in range(2):
        lanes = slice(half * LANES, (half + 1) * LANES)
        place = (lane_iota((8, LANES)) + half * LANES).astype(F32)
        in_section = (place >= bound_ref[0:8, :]) & (place < bound_ref[8:16, :])
        for k in range(3):
            row = sorted_ref[k : k + 1, lanes] * at_panel[:, lanes]
            terms[k] = terms[k] + jnp.where(in_section, row, 0.0)
    meta = panel_ref[META_ROW - GEOM_ROW : META_ROW - GEOM_ROW + 1, :]
    for k, row in enumerate(section_rows(terms)):
        meta = meta + pltpu.roll(row, 8 * (k + 1), 1)

    for row in range(GEOM_ROW, SEND_ROWS):
        value = meta if row == META_ROW else panel_ref[row - GEOM_ROW : row - GEOM_ROW + 1, :]
        send_ref[pl.ds(row, COLS, stride=SEND_ROWS), :] = jnp.broadcast_to(value, (COLS, LANES))
    ports = [level(mat_ref, PORT_AT + j) for j in range(3)] + [first, last]
    ports += [level(mat_ref, PORT_AT + 3), level(mat_ref, PORT_AT + 4)]
    ports += [level(w_ref, 0), level(w_ref, CZ - 1)]
    for at, value in enumerate(ports):
        for half in range(2):
            row = half * 8 + at if at < 8 else 16 + half
            for group in range(0, COLS, OWNERS):
                send_ref[pl.ds(group * SEND_ROWS + row, OWNERS, stride=SEND_ROWS), :] = value[
                    :, half * LANES : (half + 1) * LANES
                ]


def solve_columns(half, recv_ref, group_ref, ends_ref, all_ref, parts_ref):
    def value(at, x):
        row = half * 8 + at if at < 8 else 16 + half
        return recv_ref[pl.ds(x * SEND_ROWS + row, 4, stride=4 * SEND_ROWS), :]

    per = [[value(at, x) for x in range(4)] for at in range(9)]
    low_k, high_k, link, low_r, high_r, low_d, high_d, low_w, high_w = per
    join = [2.0 / (high_d[x] + low_d[x + 1]) for x in range(3)]
    for x in range(3):
        high_r[x] = high_r[x] - HALF_DIV * low_w[x + 1]
        low_r[x + 1] = low_r[x + 1] + HALF_DIV * high_w[x]
    ground, source, edges = [], [], []
    for x in range(4):
        ground += [low_k[x], high_k[x]]
        source += [low_r[x], high_r[x]]
        edges += [link[x]] + ([join[x]] if x < 3 else [])
    first, last, across, to_low, to_high, inverse = condense(ground, edges)
    first_r, last_r, offsets = condense_source(source, to_low, to_high, inverse)

    stored = [first, last, across, first_r, last_r, low_d[0], high_d[3], low_w[0], high_w[3]]
    for at, x in enumerate(stored):
        group_ref[half, at * 4 : (at + 1) * 4, :] = x
    per = [[group_ref[half, at * 4 + z : at * 4 + z + 1, :] for z in range(4)] for at in range(9)]
    low_k, high_k, link, low_r, high_r, low_d, high_d, low_w, high_w = per
    outer = [2.0 / (high_d[z] + low_d[z + 1]) for z in range(3)]
    for z in range(3):
        high_r[z] = high_r[z] - HALF_DIV * low_w[z + 1]
        low_r[z + 1] = low_r[z + 1] + HALF_DIV * high_w[z]
    ground, source, edges = [], [], []
    for z in range(4):
        ground += [low_k[z], high_k[z]]
        source += [low_r[z], high_r[z]]
        edges += [link[z]] + ([outer[z]] if z < 3 else [])
    k_a, k_b, f_ab, *factors = condense(ground, edges)
    r_a, r_b, outer_offsets = condense_source(source, *factors)
    scale = 1.0 / (k_a * k_b + f_ab * (k_a + k_b))
    p_a = ((k_b + f_ab) * r_a + f_ab * r_b) * scale
    p_b = ((k_a + f_ab) * r_b + f_ab * r_a) * scale
    nodes = expand(p_a, p_b, *factors[:2], outer_offsets)
    zero_row = jnp.zeros((1, LANES), F32)
    flux = [outer[z] * (nodes[2 * z + 2] - nodes[2 * z + 1]) for z in range(3)]
    for z in range(4):
        ends_ref[half, z : z + 1, :] = nodes[2 * z]
        ends_ref[half, 4 + z : 5 + z, :] = nodes[2 * z + 1]
        ends_ref[half, 8 + z : 9 + z, :] = flux[z - 1] if z > 0 else zero_row
        ends_ref[half, 12 + z : 13 + z, :] = flux[z] if z < 3 else zero_row

    nodes = expand(ends_ref[half, 0:4, :], ends_ref[half, 4:8, :], to_low, to_high, offsets)
    inner = [join[x] * (nodes[2 * x + 2] - nodes[2 * x + 1]) for x in range(3)]
    below = [ends_ref[half, 8:12, :]] + inner
    above = inner + [ends_ref[half, 12:16, :]]

    def put(ref, rows, at, x, what):
        ref[pl.ds(x * rows + at, 4, stride=4 * rows), :] = what

    for x in range(4):
        for at, what in enumerate([nodes[2 * x], nodes[2 * x + 1], below[x], above[x]]):
            put(all_ref, BACK_ROWS, half * 4 + at, x, what)
        for end in range(2):
            for at, part in enumerate(split_three(nodes[2 * x + end])):
                put(parts_ref, 16, half * 8 + 3 * end + at, x, part.astype(F32))
            put(parts_ref, 16, half * 8 + 6 + end, x, jnp.zeros((4, LANES), F32))


def owner_kernel(
    recv_ref, back_ref, group_ref, ends_ref, all_ref, parts_ref, place_ref, picked_ref
):
    for half in range(2):
        solve_columns(half, recv_ref, group_ref, ends_ref, all_ref, parts_ref)

    column_device = lax.axis_index("col")
    mine = lax.rem(column_device, OWNERS) * NY

    def panel(row):
        return recv_ref[pl.ds(row, COLS, stride=SEND_ROWS), :]

    inside, upper = [], []
    for half in range(2):
        place = panel(COLUMN_ROW + half).astype(jnp.int32) - mine
        inside.append((place >= 0) & (place < NY))
        upper.append(place >= LANES)
        place_ref[half * COLS : (half + 1) * COLS, :] = (place & (LANES - 1)).astype(F32)
    want = row_iota((LANES, LANES)).astype(F32).astype(jnp.bfloat16)
    for block in range(COLS):
        ends = parts_ref[block * 16 : (block + 1) * 16, :].astype(jnp.bfloat16)
        onehots = []
        for half in range(2):
            at = half * COLS + block
            place = place_ref[at : at + 1, :].astype(jnp.bfloat16)
            onehots.append(jnp.where(want == place, jnp.bfloat16(1.0), jnp.bfloat16(0.0)))
        got = jnp.dot(ends, jnp.concatenate(onehots, 1), preferred_element_type=F32)
        for half in range(2):
            at = half * COLS + block
            picked_ref[at * 16 : (at + 1) * 16, :] = got[:, half * LANES : (half + 1) * LANES]
    meta = panel(META_ROW)
    starts = [meta[:, j : j + 1] for j in range(8)] + [float(PANELS_DEV)]
    sums = [[None] * 8 for _ in range(3)]
    for half in range(2):

        def got(at):
            return picked_ref[pl.ds(half * COLS * 16 + at, COLS, stride=16), :]

        low = [got(8 * h) + got(8 * h + 1) + got(8 * h + 2) for h in range(2)]
        high = [got(8 * h + 3) + got(8 * h + 4) + got(8 * h + 5) for h in range(2)]
        low = jnp.where(upper[half], low[1], low[0])
        high = jnp.where(upper[half], high[1], high[0])
        at_panel = high + panel(SHARE_ROW + half) * (low - high)
        at_panel = jnp.where(inside[half], at_panel, 0.0)
        place = (lane_iota((COLS, LANES)) + half * LANES).astype(F32)
        reached = [place >= start for start in starts]
        terms = [panel(GEOM_ROW + 2 * k + half) * at_panel for k in range(3)]
        for j in range(8):
            in_section = reached[j] & jnp.logical_not(reached[j + 1])
            for k in range(3):
                part = jnp.where(in_section, terms[k], 0.0)
                part = part[0:8, :] + part[8:16, :]
                sums[k][j] = part if half == 0 else sums[k][j] + part
    terms = [
        jnp.concatenate([jnp.sum(x, axis=0, keepdims=True) for x in sums[k]], 0)
        for k in range(3)
    ]
    constant = jnp.sum(meta, axis=0, keepdims=True)
    lanes = lane_iota((1, LANES))
    own = lax.rem(column_device, OWNERS) == 0
    rows = section_rows(terms)
    for k in range(3):
        moved = pltpu.roll(constant, LANES - 8 * (k + 1), 1)
        rows[k] = rows[k] + jnp.where((lanes < 8) & own, moved, 0.0)
    packed = sum(pltpu.roll(row, 8 * k, 1) for k, row in enumerate(rows))
    all_ref[pl.ds(8, COLS, stride=BACK_ROWS), :] = jnp.broadcast_to(packed, (COLS, LANES))
    mine = pl.multiple_of((column_device // OWNERS) * (OWNERS * BACK_ROWS), OWNERS * BACK_ROWS)
    back_ref[...] = all_ref[pl.ds(mine, OWNERS * BACK_ROWS), :]


def load_kernel(back_ref, load_ref):
    packed = back_ref[pl.ds(8, OWNERS, stride=BACK_ROWS), :]
    packed = jnp.sum(packed, axis=0, keepdims=True)
    rows = [packed] + [pltpu.roll(packed, LANES - 8 * k, 1) for k in range(1, 3)]
    load_ref[...] = jnp.concatenate(rows + [jnp.zeros((5, LANES), F32)], 0)


def field_kernel(back_ref, mat_ref, offset_ref, w_ref, pressure_ref, velocity_ref):
    def end(at):
        halves = [back_ref[pl.ds(half * 4 + at, CX, stride=BACK_ROWS), :] for half in range(2)]
        return jnp.concatenate(halves, axis=1)

    to_low = [level(mat_ref, A_AT + j) for j in range(CZ - 2)]
    to_high = [level(mat_ref, B_AT + j) for j in range(CZ - 2)]
    offsets = [level(offset_ref, j) for j in range(CZ - 2)]
    pressure = expand(end(0), end(1), to_low, to_high, offsets)
    flux = [end(2)]
    for z in range(CZ - 1):
        flux.append(level(mat_ref, FACE_AT + z) * (pressure[z + 1] - pressure[z]))
    flux.append(end(3))
    for z in range(CZ):
        pressure_ref[z * CX : (z + 1) * CX, :] = pressure[z]
        velocity_ref[z * CX : (z + 1) * CX, :] = level(w_ref, z) - 0.5 * (flux[z + 1] + flux[z])


def section_kernel(load_ref, pair_ref, other_ref, out_ref):
    core = lax.rem(lax.axis_index("slab"), 2)
    even = core == 0
    received, beyond = pair_ref[1 - core], other_ref[...]
    from_left = jnp.where(even, beyond, received)
    from_right = jnp.where(even, received, beyond)
    lanes = lane_iota((8, LANES))
    total = load_ref[...]
    total = total + jnp.where(lanes < 4, pltpu.roll(from_left, LANES - 4, 1), 0.0)
    total = total + jnp.where(lanes >= 4, pltpu.roll(from_right, 4, 1), 0.0)
    total = pltpu.roll(total, LANES - REACH, 1)
    out_ref[...] = total[0:3, 0:SEC_DEV]


def call(kernel, outs, scratch=(), flops=20000):
    shapes = [jax.ShapeDtypeStruct(shape, F32) for shape in outs]
    return pl.pallas_call(
        kernel,
        out_shape=shapes if len(shapes) > 1 else shapes[0],
        scratch_shapes=[pltpu.VMEM(shape, F32) for shape in scratch],
        compiler_params=pltpu.CompilerParams(vmem_limit_bytes=16 * 1024 * 1024),
        cost_estimate=pl.CostEstimate(flops=flops, bytes_accessed=500000, transcendentals=0),
    )


def exchange(x, parts, groups=None):
    rows, lanes = x.shape
    x = x.reshape(parts, 1, rows // parts * lanes)
    x = lax.all_to_all(x, "col", 0, 0, axis_index_groups=groups, tiled=True)
    return x.reshape(rows, lanes)


def per_device(p_star, u_star, v_star, w_star, flags, panel_cell, panel_section, panel_geom):
    flat = (CZ * CX, NY)
    p, u, v, w = (x.reshape(flat) for x in (p_star, u_star, v_star, w_star))
    flags = flags.reshape(flat)
    cell = panel_cell.reshape(1, PANELS_DEV)
    section = panel_section.reshape(1, PANELS_DEV)
    slabs = lax.axis_size("slab")
    cores = [[i, i + 1] for i in range(0, slabs, 2)]
    others = [(i, i + 1) for i in range(1, slabs - 1, 2)]
    others += [(j, i) for i, j in others]

    inputs = [p, u, v, w, flags, cell, section, panel_geom]
    shapes = [(CZ, NY), (CZ, NY), (16, LANES), (8, PANELS_DEV)]
    p, u, v, w, flags, to_other, to_pair, bounds, ordered = pl.pallas_call(
        fetch_kernel,
        out_shape=[jax.ShapeDtypeStruct(x.shape, x.dtype) for x in inputs[:5]]
        + [jax.ShapeDtypeStruct(shape, F32) for shape in shapes],
        in_specs=[pl.BlockSpec(memory_space=pltpu.HBM)] * 8,
        scratch_shapes=[pltpu.VMEM(x.shape, x.dtype) for x in inputs[5:]]
        + [pltpu.SemaphoreType.DMA((8,))],
        compiler_params=pltpu.CompilerParams(vmem_limit_bytes=16 * 1024 * 1024),
        cost_estimate=pl.CostEstimate(flops=20000, bytes_accessed=500000, transcendentals=0),
    )(*[pltpu.with_memory_space_constraint(x, pltpu.HBM) for x in inputs])
    from_other = lax.ppermute(to_other, "slab", others)
    from_pair = lax.all_gather(to_pair, "slab", axis_index_groups=cores)
    mat, source, panel = call(
        matrix_kernel, [(MAT_LEVELS * CX, NY), flat, (16, LANES)], flops=5000000
    )(p, u, v, w, flags, bounds, ordered)
    send, offsets = call(pack_kernel, [(COLS * SEND_ROWS, LANES), ((CZ - 2) * CX, NY)])(
        mat, source, from_other, from_pair, w, panel, bounds, ordered
    )
    recv = exchange(send, COLS)
    back = call(
        owner_kernel,
        [(OWNERS * BACK_ROWS, LANES)],
        [
            (2, 40, LANES),
            (2, 16, LANES),
            (COLS * BACK_ROWS, LANES),
            (COLS * 16, LANES),
            (2 * COLS, LANES),
            (2 * COLS * 16, LANES),
        ],
    )(recv)
    sets = [list(range(at, at + OWNERS)) for at in range(0, COLS, OWNERS)]
    back = exchange(back, OWNERS, sets)
    loads = call(load_kernel, [(8, LANES)])(back)
    loads_other = lax.ppermute(loads, "slab", others)
    loads_pair = lax.all_gather(loads, "slab", axis_index_groups=cores)
    pressure, velocity = call(field_kernel, [flat, flat], flops=5000000)(back, mat, offsets, w)
    section_loads = call(section_kernel, [(3, SEC_DEV)])(loads, loads_pair, loads_other)
    return pressure.reshape(p_star.shape), velocity.reshape(p_star.shape), section_loads


def solution(mesh):
    in_specs = (
        P("col", "slab", None),
        P("col", "slab", None),
        P("col", "slab", None),
        P("col", "slab", None),
        P("col", "slab", None),
        P(("col", "slab")),
        P(("col", "slab")),
        P(None, ("col", "slab")),
    )
    out_specs = (P("col", "slab", None), P("col", "slab", None), P(None, "slab"))
    return jax.shard_map(
        per_device, mesh=mesh, in_specs=in_specs, out_specs=out_specs, check_vma=False
    )
```

```python
import functools

import jax
import jax.numpy as jnp
from jax import lax
from jax.experimental import pallas as pl
from jax.experimental.pallas import tpu as pltpu
from jax.sharding import PartitionSpec as P

SEC_DEV = 4
EOS_ITERS = 3
KAPPA_SCALE = 0.01
AIR_DENSITY = 0.1
GAMMA_HORIZ = 0.001
DIVERGENCE_SCALE = 0.005
HALF_DIV = 0.5 * DIVERGENCE_SCALE

CZ = 8
CX = 8
NY = 256
LANES = 128
COLS = 16
PANELS_DEV = 256
REACH = 2
OWNERS = 8
SEND_ROWS = 29
BACK_ROWS = 9
GEOM_ROW, SHARE_ROW, COLUMN_ROW, META_ROW = 18, 24, 26, 28

F32 = jnp.float32


def row_iota(shape):
    return lax.broadcasted_iota(jnp.int32, shape, 0)


def lane_iota(shape):
    return lax.broadcasted_iota(jnp.int32, shape, 1)


def level(ref, z):
    return ref[z * CX : (z + 1) * CX, :]


def split_three(x):
    high = x.astype(jnp.bfloat16)
    rest = x - high.astype(F32)
    middle = rest.astype(jnp.bfloat16)
    low = (rest - middle.astype(F32)).astype(jnp.bfloat16)
    return high, middle, low


def exact_dot(x, onehot):
    rows = x.shape[0]
    parts = split_three(x)
    if rows % 16:
        parts = [part.astype(F32) for part in parts]
    parts = jnp.concatenate(parts, 0).astype(jnp.bfloat16)
    got = jnp.dot(parts, onehot, preferred_element_type=F32)
    return got[:rows] + got[rows : 2 * rows] + got[2 * rows :]


def pick(fields, onehot, row_mask):
    total = exact_dot(fields, onehot)
    return jnp.sum(jnp.where(row_mask, total, 0.0), axis=0, keepdims=True)


def panel_masks(cell):
    onehot = (row_iota((NY, PANELS_DEV)) == (cell & (NY - 1))).astype(F32)
    row_mask = row_iota((CZ * CX, PANELS_DEV)) == (cell >> 8)
    return onehot.astype(jnp.bfloat16), row_mask


def halving(count):
    nodes, order = list(range(count)), []
    while len(nodes) > 2:
        gone = range(1, len(nodes) - 1, 2)
        order += [(nodes[i], nodes[i - 1], nodes[i + 1]) for i in gone]
        nodes = [node for i, node in enumerate(nodes) if i not in gone]
    return order


def condense(ground, edges):
    count = len(ground)
    ground = list(ground)
    edges = {(i, i + 1): edge for i, edge in enumerate(edges)}
    to_low, to_high, inverse = ([None] * (count - 2) for _ in range(3))
    for node, low, high in halving(count):
        inv = 1.0 / (ground[node] + edges[low, node] + edges[node, high])
        a, b = edges[low, node] * inv, edges[node, high] * inv
        to_low[node - 1], to_high[node - 1], inverse[node - 1] = a, b, inv
        ground[low] = ground[low] + a * ground[node]
        ground[high] = ground[high] + b * ground[node]
        edges[low, high] = edges[low, node] * b
    return ground[0], ground[-1], edges[0, count - 1], to_low, to_high, inverse


def condense_source(source, to_low, to_high, inverse):
    source = list(source)
    for node, low, high in halving(len(source)):
        source[low] = source[low] + to_low[node - 1] * source[node]
        source[high] = source[high] + to_high[node - 1] * source[node]
    offsets = [x * inv for x, inv in zip(source[1:-1], inverse)]
    return source[0], source[-1], offsets


def expand(first, last, to_low, to_high, offsets):
    values = [first] + [None] * len(offsets) + [last]
    for node, low, high in reversed(halving(len(values))):
        inflow = to_low[node - 1] * values[low] + to_high[node - 1] * values[high]
        values[node] = inflow if offsets[node - 1] is None else offsets[node - 1] + inflow
    return values


def to_row(column):
    on_diagonal = row_iota((8, LANES)) == lane_iota((8, LANES))
    return jnp.sum(jnp.where(on_diagonal, column, 0.0), axis=0, keepdims=True)


def section_rows(terms):
    return [to_row(jnp.sum(term, axis=1, keepdims=True)) for term in terms]


def sort_panels(section, rows):
    square = (PANELS_DEV, PANELS_DEV)
    key = section * PANELS_DEV + lane_iota((1, PANELS_DEV))
    key = key.astype(F32)
    on_diagonal = row_iota(square) == lane_iota(square)
    key_column = jnp.sum(jnp.where(on_diagonal, key, 0.0), axis=1, keepdims=True)
    rank = jnp.sum(jnp.where(key < key_column, 1.0, 0.0), axis=1, keepdims=True)
    order = jnp.where(lane_iota(square).astype(F32) == rank, 1.0, 0.0).astype(jnp.bfloat16)
    return exact_dot(rows, order)


def fetch_kernel(*refs):
    sources, targets = refs[:8], refs[8:13] + refs[17:20]
    other_ref, pair_ref, bound_ref, sorted_ref = refs[13:17]
    p_ref, u_ref = targets[:2]
    cell_ref, sec_ref, geom_ref = targets[5:]
    fetches = [
        pltpu.make_async_copy(source, target, refs[20].at[i])
        for i, (source, target) in enumerate(zip(sources, targets))
    ]
    for fetch in fetches[5:] + fetches[:5]:
        fetch.start()
    slab = lax.axis_index("slab")
    even = lax.rem(slab, 2) == 0
    for fetch in fetches[5:]:
        fetch.wait()
    section = sec_ref[...] - (slab * SEC_DEV - REACH)
    rows = [geom_ref[k : k + 1, :] for k in range(3)] + [cell_ref[...].astype(F32)]
    rows = jnp.concatenate(rows + [jnp.zeros((4, PANELS_DEV), F32)], 0)
    sorted_ref[...] = sort_panels(section, rows)
    at_section = row_iota((8, PANELS_DEV))
    for at, before in enumerate((section < at_section, section <= at_section)):
        count = jnp.sum(jnp.where(before, 1.0, 0.0), axis=1, keepdims=True)
        bound_ref[at * 8 : (at + 1) * 8, :] = jnp.broadcast_to(count, (8, LANES))
    for fetch in fetches[:5]:
        fetch.wait()
    for z in range(CZ):
        first, last = z * CX, (z + 1) * CX - 1
        leading = GAMMA_HORIZ * p_ref[first : first + 1, :] - HALF_DIV * u_ref[first : first + 1, :]
        trailing = GAMMA_HORIZ * p_ref[last : last + 1, :] + HALF_DIV * u_ref[last : last + 1, :]
        other_ref[z : z + 1, :] = jnp.where(even, leading, trailing)
        pair_ref[z : z + 1, :] = jnp.where(even, trailing, leading)


A_AT, B_AT, I_AT, FACE_AT, PORT_AT = 0, 6, 12, 18, 25
MAT_LEVELS = 30


def matrix_kernel(
    p_ref, u_ref, v_ref, w_ref, flags_ref, bound_ref, sorted_ref, mat_ref, src_ref, panel_ref
):
    shape = (CX, NY)
    rows, lanes = row_iota(shape), lane_iota(shape)
    densities, kappas = [], []
    for z in range(CZ):
        p, flags = level(p_ref, z), level(flags_ref, z)
        air = jnp.where(flags == 1, 1.0, jnp.where(flags == 2, 0.5, 0.0)).astype(F32)
        water = jnp.ones_like(p)
        for _ in range(EOS_ITERS):
            square = water * water
            cube = square * water
            sixth = cube * cube
            water = water - (sixth * water - 1.0 - p) / (7.0 * sixth)
        shifted = 1.0 + p
        air_density = AIR_DENSITY * jnp.exp(jnp.log(shifted) * (1.0 / 1.4))
        densities.append(air * air_density + (1.0 - air) * water)
        kappa = KAPPA_SCALE * (air / (1.4 * shifted) + (1.0 - air) / (7.0 * shifted))
        kappas.append(kappa)

        u, v = level(u_ref, z), level(v_ref, z)

        def beside(x, axis, step):
            size = shape[axis]
            moved = pltpu.roll(x, (-step) % size, axis)
            at = rows if axis == 0 else lanes
            return jnp.where(at == (size - 1 if step > 0 else 0), 0.0, moved)

        laplacian = (
            beside(p, 0, 1) + beside(p, 0, -1) + beside(p, 1, 1) + beside(p, 1, -1) - 4.0 * p
        )
        divergence = 0.5 * (beside(u, 0, 1) - beside(u, 0, -1)) + 0.5 * (
            beside(v, 1, 1) - beside(v, 1, -1)
        )
        if z == 0:
            w_difference = level(w_ref, 1)
        elif z == CZ - 1:
            w_difference = -level(w_ref, CZ - 2)
        else:
            w_difference = level(w_ref, z + 1) - level(w_ref, z - 1)
        divergence = divergence + 0.5 * w_difference
        src_ref[z * CX : (z + 1) * CX, :] = (
            kappa * p + GAMMA_HORIZ * laplacian - DIVERGENCE_SCALE * divergence
        )
    faces = [2.0 / (densities[z] + densities[z + 1]) for z in range(CZ - 1)]
    first, last, link, to_low, to_high, inverse = condense(kappas, faces)
    stored = to_low + to_high + inverse + faces + [first, last, link, densities[0], densities[-1]]
    for at, value in enumerate(stored):
        mat_ref[at * CX : (at + 1) * CX, :] = value

    zero, one = jnp.zeros(shape, F32), jnp.ones(shape, F32)
    no_offset = [None] * (CZ - 2)
    rows = sorted_ref[...]
    cell = rows[3:4, :].astype(jnp.int32)
    onehot, row_mask = panel_masks(cell)
    from_first = expand(one, zero, to_low, to_high, no_offset)
    from_last = expand(zero, one, to_low, to_high, no_offset)
    at_first = pick(jnp.concatenate(from_first, 0), onehot, row_mask)
    at_last = pick(jnp.concatenate(from_last, 0), onehot, row_mask)
    panel_rows = [rows[k : k + 1, :] * (at_first + at_last) for k in range(3)]
    panel_rows.append(at_first / (at_first + at_last))
    panel_rows.append((cell & (CX * NY - 1)).astype(F32))
    panel_ref[...] = jnp.zeros_like(panel_ref)
    for at, row in enumerate(panel_rows):
        for half in range(2):
            panel_ref[2 * at + half : 2 * at + half + 1, :] = row[
                :, half * LANES : (half + 1) * LANES
            ]
    panel_ref[META_ROW - GEOM_ROW : META_ROW - GEOM_ROW + 1, :] = to_row(bound_ref[0:8, 0:1])


def pack_kernel(
    mat_ref, src_ref, other_ref, pair_ref, w_ref, panel_ref, bound_ref, sorted_ref,
    send_ref, offset_ref,
):
    core = lax.rem(lax.axis_index("slab"), 2)
    even = core == 0
    shape = (CX, NY)
    rows = row_iota(shape)
    received, beyond = pair_ref[1 - core], other_ref[...]
    from_left = jnp.where(even, beyond, received)
    from_right = jnp.where(even, received, beyond)
    source = []
    for z in range(CZ):
        halo = jnp.where(rows == 0, from_left[z : z + 1, :], 0.0) + jnp.where(
            rows == CX - 1, from_right[z : z + 1, :], 0.0
        )
        source.append(level(src_ref, z) + halo)
    to_low = [level(mat_ref, A_AT + j) for j in range(CZ - 2)]
    to_high = [level(mat_ref, B_AT + j) for j in range(CZ - 2)]
    inverse = [level(mat_ref, I_AT + j) for j in range(CZ - 2)]
    first, last, offsets = condense_source(source, to_low, to_high, inverse)
    for j, offset in enumerate(offsets):
        offset_ref[j * CX : (j + 1) * CX, :] = offset

    zero = jnp.zeros(shape, F32)
    constant = expand(zero, zero, to_low, to_high, offsets)
    onehot, row_mask = panel_masks(sorted_ref[3:4, :].astype(jnp.int32))
    at_panel = pick(jnp.concatenate(constant, 0), onehot, row_mask)
    terms = [0.0, 0.0, 0.0]
    for half in range(2):
        lanes = slice(half * LANES, (half + 1) * LANES)
        place = (lane_iota((8, LANES)) + half * LANES).astype(F32)
        in_section = (place >= bound_ref[0:8, :]) & (place < bound_ref[8:16, :])
        for k in range(3):
            row = sorted_ref[k : k + 1, lanes] * at_panel[:, lanes]
            terms[k] = terms[k] + jnp.where(in_section, row, 0.0)
    meta = panel_ref[META_ROW - GEOM_ROW : META_ROW - GEOM_ROW + 1, :]
    for k, row in enumerate(section_rows(terms)):
        meta = meta + pltpu.roll(row, 8 * (k + 1), 1)

    for row in range(GEOM_ROW, SEND_ROWS):
        value = meta if row == META_ROW else panel_ref[row - GEOM_ROW : row - GEOM_ROW + 1, :]
        send_ref[pl.ds(row, COLS, stride=SEND_ROWS), :] = jnp.broadcast_to(value, (COLS, LANES))
    ports = [level(mat_ref, PORT_AT + j) for j in range(3)] + [first, last]
    ports += [level(mat_ref, PORT_AT + 3), level(mat_ref, PORT_AT + 4)]
    ports += [level(w_ref, 0), level(w_ref, CZ - 1)]
    for at, value in enumerate(ports):
        for half in range(2):
            row = half * 8 + at if at < 8 else 16 + half
            for group in range(0, COLS, OWNERS):
                send_ref[pl.ds(group * SEND_ROWS + row, OWNERS, stride=SEND_ROWS), :] = value[
                    :, half * LANES : (half + 1) * LANES
                ]


def solve_columns(half, recv_ref, group_ref, ends_ref, all_ref, parts_ref):
    def value(at, x):
        row = half * 8 + at if at < 8 else 16 + half
        return recv_ref[pl.ds(x * SEND_ROWS + row, 4, stride=4 * SEND_ROWS), :]

    per = [[value(at, x) for x in range(4)] for at in range(9)]
    low_k, high_k, link, low_r, high_r, low_d, high_d, low_w, high_w = per
    join = [2.0 / (high_d[x] + low_d[x + 1]) for x in range(3)]
    for x in range(3):
        high_r[x] = high_r[x] - HALF_DIV * low_w[x + 1]
        low_r[x + 1] = low_r[x + 1] + HALF_DIV * high_w[x]
    ground, source, edges = [], [], []
    for x in range(4):
        ground += [low_k[x], high_k[x]]
        source += [low_r[x], high_r[x]]
        edges += [link[x]] + ([join[x]] if x < 3 else [])
    first, last, across, to_low, to_high, inverse = condense(ground, edges)
    first_r, last_r, offsets = condense_source(source, to_low, to_high, inverse)

    stored = [first, last, across, first_r, last_r, low_d[0], high_d[3], low_w[0], high_w[3]]
    for at, x in enumerate(stored):
        group_ref[half, at * 4 : (at + 1) * 4, :] = x
    per = [[group_ref[half, at * 4 + z : at * 4 + z + 1, :] for z in range(4)] for at in range(9)]
    low_k, high_k, link, low_r, high_r, low_d, high_d, low_w, high_w = per
    outer = [2.0 / (high_d[z] + low_d[z + 1]) for z in range(3)]
    for z in range(3):
        high_r[z] = high_r[z] - HALF_DIV * low_w[z + 1]
        low_r[z + 1] = low_r[z + 1] + HALF_DIV * high_w[z]
    ground, source, edges = [], [], []
    for z in range(4):
        ground += [low_k[z], high_k[z]]
        source += [low_r[z], high_r[z]]
        edges += [link[z]] + ([outer[z]] if z < 3 else [])
    k_a, k_b, f_ab, *factors = condense(ground, edges)
    r_a, r_b, outer_offsets = condense_source(source, *factors)
    scale = 1.0 / (k_a * k_b + f_ab * (k_a + k_b))
    p_a = ((k_b + f_ab) * r_a + f_ab * r_b) * scale
    p_b = ((k_a + f_ab) * r_b + f_ab * r_a) * scale
    nodes = expand(p_a, p_b, *factors[:2], outer_offsets)
    zero_row = jnp.zeros((1, LANES), F32)
    flux = [outer[z] * (nodes[2 * z + 2] - nodes[2 * z + 1]) for z in range(3)]
    for z in range(4):
        ends_ref[half, z : z + 1, :] = nodes[2 * z]
        ends_ref[half, 4 + z : 5 + z, :] = nodes[2 * z + 1]
        ends_ref[half, 8 + z : 9 + z, :] = flux[z - 1] if z > 0 else zero_row
        ends_ref[half, 12 + z : 13 + z, :] = flux[z] if z < 3 else zero_row

    nodes = expand(ends_ref[half, 0:4, :], ends_ref[half, 4:8, :], to_low, to_high, offsets)
    inner = [join[x] * (nodes[2 * x + 2] - nodes[2 * x + 1]) for x in range(3)]
    below = [ends_ref[half, 8:12, :]] + inner
    above = inner + [ends_ref[half, 12:16, :]]

    def put(ref, rows, at, x, what):
        ref[pl.ds(x * rows + at, 4, stride=4 * rows), :] = what

    for x in range(4):
        for at, what in enumerate([nodes[2 * x], nodes[2 * x + 1], below[x], above[x]]):
            put(all_ref, BACK_ROWS, half * 4 + at, x, what)
        for end in range(2):
            for at, part in enumerate(split_three(nodes[2 * x + end])):
                put(parts_ref, 16, half * 8 + 3 * end + at, x, part.astype(F32))
            put(parts_ref, 16, half * 8 + 6 + end, x, jnp.zeros((4, LANES), F32))


def owner_kernel(
    recv_ref, back_ref, group_ref, ends_ref, all_ref, parts_ref, place_ref, picked_ref
):
    for half in range(2):
        solve_columns(half, recv_ref, group_ref, ends_ref, all_ref, parts_ref)

    column_device = lax.axis_index("col")
    mine = lax.rem(column_device, OWNERS) * NY

    def panel(row):
        return recv_ref[pl.ds(row, COLS, stride=SEND_ROWS), :]

    inside, upper = [], []
    for half in range(2):
        place = panel(COLUMN_ROW + half).astype(jnp.int32) - mine
        inside.append((place >= 0) & (place < NY))
        upper.append(place >= LANES)
        place_ref[half * COLS : (half + 1) * COLS, :] = (place & (LANES - 1)).astype(F32)
    want = row_iota((LANES, LANES)).astype(F32).astype(jnp.bfloat16)
    for block in range(COLS):
        ends = parts_ref[block * 16 : (block + 1) * 16, :].astype(jnp.bfloat16)
        onehots = []
        for half in range(2):
            at = half * COLS + block
            place = place_ref[at : at + 1, :].astype(jnp.bfloat16)
            onehots.append(jnp.where(want == place, jnp.bfloat16(1.0), jnp.bfloat16(0.0)))
        got = jnp.dot(ends, jnp.concatenate(onehots, 1), preferred_element_type=F32)
        for half in range(2):
            at = half * COLS + block
            picked_ref[at * 16 : (at + 1) * 16, :] = got[:, half * LANES : (half + 1) * LANES]
    meta = panel(META_ROW)
    starts = [meta[:, j : j + 1] for j in range(8)] + [float(PANELS_DEV)]
    sums = [[None] * 8 for _ in range(3)]
    for half in range(2):

        def got(at):
            return picked_ref[pl.ds(half * COLS * 16 + at, COLS, stride=16), :]

        low = [got(8 * h) + got(8 * h + 1) + got(8 * h + 2) for h in range(2)]
        high = [got(8 * h + 3) + got(8 * h + 4) + got(8 * h + 5) for h in range(2)]
        low = jnp.where(upper[half], low[1], low[0])
        high = jnp.where(upper[half], high[1], high[0])
        at_panel = high + panel(SHARE_ROW + half) * (low - high)
        at_panel = jnp.where(inside[half], at_panel, 0.0)
        place = (lane_iota((COLS, LANES)) + half * LANES).astype(F32)
        reached = [place >= start for start in starts]
        terms = [panel(GEOM_ROW + 2 * k + half) * at_panel for k in range(3)]
        for j in range(8):
            in_section = reached[j] & jnp.logical_not(reached[j + 1])
            for k in range(3):
                part = jnp.where(in_section, terms[k], 0.0)
                part = part[0:8, :] + part[8:16, :]
                sums[k][j] = part if half == 0 else sums[k][j] + part
    terms = [
        jnp.concatenate([jnp.sum(x, axis=0, keepdims=True) for x in sums[k]], 0)
        for k in range(3)
    ]
    constant = jnp.sum(meta, axis=0, keepdims=True)
    lanes = lane_iota((1, LANES))
    own = lax.rem(column_device, OWNERS) == 0
    rows = section_rows(terms)
    for k in range(3):
        moved = pltpu.roll(constant, LANES - 8 * (k + 1), 1)
        rows[k] = rows[k] + jnp.where((lanes < 8) & own, moved, 0.0)
    packed = sum(pltpu.roll(row, 8 * k, 1) for k, row in enumerate(rows))
    all_ref[pl.ds(8, COLS, stride=BACK_ROWS), :] = jnp.broadcast_to(packed, (COLS, LANES))
    mine = pl.multiple_of((column_device // OWNERS) * (OWNERS * BACK_ROWS), OWNERS * BACK_ROWS)
    back_ref[...] = all_ref[pl.ds(mine, OWNERS * BACK_ROWS), :]


def load_kernel(back_ref, load_ref):
    packed = back_ref[pl.ds(8, OWNERS, stride=BACK_ROWS), :]
    packed = jnp.sum(packed, axis=0, keepdims=True)
    rows = [packed] + [pltpu.roll(packed, LANES - 8 * k, 1) for k in range(1, 3)]
    load_ref[...] = jnp.concatenate(rows + [jnp.zeros((5, LANES), F32)], 0)


def field_kernel(back_ref, mat_ref, offset_ref, w_ref, pressure_ref, velocity_ref):
    def end(at):
        halves = [back_ref[pl.ds(half * 4 + at, CX, stride=BACK_ROWS), :] for half in range(2)]
        return jnp.concatenate(halves, axis=1)

    to_low = [level(mat_ref, A_AT + j) for j in range(CZ - 2)]
    to_high = [level(mat_ref, B_AT + j) for j in range(CZ - 2)]
    offsets = [level(offset_ref, j) for j in range(CZ - 2)]
    pressure = expand(end(0), end(1), to_low, to_high, offsets)
    flux = [end(2)]
    for z in range(CZ - 1):
        flux.append(level(mat_ref, FACE_AT + z) * (pressure[z + 1] - pressure[z]))
    flux.append(end(3))
    for z in range(CZ):
        pressure_ref[z * CX : (z + 1) * CX, :] = pressure[z]
        velocity_ref[z * CX : (z + 1) * CX, :] = level(w_ref, z) - 0.5 * (flux[z + 1] + flux[z])


def section_kernel(load_ref, pair_ref, other_ref, out_ref):
    core = lax.rem(lax.axis_index("slab"), 2)
    even = core == 0
    received, beyond = pair_ref[1 - core], other_ref[...]
    from_left = jnp.where(even, beyond, received)
    from_right = jnp.where(even, received, beyond)
    lanes = lane_iota((8, LANES))
    total = load_ref[...]
    total = total + jnp.where(lanes < 4, pltpu.roll(from_left, LANES - 4, 1), 0.0)
    total = total + jnp.where(lanes >= 4, pltpu.roll(from_right, 4, 1), 0.0)
    total = pltpu.roll(total, LANES - REACH, 1)
    out_ref[...] = total[0:3, 0:SEC_DEV]


def call(kernel, outs, scratch=(), flops=20000):
    shapes = [jax.ShapeDtypeStruct(shape, F32) for shape in outs]
    return pl.pallas_call(
        kernel,
        out_shape=shapes if len(shapes) > 1 else shapes[0],
        scratch_shapes=[pltpu.VMEM(shape, F32) for shape in scratch],
        compiler_params=pltpu.CompilerParams(vmem_limit_bytes=16 * 1024 * 1024),
        cost_estimate=pl.CostEstimate(flops=flops, bytes_accessed=500000, transcendentals=0),
    )


def exchange(x, parts, groups=None):
    rows, lanes = x.shape
    x = x.reshape(parts, 1, rows // parts * lanes)
    x = lax.all_to_all(x, "col", 0, 0, axis_index_groups=groups, tiled=True)
    return x.reshape(rows, lanes)


def per_device(p_star, u_star, v_star, w_star, flags, panel_cell, panel_section, panel_geom):
    flat = (CZ * CX, NY)
    p, u, v, w = (x.reshape(flat) for x in (p_star, u_star, v_star, w_star))
    flags = flags.reshape(flat)
    cell = panel_cell.reshape(1, PANELS_DEV)
    section = panel_section.reshape(1, PANELS_DEV)
    slabs = lax.axis_size("slab")
    cores = [[i, i + 1] for i in range(0, slabs, 2)]
    others = [(i, i + 1) for i in range(1, slabs - 1, 2)]
    others += [(j, i) for i, j in others]

    inputs = [p, u, v, w, flags, cell, section, panel_geom]
    shapes = [(CZ, NY), (CZ, NY), (16, LANES), (8, PANELS_DEV)]
    p, u, v, w, flags, to_other, to_pair, bounds, ordered = pl.pallas_call(
        fetch_kernel,
        out_shape=[jax.ShapeDtypeStruct(x.shape, x.dtype) for x in inputs[:5]]
        + [jax.ShapeDtypeStruct(shape, F32) for shape in shapes],
        in_specs=[pl.BlockSpec(memory_space=pltpu.HBM)] * 8,
        scratch_shapes=[pltpu.VMEM(x.shape, x.dtype) for x in inputs[5:]]
        + [pltpu.SemaphoreType.DMA((8,))],
        compiler_params=pltpu.CompilerParams(vmem_limit_bytes=16 * 1024 * 1024),
        cost_estimate=pl.CostEstimate(flops=20000, bytes_accessed=500000, transcendentals=0),
    )(*[pltpu.with_memory_space_constraint(x, pltpu.HBM) for x in inputs])
    from_other = lax.ppermute(to_other, "slab", others)
    from_pair = lax.all_gather(to_pair, "slab", axis_index_groups=cores)
    mat, source, panel = call(
        matrix_kernel, [(MAT_LEVELS * CX, NY), flat, (16, LANES)], flops=5000000
    )(p, u, v, w, flags, bounds, ordered)
    send, offsets = call(pack_kernel, [(COLS * SEND_ROWS, LANES), ((CZ - 2) * CX, NY)])(
        mat, source, from_other, from_pair, w, panel, bounds, ordered
    )
    recv = exchange(send, COLS)
    back = call(
        owner_kernel,
        [(OWNERS * BACK_ROWS, LANES)],
        [
            (2, 40, LANES),
            (2, 16, LANES),
            (COLS * BACK_ROWS, LANES),
            (COLS * 16, LANES),
            (2 * COLS, LANES),
            (2 * COLS * 16, LANES),
        ],
    )(recv)
    sets = [list(range(at, at + OWNERS)) for at in range(0, COLS, OWNERS)]
    back = exchange(back, OWNERS, sets)
    loads = call(load_kernel, [(8, LANES)])(back)
    loads_other = lax.ppermute(loads, "slab", others)
    loads_pair = lax.all_gather(loads, "slab", axis_index_groups=cores)
    pressure, velocity = call(field_kernel, [flat, flat], flops=5000000)(back, mat, offsets, w)
    section_loads = call(section_kernel, [(3, SEC_DEV)])(loads, loads_pair, loads_other)
    return pressure.reshape(p_star.shape), velocity.reshape(p_star.shape), section_loads


def solution(mesh):
    in_specs = (
        P("col", "slab", None),
        P("col", "slab", None),
        P("col", "slab", None),
        P("col", "slab", None),
        P("col", "slab", None),
        P(("col", "slab")),
        P(("col", "slab")),
        P(None, ("col", "slab")),
    )
    out_specs = (P("col", "slab", None), P("col", "slab", None), P(None, "slab"))
    return jax.shard_map(
        per_device, mesh=mesh, in_specs=in_specs, out_specs=out_specs, check_vma=False
    )
```

```python
import functools

import jax
import jax.numpy as jnp
from jax import lax
from jax.experimental import pallas as pl
from jax.experimental.pallas import tpu as pltpu
from jax.sharding import PartitionSpec as P

SEC_DEV = 4
EOS_ITERS = 3
KAPPA_SCALE = 0.01
AIR_DENSITY = 0.1
GAMMA_HORIZ = 0.001
DIVERGENCE_SCALE = 0.005
HALF_DIV = 0.5 * DIVERGENCE_SCALE

CZ = 8
CX = 8
NY = 256
LANES = 128
COLS = 16
PANELS_DEV = 256
REACH = 2
OWNERS = 8
SEND_ROWS = 29
BACK_ROWS = 9
GEOM_ROW, SHARE_ROW, COLUMN_ROW, META_ROW = 18, 24, 26, 28

F32 = jnp.float32


def row_iota(shape):
    return lax.broadcasted_iota(jnp.int32, shape, 0)


def lane_iota(shape):
    return lax.broadcasted_iota(jnp.int32, shape, 1)


def level(ref, z):
    return ref[z * CX : (z + 1) * CX, :]


def split_three(x):
    high = x.astype(jnp.bfloat16)
    rest = x - high.astype(F32)
    middle = rest.astype(jnp.bfloat16)
    low = (rest - middle.astype(F32)).astype(jnp.bfloat16)
    return high, middle, low


def exact_dot(x, onehot):
    rows = x.shape[0]
    parts = split_three(x)
    if rows % 16:
        parts = [part.astype(F32) for part in parts]
    parts = jnp.concatenate(parts, 0).astype(jnp.bfloat16)
    got = jnp.dot(parts, onehot, preferred_element_type=F32)
    return got[:rows] + got[rows : 2 * rows] + got[2 * rows :]


def pick(fields, onehot, row_mask):
    total = exact_dot(fields, onehot)
    return jnp.sum(jnp.where(row_mask, total, 0.0), axis=0, keepdims=True)


def panel_masks(cell):
    onehot = (row_iota((NY, PANELS_DEV)) == (cell & (NY - 1))).astype(F32)
    row_mask = row_iota((CZ * CX, PANELS_DEV)) == (cell >> 8)
    return onehot.astype(jnp.bfloat16), row_mask


def halving(count):
    nodes, order = list(range(count)), []
    while len(nodes) > 2:
        gone = range(1, len(nodes) - 1, 2)
        order += [(nodes[i], nodes[i - 1], nodes[i + 1]) for i in gone]
        nodes = [node for i, node in enumerate(nodes) if i not in gone]
    return order


def condense(ground, edges):
    count = len(ground)
    ground = list(ground)
    edges = {(i, i + 1): edge for i, edge in enumerate(edges)}
    to_low, to_high, inverse = ([None] * (count - 2) for _ in range(3))
    for node, low, high in halving(count):
        inv = 1.0 / (ground[node] + edges[low, node] + edges[node, high])
        a, b = edges[low, node] * inv, edges[node, high] * inv
        to_low[node - 1], to_high[node - 1], inverse[node - 1] = a, b, inv
        ground[low] = ground[low] + a * ground[node]
        ground[high] = ground[high] + b * ground[node]
        edges[low, high] = edges[low, node] * b
    return ground[0], ground[-1], edges[0, count - 1], to_low, to_high, inverse


def condense_source(source, to_low, to_high, inverse):
    source = list(source)
    for node, low, high in halving(len(source)):
        source[low] = source[low] + to_low[node - 1] * source[node]
        source[high] = source[high] + to_high[node - 1] * source[node]
    offsets = [x * inv for x, inv in zip(source[1:-1], inverse)]
    return source[0], source[-1], offsets


def expand(first, last, to_low, to_high, offsets):
    values = [first] + [None] * len(offsets) + [last]
    for node, low, high in reversed(halving(len(values))):
        inflow = to_low[node - 1] * values[low] + to_high[node - 1] * values[high]
        values[node] = inflow if offsets[node - 1] is None else offsets[node - 1] + inflow
    return values


def to_row(column):
    on_diagonal = row_iota((8, LANES)) == lane_iota((8, LANES))
    return jnp.sum(jnp.where(on_diagonal, column, 0.0), axis=0, keepdims=True)


def section_rows(terms):
    return [to_row(jnp.sum(term, axis=1, keepdims=True)) for term in terms]


def sort_panels(section, rows):
    square = (PANELS_DEV, PANELS_DEV)
    key = section * PANELS_DEV + lane_iota((1, PANELS_DEV))
    key = key.astype(F32)
    on_diagonal = row_iota(square) == lane_iota(square)
    key_column = jnp.sum(jnp.where(on_diagonal, key, 0.0), axis=1, keepdims=True)
    rank = jnp.sum(jnp.where(key < key_column, 1.0, 0.0), axis=1, keepdims=True)
    order = jnp.where(lane_iota(square).astype(F32) == rank, 1.0, 0.0).astype(jnp.bfloat16)
    return exact_dot(rows, order)


def fetch_kernel(*refs):
    sources, targets = refs[:8], refs[8:13] + refs[17:20]
    other_ref, pair_ref, bound_ref, sorted_ref = refs[13:17]
    p_ref, u_ref = targets[:2]
    cell_ref, sec_ref, geom_ref = targets[5:]
    fetches = [
        pltpu.make_async_copy(source, target, refs[20].at[i])
        for i, (source, target) in enumerate(zip(sources, targets))
    ]
    for fetch in fetches[5:] + fetches[:5]:
        fetch.start()
    slab = lax.axis_index("slab")
    even = lax.rem(slab, 2) == 0
    for fetch in fetches[5:]:
        fetch.wait()
    section = sec_ref[...] - (slab * SEC_DEV - REACH)
    rows = [geom_ref[k : k + 1, :] for k in range(3)] + [cell_ref[...].astype(F32)]
    rows = jnp.concatenate(rows + [jnp.zeros((4, PANELS_DEV), F32)], 0)
    sorted_ref[...] = sort_panels(section, rows)
    at_section = row_iota((8, PANELS_DEV))
    for at, before in enumerate((section < at_section, section <= at_section)):
        count = jnp.sum(jnp.where(before, 1.0, 0.0), axis=1, keepdims=True)
        bound_ref[at * 8 : (at + 1) * 8, :] = jnp.broadcast_to(count, (8, LANES))
    for fetch in fetches[:5]:
        fetch.wait()
    for z in range(CZ):
        first, last = z * CX, (z + 1) * CX - 1
        leading = GAMMA_HORIZ * p_ref[first : first + 1, :] - HALF_DIV * u_ref[first : first + 1, :]
        trailing = GAMMA_HORIZ * p_ref[last : last + 1, :] + HALF_DIV * u_ref[last : last + 1, :]
        other_ref[z : z + 1, :] = jnp.where(even, leading, trailing)
        pair_ref[z : z + 1, :] = jnp.where(even, trailing, leading)


A_AT, B_AT, I_AT, FACE_AT, PORT_AT = 0, 6, 12, 18, 25
MAT_LEVELS = 30


def matrix_kernel(
    p_ref, u_ref, v_ref, w_ref, flags_ref, bound_ref, sorted_ref, mat_ref, src_ref, panel_ref
):
    shape = (CX, NY)
    rows, lanes = row_iota(shape), lane_iota(shape)
    densities, kappas = [], []
    for z in range(CZ):
        p, flags = level(p_ref, z), level(flags_ref, z)
        air = jnp.where(flags == 1, 1.0, jnp.where(flags == 2, 0.5, 0.0)).astype(F32)
        water = jnp.ones_like(p)
        for _ in range(EOS_ITERS):
            square = water * water
            cube = square * water
            sixth = cube * cube
            water = water - (sixth * water - 1.0 - p) / (7.0 * sixth)
        shifted = 1.0 + p
        air_density = AIR_DENSITY * jnp.exp(jnp.log(shifted) * (1.0 / 1.4))
        densities.append(air * air_density + (1.0 - air) * water)
        kappa = KAPPA_SCALE * (air / (1.4 * shifted) + (1.0 - air) / (7.0 * shifted))
        kappas.append(kappa)

        u, v = level(u_ref, z), level(v_ref, z)

        def beside(x, axis, step):
            size = shape[axis]
            moved = pltpu.roll(x, (-step) % size, axis)
            at = rows if axis == 0 else lanes
            return jnp.where(at == (size - 1 if step > 0 else 0), 0.0, moved)

        laplacian = (
            beside(p, 0, 1) + beside(p, 0, -1) + beside(p, 1, 1) + beside(p, 1, -1) - 4.0 * p
        )
        divergence = 0.5 * (beside(u, 0, 1) - beside(u, 0, -1)) + 0.5 * (
            beside(v, 1, 1) - beside(v, 1, -1)
        )
        if z == 0:
            w_difference = level(w_ref, 1)
        elif z == CZ - 1:
            w_difference = -level(w_ref, CZ - 2)
        else:
            w_difference = level(w_ref, z + 1) - level(w_ref, z - 1)
        divergence = divergence + 0.5 * w_difference
        src_ref[z * CX : (z + 1) * CX, :] = (
            kappa * p + GAMMA_HORIZ * laplacian - DIVERGENCE_SCALE * divergence
        )
    faces = [2.0 / (densities[z] + densities[z + 1]) for z in range(CZ - 1)]
    first, last, link, to_low, to_high, inverse = condense(kappas, faces)
    stored = to_low + to_high + inverse + faces + [first, last, link, densities[0], densities[-1]]
    for at, value in enumerate(stored):
        mat_ref[at * CX : (at + 1) * CX, :] = value

    zero, one = jnp.zeros(shape, F32), jnp.ones(shape, F32)
    no_offset = [None] * (CZ - 2)
    rows = sorted_ref[...]
    cell = rows[3:4, :].astype(jnp.int32)
    onehot, row_mask = panel_masks(cell)
    from_first = expand(one, zero, to_low, to_high, no_offset)
    from_last = expand(zero, one, to_low, to_high, no_offset)
    at_first = pick(jnp.concatenate(from_first, 0), onehot, row_mask)
    at_last = pick(jnp.concatenate(from_last, 0), onehot, row_mask)
    panel_rows = [rows[k : k + 1, :] * (at_first + at_last) for k in range(3)]
    panel_rows.append(at_first / (at_first + at_last))
    panel_rows.append((cell & (CX * NY - 1)).astype(F32))
    panel_ref[...] = jnp.zeros_like(panel_ref)
    for at, row in enumerate(panel_rows):
        for half in range(2):
            panel_ref[2 * at + half : 2 * at + half + 1, :] = row[
                :, half * LANES : (half + 1) * LANES
            ]
    panel_ref[META_ROW - GEOM_ROW : META_ROW - GEOM_ROW + 1, :] = to_row(bound_ref[0:8, 0:1])


def pack_kernel(
    mat_ref, src_ref, other_ref, pair_ref, w_ref, panel_ref, bound_ref, sorted_ref,
    send_ref, offset_ref,
):
    core = lax.rem(lax.axis_index("slab"), 2)
    even = core == 0
    shape = (CX, NY)
    rows = row_iota(shape)
    received, beyond = pair_ref[1 - core], other_ref[...]
    from_left = jnp.where(even, beyond, received)
    from_right = jnp.where(even, received, beyond)
    source = []
    for z in range(CZ):
        halo = jnp.where(rows == 0, from_left[z : z + 1, :], 0.0) + jnp.where(
            rows == CX - 1, from_right[z : z + 1, :], 0.0
        )
        source.append(level(src_ref, z) + halo)
    to_low = [level(mat_ref, A_AT + j) for j in range(CZ - 2)]
    to_high = [level(mat_ref, B_AT + j) for j in range(CZ - 2)]
    inverse = [level(mat_ref, I_AT + j) for j in range(CZ - 2)]
    first, last, offsets = condense_source(source, to_low, to_high, inverse)
    for j, offset in enumerate(offsets):
        offset_ref[j * CX : (j + 1) * CX, :] = offset

    zero = jnp.zeros(shape, F32)
    constant = expand(zero, zero, to_low, to_high, offsets)
    onehot, row_mask = panel_masks(sorted_ref[3:4, :].astype(jnp.int32))
    at_panel = pick(jnp.concatenate(constant, 0), onehot, row_mask)
    terms = [0.0, 0.0, 0.0]
    for half in range(2):
        lanes = slice(half * LANES, (half + 1) * LANES)
        place = (lane_iota((8, LANES)) + half * LANES).astype(F32)
        in_section = (place >= bound_ref[0:8, :]) & (place < bound_ref[8:16, :])
        for k in range(3):
            row = sorted_ref[k : k + 1, lanes] * at_panel[:, lanes]
            terms[k] = terms[k] + jnp.where(in_section, row, 0.0)
    meta = panel_ref[META_ROW - GEOM_ROW : META_ROW - GEOM_ROW + 1, :]
    for k, row in enumerate(section_rows(terms)):
        meta = meta + pltpu.roll(row, 8 * (k + 1), 1)

    for row in range(GEOM_ROW, SEND_ROWS):
        value = meta if row == META_ROW else panel_ref[row - GEOM_ROW : row - GEOM_ROW + 1, :]
        send_ref[pl.ds(row, COLS, stride=SEND_ROWS), :] = jnp.broadcast_to(value, (COLS, LANES))
    ports = [level(mat_ref, PORT_AT + j) for j in range(3)] + [first, last]
    ports += [level(mat_ref, PORT_AT + 3), level(mat_ref, PORT_AT + 4)]
    ports += [level(w_ref, 0), level(w_ref, CZ - 1)]
    for at, value in enumerate(ports):
        for half in range(2):
            row = half * 8 + at if at < 8 else 16 + half
            for group in range(0, COLS, OWNERS):
                send_ref[pl.ds(group * SEND_ROWS + row, OWNERS, stride=SEND_ROWS), :] = value[
                    :, half * LANES : (half + 1) * LANES
                ]


def solve_columns(half, recv_ref, group_ref, ends_ref, all_ref, parts_ref):
    def value(at, x):
        row = half * 8 + at if at < 8 else 16 + half
        return recv_ref[pl.ds(x * SEND_ROWS + row, 4, stride=4 * SEND_ROWS), :]

    per = [[value(at, x) for x in range(4)] for at in range(9)]
    low_k, high_k, link, low_r, high_r, low_d, high_d, low_w, high_w = per
    join = [2.0 / (high_d[x] + low_d[x + 1]) for x in range(3)]
    for x in range(3):
        high_r[x] = high_r[x] - HALF_DIV * low_w[x + 1]
        low_r[x + 1] = low_r[x + 1] + HALF_DIV * high_w[x]
    ground, source, edges = [], [], []
    for x in range(4):
        ground += [low_k[x], high_k[x]]
        source += [low_r[x], high_r[x]]
        edges += [link[x]] + ([join[x]] if x < 3 else [])
    first, last, across, to_low, to_high, inverse = condense(ground, edges)
    first_r, last_r, offsets = condense_source(source, to_low, to_high, inverse)

    stored = [first, last, across, first_r, last_r, low_d[0], high_d[3], low_w[0], high_w[3]]
    for at, x in enumerate(stored):
        group_ref[half, at * 4 : (at + 1) * 4, :] = x
    per = [[group_ref[half, at * 4 + z : at * 4 + z + 1, :] for z in range(4)] for at in range(9)]
    low_k, high_k, link, low_r, high_r, low_d, high_d, low_w, high_w = per
    outer = [2.0 / (high_d[z] + low_d[z + 1]) for z in range(3)]
    for z in range(3):
        high_r[z] = high_r[z] - HALF_DIV * low_w[z + 1]
        low_r[z + 1] = low_r[z + 1] + HALF_DIV * high_w[z]
    ground, source, edges = [], [], []
    for z in range(4):
        ground += [low_k[z], high_k[z]]
        source += [low_r[z], high_r[z]]
        edges += [link[z]] + ([outer[z]] if z < 3 else [])
    k_a, k_b, f_ab, *factors = condense(ground, edges)
    r_a, r_b, outer_offsets = condense_source(source, *factors)
    scale = 1.0 / (k_a * k_b + f_ab * (k_a + k_b))
    p_a = ((k_b + f_ab) * r_a + f_ab * r_b) * scale
    p_b = ((k_a + f_ab) * r_b + f_ab * r_a) * scale
    nodes = expand(p_a, p_b, *factors[:2], outer_offsets)
    zero_row = jnp.zeros((1, LANES), F32)
    flux = [outer[z] * (nodes[2 * z + 2] - nodes[2 * z + 1]) for z in range(3)]
    for z in range(4):
        ends_ref[half, z : z + 1, :] = nodes[2 * z]
        ends_ref[half, 4 + z : 5 + z, :] = nodes[2 * z + 1]
        ends_ref[half, 8 + z : 9 + z, :] = flux[z - 1] if z > 0 else zero_row
        ends_ref[half, 12 + z : 13 + z, :] = flux[z] if z < 3 else zero_row

    nodes = expand(ends_ref[half, 0:4, :], ends_ref[half, 4:8, :], to_low, to_high, offsets)
    inner = [join[x] * (nodes[2 * x + 2] - nodes[2 * x + 1]) for x in range(3)]
    below = [ends_ref[half, 8:12, :]] + inner
    above = inner + [ends_ref[half, 12:16, :]]

    def put(ref, rows, at, x, what):
        ref[pl.ds(x * rows + at, 4, stride=4 * rows), :] = what

    for x in range(4):
        for at, what in enumerate([nodes[2 * x], nodes[2 * x + 1], below[x], above[x]]):
            put(all_ref, BACK_ROWS, half * 4 + at, x, what)
        for end in range(2):
            for at, part in enumerate(split_three(nodes[2 * x + end])):
                put(parts_ref, 16, half * 8 + 3 * end + at, x, part.astype(F32))
            put(parts_ref, 16, half * 8 + 6 + end, x, jnp.zeros((4, LANES), F32))


def owner_kernel(
    recv_ref, back_ref, group_ref, ends_ref, all_ref, parts_ref, place_ref, picked_ref
):
    for half in range(2):
        solve_columns(half, recv_ref, group_ref, ends_ref, all_ref, parts_ref)

    column_device = lax.axis_index("col")
    mine = lax.rem(column_device, OWNERS) * NY

    def panel(row):
        return recv_ref[pl.ds(row, COLS, stride=SEND_ROWS), :]

    inside, upper = [], []
    for half in range(2):
        place = panel(COLUMN_ROW + half).astype(jnp.int32) - mine
        inside.append((place >= 0) & (place < NY))
        upper.append(place >= LANES)
        place_ref[half * COLS : (half + 1) * COLS, :] = (place & (LANES - 1)).astype(F32)
    want = row_iota((LANES, LANES)).astype(F32).astype(jnp.bfloat16)
    for block in range(COLS):
        ends = parts_ref[block * 16 : (block + 1) * 16, :].astype(jnp.bfloat16)
        onehots = []
        for half in range(2):
            at = half * COLS + block
            place = place_ref[at : at + 1, :].astype(jnp.bfloat16)
            onehots.append(jnp.where(want == place, jnp.bfloat16(1.0), jnp.bfloat16(0.0)))
        got = jnp.dot(ends, jnp.concatenate(onehots, 1), preferred_element_type=F32)
        for half in range(2):
            at = half * COLS + block
            picked_ref[at * 16 : (at + 1) * 16, :] = got[:, half * LANES : (half + 1) * LANES]
    meta = panel(META_ROW)
    starts = [meta[:, j : j + 1] for j in range(8)] + [float(PANELS_DEV)]
    sums = [[None] * 8 for _ in range(3)]
    for half in range(2):

        def got(at):
            return picked_ref[pl.ds(half * COLS * 16 + at, COLS, stride=16), :]

        low = [got(8 * h) + got(8 * h + 1) + got(8 * h + 2) for h in range(2)]
        high = [got(8 * h + 3) + got(8 * h + 4) + got(8 * h + 5) for h in range(2)]
        low = jnp.where(upper[half], low[1], low[0])
        high = jnp.where(upper[half], high[1], high[0])
        at_panel = high + panel(SHARE_ROW + half) * (low - high)
        at_panel = jnp.where(inside[half], at_panel, 0.0)
        place = (lane_iota((COLS, LANES)) + half * LANES).astype(F32)
        reached = [place >= start for start in starts]
        terms = [panel(GEOM_ROW + 2 * k + half) * at_panel for k in range(3)]
        for j in range(8):
            in_section = reached[j] & jnp.logical_not(reached[j + 1])
            for k in range(3):
                part = jnp.where(in_section, terms[k], 0.0)
                part = part[0:8, :] + part[8:16, :]
                sums[k][j] = part if half == 0 else sums[k][j] + part
    terms = [
        jnp.concatenate([jnp.sum(x, axis=0, keepdims=True) for x in sums[k]], 0)
        for k in range(3)
    ]
    constant = jnp.sum(meta, axis=0, keepdims=True)
    lanes = lane_iota((1, LANES))
    own = lax.rem(column_device, OWNERS) == 0
    rows = section_rows(terms)
    for k in range(3):
        moved = pltpu.roll(constant, LANES - 8 * (k + 1), 1)
        rows[k] = rows[k] + jnp.where((lanes < 8) & own, moved, 0.0)
    packed = sum(pltpu.roll(row, 8 * k, 1) for k, row in enumerate(rows))
    all_ref[pl.ds(8, COLS, stride=BACK_ROWS), :] = jnp.broadcast_to(packed, (COLS, LANES))
    mine = pl.multiple_of((column_device // OWNERS) * (OWNERS * BACK_ROWS), OWNERS * BACK_ROWS)
    back_ref[...] = all_ref[pl.ds(mine, OWNERS * BACK_ROWS), :]


def load_kernel(back_ref, load_ref):
    packed = back_ref[pl.ds(8, OWNERS, stride=BACK_ROWS), :]
    load_ref[...] = jnp.sum(packed, axis=0, keepdims=True)


def field_kernel(back_ref, mat_ref, offset_ref, w_ref, pressure_ref, velocity_ref):
    def end(at):
        halves = [back_ref[pl.ds(half * 4 + at, CX, stride=BACK_ROWS), :] for half in range(2)]
        return jnp.concatenate(halves, axis=1)

    to_low = [level(mat_ref, A_AT + j) for j in range(CZ - 2)]
    to_high = [level(mat_ref, B_AT + j) for j in range(CZ - 2)]
    offsets = [level(offset_ref, j) for j in range(CZ - 2)]
    pressure = expand(end(0), end(1), to_low, to_high, offsets)
    flux = [end(2)]
    for z in range(CZ - 1):
        flux.append(level(mat_ref, FACE_AT + z) * (pressure[z + 1] - pressure[z]))
    flux.append(end(3))
    for z in range(CZ):
        pressure_ref[z * CX : (z + 1) * CX, :] = pressure[z]
        velocity_ref[z * CX : (z + 1) * CX, :] = level(w_ref, z) - 0.5 * (flux[z + 1] + flux[z])


def section_kernel(load_ref, pair_ref, other_ref, out_ref):
    core = lax.rem(lax.axis_index("slab"), 2)
    even = core == 0
    received, beyond = pair_ref[1 - core], other_ref[...]
    from_left = jnp.where(even, beyond, received)
    from_right = jnp.where(even, received, beyond)
    lower = (lane_iota((1, LANES)) & 7) < 4
    total = load_ref[...] + jnp.where(
        lower, pltpu.roll(from_left, LANES - 4, 1), pltpu.roll(from_right, 4, 1)
    )
    for k in range(3):
        moved = pltpu.roll(total, LANES - 8 * k - REACH, 1)
        out_ref[k : k + 1, :] = moved[:, 0:SEC_DEV]


def call(kernel, outs, scratch=(), flops=20000):
    shapes = [jax.ShapeDtypeStruct(shape, F32) for shape in outs]
    return pl.pallas_call(
        kernel,
        out_shape=shapes if len(shapes) > 1 else shapes[0],
        scratch_shapes=[pltpu.VMEM(shape, F32) for shape in scratch],
        compiler_params=pltpu.CompilerParams(vmem_limit_bytes=16 * 1024 * 1024),
        cost_estimate=pl.CostEstimate(flops=flops, bytes_accessed=500000, transcendentals=0),
    )


def exchange(x, parts, groups=None):
    rows, lanes = x.shape
    x = x.reshape(parts, 1, rows // parts * lanes)
    x = lax.all_to_all(x, "col", 0, 0, axis_index_groups=groups, tiled=True)
    return x.reshape(rows, lanes)


def per_device(p_star, u_star, v_star, w_star, flags, panel_cell, panel_section, panel_geom):
    flat = (CZ * CX, NY)
    p, u, v, w = (x.reshape(flat) for x in (p_star, u_star, v_star, w_star))
    flags = flags.reshape(flat)
    cell = panel_cell.reshape(1, PANELS_DEV)
    section = panel_section.reshape(1, PANELS_DEV)
    slabs = lax.axis_size("slab")
    cores = [[i, i + 1] for i in range(0, slabs, 2)]
    others = [(i, i + 1) for i in range(1, slabs - 1, 2)]
    others += [(j, i) for i, j in others]

    inputs = [p, u, v, w, flags, cell, section, panel_geom]
    shapes = [(CZ, NY), (CZ, NY), (16, LANES), (8, PANELS_DEV)]
    p, u, v, w, flags, to_other, to_pair, bounds, ordered = pl.pallas_call(
        fetch_kernel,
        out_shape=[jax.ShapeDtypeStruct(x.shape, x.dtype) for x in inputs[:5]]
        + [jax.ShapeDtypeStruct(shape, F32) for shape in shapes],
        in_specs=[pl.BlockSpec(memory_space=pltpu.HBM)] * 8,
        scratch_shapes=[pltpu.VMEM(x.shape, x.dtype) for x in inputs[5:]]
        + [pltpu.SemaphoreType.DMA((8,))],
        compiler_params=pltpu.CompilerParams(vmem_limit_bytes=16 * 1024 * 1024),
        cost_estimate=pl.CostEstimate(flops=20000, bytes_accessed=500000, transcendentals=0),
    )(*[pltpu.with_memory_space_constraint(x, pltpu.HBM) for x in inputs])
    from_other = lax.ppermute(to_other, "slab", others)
    from_pair = lax.all_gather(to_pair, "slab", axis_index_groups=cores)
    mat, source, panel = call(
        matrix_kernel, [(MAT_LEVELS * CX, NY), flat, (16, LANES)], flops=5000000
    )(p, u, v, w, flags, bounds, ordered)
    send, offsets = call(pack_kernel, [(COLS * SEND_ROWS, LANES), ((CZ - 2) * CX, NY)])(
        mat, source, from_other, from_pair, w, panel, bounds, ordered
    )
    recv = exchange(send, COLS)
    back = call(
        owner_kernel,
        [(OWNERS * BACK_ROWS, LANES)],
        [
            (2, 40, LANES),
            (2, 16, LANES),
            (COLS * BACK_ROWS, LANES),
            (COLS * 16, LANES),
            (2 * COLS, LANES),
            (2 * COLS * 16, LANES),
        ],
    )(recv)
    sets = [list(range(at, at + OWNERS)) for at in range(0, COLS, OWNERS)]
    back = exchange(back, OWNERS, sets)
    loads = call(load_kernel, [(1, LANES)])(back)
    loads_other = lax.ppermute(loads, "slab", others)
    loads_pair = lax.all_gather(loads, "slab", axis_index_groups=cores)
    pressure, velocity = call(field_kernel, [flat, flat], flops=5000000)(back, mat, offsets, w)
    section_loads = call(section_kernel, [(3, SEC_DEV)])(loads, loads_pair, loads_other)
    return pressure.reshape(p_star.shape), velocity.reshape(p_star.shape), section_loads


def solution(mesh):
    in_specs = (
        P("col", "slab", None),
        P("col", "slab", None),
        P("col", "slab", None),
        P("col", "slab", None),
        P("col", "slab", None),
        P(("col", "slab")),
        P(("col", "slab")),
        P(None, ("col", "slab")),
    )
    out_specs = (P("col", "slab", None), P("col", "slab", None), P(None, "slab"))
    return jax.shard_map(
        per_device, mesh=mesh, in_specs=in_specs, out_specs=out_specs, check_vma=False
    )
```

```python
import functools

import jax
import jax.numpy as jnp
from jax import lax
from jax.experimental import pallas as pl
from jax.experimental.pallas import tpu as pltpu
from jax.sharding import PartitionSpec as P

SEC_DEV = 4
EOS_ITERS = 3
KAPPA_SCALE = 0.01
AIR_DENSITY = 0.1
GAMMA_HORIZ = 0.001
DIVERGENCE_SCALE = 0.005
HALF_DIV = 0.5 * DIVERGENCE_SCALE

CZ = 8
CX = 8
NY = 256
LANES = 128
COLS = 16
PANELS_DEV = 256
REACH = 2
OWNERS = 8
SEND_ROWS = 29
BACK_ROWS = 9
GEOM_ROW, SHARE_ROW, COLUMN_ROW, META_ROW = 18, 24, 26, 28

F32 = jnp.float32


def row_iota(shape):
    return lax.broadcasted_iota(jnp.int32, shape, 0)


def lane_iota(shape):
    return lax.broadcasted_iota(jnp.int32, shape, 1)


def level(ref, z):
    return ref[z * CX : (z + 1) * CX, :]


def split_three(x):
    high = x.astype(jnp.bfloat16)
    rest = x - high.astype(F32)
    middle = rest.astype(jnp.bfloat16)
    low = (rest - middle.astype(F32)).astype(jnp.bfloat16)
    return high, middle, low


def exact_dot(x, onehot):
    rows = x.shape[0]
    parts = split_three(x)
    if rows % 16:
        parts = [part.astype(F32) for part in parts]
    parts = jnp.concatenate(parts, 0).astype(jnp.bfloat16)
    got = jnp.dot(parts, onehot, preferred_element_type=F32)
    return got[:rows] + got[rows : 2 * rows] + got[2 * rows :]


def pick(fields, onehot, row_mask):
    total = exact_dot(fields, onehot)
    return jnp.sum(jnp.where(row_mask, total, 0.0), axis=0, keepdims=True)


def panel_masks(cell):
    onehot = (row_iota((NY, PANELS_DEV)) == (cell & (NY - 1))).astype(F32)
    row_mask = row_iota((CZ * CX, PANELS_DEV)) == (cell >> 8)
    return onehot.astype(jnp.bfloat16), row_mask


def halving(count):
    nodes, order = list(range(count)), []
    while len(nodes) > 2:
        gone = range(1, len(nodes) - 1, 2)
        order += [(nodes[i], nodes[i - 1], nodes[i + 1]) for i in gone]
        nodes = [node for i, node in enumerate(nodes) if i not in gone]
    return order


def condense(ground, edges):
    count = len(ground)
    ground = list(ground)
    edges = {(i, i + 1): edge for i, edge in enumerate(edges)}
    to_low, to_high, inverse = ([None] * (count - 2) for _ in range(3))
    for node, low, high in halving(count):
        inv = 1.0 / (ground[node] + edges[low, node] + edges[node, high])
        a, b = edges[low, node] * inv, edges[node, high] * inv
        to_low[node - 1], to_high[node - 1], inverse[node - 1] = a, b, inv
        ground[low] = ground[low] + a * ground[node]
        ground[high] = ground[high] + b * ground[node]
        edges[low, high] = edges[low, node] * b
    return ground[0], ground[-1], edges[0, count - 1], to_low, to_high, inverse


def condense_source(source, to_low, to_high, inverse):
    source = list(source)
    for node, low, high in halving(len(source)):
        source[low] = source[low] + to_low[node - 1] * source[node]
        source[high] = source[high] + to_high[node - 1] * source[node]
    offsets = [x * inv for x, inv in zip(source[1:-1], inverse)]
    return source[0], source[-1], offsets


def expand(first, last, to_low, to_high, offsets):
    values = [first] + [None] * len(offsets) + [last]
    for node, low, high in reversed(halving(len(values))):
        inflow = to_low[node - 1] * values[low] + to_high[node - 1] * values[high]
        values[node] = inflow if offsets[node - 1] is None else offsets[node - 1] + inflow
    return values


def to_row(column):
    on_diagonal = row_iota((8, LANES)) == lane_iota((8, LANES))
    return jnp.sum(jnp.where(on_diagonal, column, 0.0), axis=0, keepdims=True)


def section_rows(terms):
    return [to_row(jnp.sum(term, axis=1, keepdims=True)) for term in terms]


def sort_panels(section, rows):
    square = (PANELS_DEV, PANELS_DEV)
    key = section * PANELS_DEV + lane_iota((1, PANELS_DEV))
    key = key.astype(F32)
    on_diagonal = row_iota(square) == lane_iota(square)
    key_column = jnp.sum(jnp.where(on_diagonal, key, 0.0), axis=1, keepdims=True)
    rank = jnp.sum(jnp.where(key < key_column, 1.0, 0.0), axis=1, keepdims=True)
    order = jnp.where(lane_iota(square).astype(F32) == rank, 1.0, 0.0).astype(jnp.bfloat16)
    return exact_dot(rows, order)


def fetch_kernel(*refs):
    sources, targets = refs[:8], refs[8:13] + refs[17:20]
    other_ref, pair_ref, bound_ref, sorted_ref = refs[13:17]
    p_ref, u_ref = targets[:2]
    cell_ref, sec_ref, geom_ref = targets[5:]
    fetches = [
        pltpu.make_async_copy(source, target, refs[20].at[i])
        for i, (source, target) in enumerate(zip(sources, targets))
    ]
    for fetch in fetches[5:] + fetches[:5]:
        fetch.start()
    slab = lax.axis_index("slab")
    even = lax.rem(slab, 2) == 0
    for fetch in fetches[5:]:
        fetch.wait()
    section = sec_ref[...] - (slab * SEC_DEV - REACH)
    rows = [geom_ref[k : k + 1, :] for k in range(3)] + [cell_ref[...].astype(F32)]
    rows = jnp.concatenate(rows + [jnp.zeros((4, PANELS_DEV), F32)], 0)
    sorted_ref[...] = sort_panels(section, rows)
    at_section = row_iota((8, PANELS_DEV))
    for at, before in enumerate((section < at_section, section <= at_section)):
        count = jnp.sum(jnp.where(before, 1.0, 0.0), axis=1, keepdims=True)
        bound_ref[at * 8 : (at + 1) * 8, :] = jnp.broadcast_to(count, (8, LANES))
    for fetch in fetches[:5]:
        fetch.wait()
    for z in range(CZ):
        first, last = z * CX, (z + 1) * CX - 1
        leading = GAMMA_HORIZ * p_ref[first : first + 1, :] - HALF_DIV * u_ref[first : first + 1, :]
        trailing = GAMMA_HORIZ * p_ref[last : last + 1, :] + HALF_DIV * u_ref[last : last + 1, :]
        other_ref[z : z + 1, :] = jnp.where(even, leading, trailing)
        pair_ref[z : z + 1, :] = jnp.where(even, trailing, leading)


A_AT, B_AT, I_AT, FACE_AT, PORT_AT = 0, 6, 12, 18, 25
MAT_LEVELS = 30


def matrix_kernel(
    p_ref, u_ref, v_ref, w_ref, flags_ref, bound_ref, sorted_ref, mat_ref, src_ref, panel_ref
):
    shape = (CX, NY)
    rows, lanes = row_iota(shape), lane_iota(shape)
    densities, kappas = [], []
    for z in range(CZ):
        p, flags = level(p_ref, z), level(flags_ref, z)
        air = jnp.where(flags == 1, 1.0, jnp.where(flags == 2, 0.5, 0.0)).astype(F32)
        water = jnp.ones_like(p)
        for _ in range(EOS_ITERS):
            square = water * water
            cube = square * water
            sixth = cube * cube
            water = water - (sixth * water - 1.0 - p) / (7.0 * sixth)
        shifted = 1.0 + p
        air_density = AIR_DENSITY * jnp.exp(jnp.log(shifted) * (1.0 / 1.4))
        densities.append(air * air_density + (1.0 - air) * water)
        kappa = KAPPA_SCALE * (air / (1.4 * shifted) + (1.0 - air) / (7.0 * shifted))
        kappas.append(kappa)

        u, v = level(u_ref, z), level(v_ref, z)

        def beside(x, axis, step):
            size = shape[axis]
            moved = pltpu.roll(x, (-step) % size, axis)
            at = rows if axis == 0 else lanes
            return jnp.where(at == (size - 1 if step > 0 else 0), 0.0, moved)

        laplacian = (
            beside(p, 0, 1) + beside(p, 0, -1) + beside(p, 1, 1) + beside(p, 1, -1) - 4.0 * p
        )
        divergence = 0.5 * (beside(u, 0, 1) - beside(u, 0, -1)) + 0.5 * (
            beside(v, 1, 1) - beside(v, 1, -1)
        )
        if z == 0:
            w_difference = level(w_ref, 1)
        elif z == CZ - 1:
            w_difference = -level(w_ref, CZ - 2)
        else:
            w_difference = level(w_ref, z + 1) - level(w_ref, z - 1)
        divergence = divergence + 0.5 * w_difference
        src_ref[z * CX : (z + 1) * CX, :] = (
            kappa * p + GAMMA_HORIZ * laplacian - DIVERGENCE_SCALE * divergence
        )
    faces = [2.0 / (densities[z] + densities[z + 1]) for z in range(CZ - 1)]
    first, last, link, to_low, to_high, inverse = condense(kappas, faces)
    stored = to_low + to_high + inverse + faces + [first, last, link, densities[0], densities[-1]]
    for at, value in enumerate(stored):
        mat_ref[at * CX : (at + 1) * CX, :] = value

    zero, one = jnp.zeros(shape, F32), jnp.ones(shape, F32)
    no_offset = [None] * (CZ - 2)
    rows = sorted_ref[...]
    cell = rows[3:4, :].astype(jnp.int32)
    onehot, row_mask = panel_masks(cell)
    from_first = expand(one, zero, to_low, to_high, no_offset)
    from_last = expand(zero, one, to_low, to_high, no_offset)
    at_first = pick(jnp.concatenate(from_first, 0), onehot, row_mask)
    at_last = pick(jnp.concatenate(from_last, 0), onehot, row_mask)
    panel_rows = [rows[k : k + 1, :] * (at_first + at_last) for k in range(3)]
    panel_rows.append(at_first / (at_first + at_last))
    panel_rows.append((cell & (CX * NY - 1)).astype(F32))
    panel_ref[...] = jnp.zeros_like(panel_ref)
    for at, row in enumerate(panel_rows):
        for half in range(2):
            panel_ref[2 * at + half : 2 * at + half + 1, :] = row[
                :, half * LANES : (half + 1) * LANES
            ]
    panel_ref[META_ROW - GEOM_ROW : META_ROW - GEOM_ROW + 1, :] = to_row(bound_ref[0:8, 0:1])


def pack_kernel(
    mat_ref, src_ref, other_ref, pair_ref, w_ref, panel_ref, bound_ref, sorted_ref,
    send_ref, offset_ref,
):
    core = lax.rem(lax.axis_index("slab"), 2)
    even = core == 0
    shape = (CX, NY)
    rows = row_iota(shape)
    received, beyond = pair_ref[1 - core], other_ref[...]
    from_left = jnp.where(even, beyond, received)
    from_right = jnp.where(even, received, beyond)
    source = []
    for z in range(CZ):
        halo = jnp.where(rows == 0, from_left[z : z + 1, :], 0.0) + jnp.where(
            rows == CX - 1, from_right[z : z + 1, :], 0.0
        )
        source.append(level(src_ref, z) + halo)
    to_low = [level(mat_ref, A_AT + j) for j in range(CZ - 2)]
    to_high = [level(mat_ref, B_AT + j) for j in range(CZ - 2)]
    inverse = [level(mat_ref, I_AT + j) for j in range(CZ - 2)]
    first, last, offsets = condense_source(source, to_low, to_high, inverse)
    for j, offset in enumerate(offsets):
        offset_ref[j * CX : (j + 1) * CX, :] = offset

    zero = jnp.zeros(shape, F32)
    constant = expand(zero, zero, to_low, to_high, offsets)
    onehot, row_mask = panel_masks(sorted_ref[3:4, :].astype(jnp.int32))
    at_panel = pick(jnp.concatenate(constant, 0), onehot, row_mask)
    terms = [0.0, 0.0, 0.0]
    for half in range(2):
        lanes = slice(half * LANES, (half + 1) * LANES)
        place = (lane_iota((8, LANES)) + half * LANES).astype(F32)
        in_section = (place >= bound_ref[0:8, :]) & (place < bound_ref[8:16, :])
        for k in range(3):
            row = sorted_ref[k : k + 1, lanes] * at_panel[:, lanes]
            terms[k] = terms[k] + jnp.where(in_section, row, 0.0)
    meta = panel_ref[META_ROW - GEOM_ROW : META_ROW - GEOM_ROW + 1, :]
    for k, row in enumerate(section_rows(terms)):
        meta = meta + pltpu.roll(row, 8 * (k + 1), 1)

    for row in range(GEOM_ROW, SEND_ROWS):
        value = meta if row == META_ROW else panel_ref[row - GEOM_ROW : row - GEOM_ROW + 1, :]
        send_ref[pl.ds(row, COLS, stride=SEND_ROWS), :] = jnp.broadcast_to(value, (COLS, LANES))
    ports = [level(mat_ref, PORT_AT + j) for j in range(3)] + [first, last]
    ports += [level(mat_ref, PORT_AT + 3), level(mat_ref, PORT_AT + 4)]
    ports += [level(w_ref, 0), level(w_ref, CZ - 1)]
    for at, value in enumerate(ports):
        for half in range(2):
            row = half * 8 + at if at < 8 else 16 + half
            for group in range(0, COLS, OWNERS):
                send_ref[pl.ds(group * SEND_ROWS + row, OWNERS, stride=SEND_ROWS), :] = value[
                    :, half * LANES : (half + 1) * LANES
                ]


def solve_columns(half, recv_ref, group_ref, ends_ref, all_ref, parts_ref):
    def value(at, x):
        row = half * 8 + at if at < 8 else 16 + half
        return recv_ref[pl.ds(x * SEND_ROWS + row, 4, stride=4 * SEND_ROWS), :]

    per = [[value(at, x) for x in range(4)] for at in range(9)]
    low_k, high_k, link, low_r, high_r, low_d, high_d, low_w, high_w = per
    join = [2.0 / (high_d[x] + low_d[x + 1]) for x in range(3)]
    for x in range(3):
        high_r[x] = high_r[x] - HALF_DIV * low_w[x + 1]
        low_r[x + 1] = low_r[x + 1] + HALF_DIV * high_w[x]
    ground, source, edges = [], [], []
    for x in range(4):
        ground += [low_k[x], high_k[x]]
        source += [low_r[x], high_r[x]]
        edges += [link[x]] + ([join[x]] if x < 3 else [])
    first, last, across, to_low, to_high, inverse = condense(ground, edges)
    first_r, last_r, offsets = condense_source(source, to_low, to_high, inverse)

    stored = [first, last, across, first_r, last_r, low_d[0], high_d[3], low_w[0], high_w[3]]
    for at, x in enumerate(stored):
        group_ref[half, at * 4 : (at + 1) * 4, :] = x
    per = [[group_ref[half, at * 4 + z : at * 4 + z + 1, :] for z in range(4)] for at in range(9)]
    low_k, high_k, link, low_r, high_r, low_d, high_d, low_w, high_w = per
    outer = [2.0 / (high_d[z] + low_d[z + 1]) for z in range(3)]
    for z in range(3):
        high_r[z] = high_r[z] - HALF_DIV * low_w[z + 1]
        low_r[z + 1] = low_r[z + 1] + HALF_DIV * high_w[z]
    ground, source, edges = [], [], []
    for z in range(4):
        ground += [low_k[z], high_k[z]]
        source += [low_r[z], high_r[z]]
        edges += [link[z]] + ([outer[z]] if z < 3 else [])
    k_a, k_b, f_ab, *factors = condense(ground, edges)
    r_a, r_b, outer_offsets = condense_source(source, *factors)
    scale = 1.0 / (k_a * k_b + f_ab * (k_a + k_b))
    p_a = ((k_b + f_ab) * r_a + f_ab * r_b) * scale
    p_b = ((k_a + f_ab) * r_b + f_ab * r_a) * scale
    nodes = expand(p_a, p_b, *factors[:2], outer_offsets)
    zero_row = jnp.zeros((1, LANES), F32)
    flux = [outer[z] * (nodes[2 * z + 2] - nodes[2 * z + 1]) for z in range(3)]
    for z in range(4):
        ends_ref[half, z : z + 1, :] = nodes[2 * z]
        ends_ref[half, 4 + z : 5 + z, :] = nodes[2 * z + 1]
        ends_ref[half, 8 + z : 9 + z, :] = flux[z - 1] if z > 0 else zero_row
        ends_ref[half, 12 + z : 13 + z, :] = flux[z] if z < 3 else zero_row

    nodes = expand(ends_ref[half, 0:4, :], ends_ref[half, 4:8, :], to_low, to_high, offsets)
    inner = [join[x] * (nodes[2 * x + 2] - nodes[2 * x + 1]) for x in range(3)]
    below = [ends_ref[half, 8:12, :]] + inner
    above = inner + [ends_ref[half, 12:16, :]]

    def put(ref, rows, at, x, what):
        ref[pl.ds(x * rows + at, 4, stride=4 * rows), :] = what

    for x in range(4):
        for at, what in enumerate([nodes[2 * x], nodes[2 * x + 1], below[x], above[x]]):
            put(all_ref, BACK_ROWS, half * 4 + at, x, what)
        for end in range(2):
            for at, part in enumerate(split_three(nodes[2 * x + end])):
                put(parts_ref, 16, half * 8 + 3 * end + at, x, part.astype(F32))
            put(parts_ref, 16, half * 8 + 6 + end, x, jnp.zeros((4, LANES), F32))


def owner_kernel(
    recv_ref, back_ref, group_ref, ends_ref, all_ref, parts_ref, place_ref, picked_ref
):
    for half in range(2):
        solve_columns(half, recv_ref, group_ref, ends_ref, all_ref, parts_ref)

    column_device = lax.axis_index("col")
    mine = lax.rem(column_device, OWNERS) * NY

    def panel(row):
        return recv_ref[pl.ds(row, COLS, stride=SEND_ROWS), :]

    inside, upper = [], []
    for half in range(2):
        place = panel(COLUMN_ROW + half).astype(jnp.int32) - mine
        inside.append((place >= 0) & (place < NY))
        upper.append(place >= LANES)
        place_ref[half * COLS : (half + 1) * COLS, :] = (place & (LANES - 1)).astype(F32)
    want = row_iota((LANES, LANES)).astype(F32).astype(jnp.bfloat16)
    for block in range(COLS):
        ends = parts_ref[block * 16 : (block + 1) * 16, :].astype(jnp.bfloat16)
        onehots = []
        for half in range(2):
            at = half * COLS + block
            place = place_ref[at : at + 1, :].astype(jnp.bfloat16)
            onehots.append(jnp.where(want == place, jnp.bfloat16(1.0), jnp.bfloat16(0.0)))
        got = jnp.dot(ends, jnp.concatenate(onehots, 1), preferred_element_type=F32)
        for half in range(2):
            at = half * COLS + block
            picked_ref[at * 16 : (at + 1) * 16, :] = got[:, half * LANES : (half + 1) * LANES]
    meta = panel(META_ROW)
    starts = [meta[:, j : j + 1] for j in range(8)] + [float(PANELS_DEV)]
    sums = [[None] * 8 for _ in range(3)]
    for half in range(2):

        def got(at):
            return picked_ref[pl.ds(half * COLS * 16 + at, COLS, stride=16), :]

        low = [got(8 * h) + got(8 * h + 1) + got(8 * h + 2) for h in range(2)]
        high = [got(8 * h + 3) + got(8 * h + 4) + got(8 * h + 5) for h in range(2)]
        low = jnp.where(upper[half], low[1], low[0])
        high = jnp.where(upper[half], high[1], high[0])
        at_panel = high + panel(SHARE_ROW + half) * (low - high)
        at_panel = jnp.where(inside[half], at_panel, 0.0)
        place = (lane_iota((COLS, LANES)) + half * LANES).astype(F32)
        reached = [place >= start for start in starts]
        terms = [panel(GEOM_ROW + 2 * k + half) * at_panel for k in range(3)]
        for j in range(8):
            in_section = reached[j] & jnp.logical_not(reached[j + 1])
            for k in range(3):
                part = jnp.where(in_section, terms[k], 0.0)
                part = part[0:8, :] + part[8:16, :]
                sums[k][j] = part if half == 0 else sums[k][j] + part
    terms = [
        jnp.concatenate([jnp.sum(x, axis=0, keepdims=True) for x in sums[k]], 0)
        for k in range(3)
    ]
    constant = jnp.sum(meta, axis=0, keepdims=True)
    lanes = lane_iota((1, LANES))
    own = lax.rem(column_device, OWNERS) == 0
    rows = section_rows(terms)
    for k in range(3):
        moved = pltpu.roll(constant, LANES - 8 * (k + 1), 1)
        rows[k] = rows[k] + jnp.where((lanes < 8) & own, moved, 0.0)
    packed = sum(pltpu.roll(row, 8 * k, 1) for k, row in enumerate(rows))
    all_ref[pl.ds(8, COLS, stride=BACK_ROWS), :] = jnp.broadcast_to(packed, (COLS, LANES))
    mine = pl.multiple_of((column_device // OWNERS) * (OWNERS * BACK_ROWS), OWNERS * BACK_ROWS)
    back_ref[...] = all_ref[pl.ds(mine, OWNERS * BACK_ROWS), :]


def load_kernel(back_ref, load_ref):
    packed = back_ref[pl.ds(8, OWNERS, stride=BACK_ROWS), :]
    load_ref[...] = jnp.sum(packed, axis=0, keepdims=True)


def final_kernel(
    back_ref, mat_ref, offset_ref, w_ref, load_ref, pair_ref, other_ref,
    pressure_ref, velocity_ref, out_ref,
):
    def end(at):
        halves = [back_ref[pl.ds(half * 4 + at, CX, stride=BACK_ROWS), :] for half in range(2)]
        return jnp.concatenate(halves, axis=1)

    to_low = [level(mat_ref, A_AT + j) for j in range(CZ - 2)]
    to_high = [level(mat_ref, B_AT + j) for j in range(CZ - 2)]
    offsets = [level(offset_ref, j) for j in range(CZ - 2)]
    pressure = expand(end(0), end(1), to_low, to_high, offsets)
    flux = [end(2)]
    for z in range(CZ - 1):
        flux.append(level(mat_ref, FACE_AT + z) * (pressure[z + 1] - pressure[z]))
    flux.append(end(3))
    for z in range(CZ):
        pressure_ref[z * CX : (z + 1) * CX, :] = pressure[z]
        velocity_ref[z * CX : (z + 1) * CX, :] = level(w_ref, z) - 0.5 * (flux[z + 1] + flux[z])

    core = lax.rem(lax.axis_index("slab"), 2)
    even = core == 0
    received, beyond = pair_ref[1 - core], other_ref[...]
    from_left = jnp.where(even, beyond, received)
    from_right = jnp.where(even, received, beyond)
    lower = (lane_iota((1, LANES)) & 7) < 4
    total = load_ref[...] + jnp.where(
        lower, pltpu.roll(from_left, LANES - 4, 1), pltpu.roll(from_right, 4, 1)
    )
    for k in range(3):
        moved = pltpu.roll(total, LANES - 8 * k - REACH, 1)
        out_ref[k : k + 1, :] = moved[:, 0:SEC_DEV]


def call(kernel, outs, scratch=(), flops=20000):
    shapes = [jax.ShapeDtypeStruct(shape, F32) for shape in outs]
    return pl.pallas_call(
        kernel,
        out_shape=shapes if len(shapes) > 1 else shapes[0],
        scratch_shapes=[pltpu.VMEM(shape, F32) for shape in scratch],
        compiler_params=pltpu.CompilerParams(vmem_limit_bytes=16 * 1024 * 1024),
        cost_estimate=pl.CostEstimate(flops=flops, bytes_accessed=500000, transcendentals=0),
    )


def exchange(x, parts, groups=None):
    rows, lanes = x.shape
    x = x.reshape(parts, 1, rows // parts * lanes)
    x = lax.all_to_all(x, "col", 0, 0, axis_index_groups=groups, tiled=True)
    return x.reshape(rows, lanes)


def per_device(p_star, u_star, v_star, w_star, flags, panel_cell, panel_section, panel_geom):
    flat = (CZ * CX, NY)
    p, u, v, w = (x.reshape(flat) for x in (p_star, u_star, v_star, w_star))
    flags = flags.reshape(flat)
    cell = panel_cell.reshape(1, PANELS_DEV)
    section = panel_section.reshape(1, PANELS_DEV)
    slabs = lax.axis_size("slab")
    cores = [[i, i + 1] for i in range(0, slabs, 2)]
    others = [(i, i + 1) for i in range(1, slabs - 1, 2)]
    others += [(j, i) for i, j in others]

    inputs = [p, u, v, w, flags, cell, section, panel_geom]
    shapes = [(CZ, NY), (CZ, NY), (16, LANES), (8, PANELS_DEV)]
    p, u, v, w, flags, to_other, to_pair, bounds, ordered = pl.pallas_call(
        fetch_kernel,
        out_shape=[jax.ShapeDtypeStruct(x.shape, x.dtype) for x in inputs[:5]]
        + [jax.ShapeDtypeStruct(shape, F32) for shape in shapes],
        in_specs=[pl.BlockSpec(memory_space=pltpu.HBM)] * 8,
        scratch_shapes=[pltpu.VMEM(x.shape, x.dtype) for x in inputs[5:]]
        + [pltpu.SemaphoreType.DMA((8,))],
        compiler_params=pltpu.CompilerParams(vmem_limit_bytes=16 * 1024 * 1024),
        cost_estimate=pl.CostEstimate(flops=20000, bytes_accessed=500000, transcendentals=0),
    )(*[pltpu.with_memory_space_constraint(x, pltpu.HBM) for x in inputs])
    from_other = lax.ppermute(to_other, "slab", others)
    from_pair = lax.all_gather(to_pair, "slab", axis_index_groups=cores)
    mat, source, panel = call(
        matrix_kernel, [(MAT_LEVELS * CX, NY), flat, (16, LANES)], flops=5000000
    )(p, u, v, w, flags, bounds, ordered)
    send, offsets = call(pack_kernel, [(COLS * SEND_ROWS, LANES), ((CZ - 2) * CX, NY)])(
        mat, source, from_other, from_pair, w, panel, bounds, ordered
    )
    recv = exchange(send, COLS)
    back = call(
        owner_kernel,
        [(OWNERS * BACK_ROWS, LANES)],
        [
            (2, 40, LANES),
            (2, 16, LANES),
            (COLS * BACK_ROWS, LANES),
            (COLS * 16, LANES),
            (2 * COLS, LANES),
            (2 * COLS * 16, LANES),
        ],
    )(recv)
    sets = [list(range(at, at + OWNERS)) for at in range(0, COLS, OWNERS)]
    back = exchange(back, OWNERS, sets)
    loads = call(load_kernel, [(1, LANES)])(back)
    loads_other = lax.ppermute(loads, "slab", others)
    loads_pair = lax.all_gather(loads, "slab", axis_index_groups=cores)
    pressure, velocity, section_loads = call(final_kernel, [flat, flat, (3, SEC_DEV)])(
        back, mat, offsets, w, loads, loads_pair, loads_other
    )
    return pressure.reshape(p_star.shape), velocity.reshape(p_star.shape), section_loads


def solution(mesh):
    in_specs = (
        P("col", "slab", None),
        P("col", "slab", None),
        P("col", "slab", None),
        P("col", "slab", None),
        P("col", "slab", None),
        P(("col", "slab")),
        P(("col", "slab")),
        P(None, ("col", "slab")),
    )
    out_specs = (P("col", "slab", None), P("col", "slab", None), P(None, "slab"))
    return jax.shard_map(
        per_device, mesh=mesh, in_specs=in_specs, out_specs=out_specs, check_vma=False
    )
```

```python
import functools

import jax
import jax.numpy as jnp
from jax import lax
from jax.experimental import pallas as pl
from jax.experimental.pallas import tpu as pltpu
from jax.sharding import PartitionSpec as P

SEC_DEV = 4
EOS_ITERS = 3
KAPPA_SCALE = 0.01
AIR_DENSITY = 0.1
GAMMA_HORIZ = 0.001
DIVERGENCE_SCALE = 0.005
HALF_DIV = 0.5 * DIVERGENCE_SCALE

CZ = 8
CX = 8
NY = 256
LANES = 128
COLS = 16
PANELS_DEV = 256
REACH = 2
OWNERS = 8
SEND_ROWS = 29
BACK_ROWS = 9
GEOM_ROW, SHARE_ROW, COLUMN_ROW, META_ROW = 18, 24, 26, 28

F32 = jnp.float32


def row_iota(shape):
    return lax.broadcasted_iota(jnp.int32, shape, 0)


def lane_iota(shape):
    return lax.broadcasted_iota(jnp.int32, shape, 1)


def level(ref, z):
    return ref[z * CX : (z + 1) * CX, :]


def split_three(x):
    high = x.astype(jnp.bfloat16)
    rest = x - high.astype(F32)
    middle = rest.astype(jnp.bfloat16)
    low = (rest - middle.astype(F32)).astype(jnp.bfloat16)
    return high, middle, low


def exact_dot(x, onehot):
    rows = x.shape[0]
    parts = split_three(x)
    if rows % 16:
        parts = [part.astype(F32) for part in parts]
    parts = jnp.concatenate(parts, 0).astype(jnp.bfloat16)
    got = jnp.dot(parts, onehot, preferred_element_type=F32)
    return got[:rows] + got[rows : 2 * rows] + got[2 * rows :]


def pick(fields, onehot, row_mask):
    total = exact_dot(fields, onehot)
    return jnp.sum(jnp.where(row_mask, total, 0.0), axis=0, keepdims=True)


def panel_masks(cell):
    onehot = (row_iota((NY, PANELS_DEV)) == (cell & (NY - 1))).astype(F32)
    row_mask = row_iota((CZ * CX, PANELS_DEV)) == (cell >> 8)
    return onehot.astype(jnp.bfloat16), row_mask


def halving(count):
    nodes, order = list(range(count)), []
    while len(nodes) > 2:
        gone = range(1, len(nodes) - 1, 2)
        order += [(nodes[i], nodes[i - 1], nodes[i + 1]) for i in gone]
        nodes = [node for i, node in enumerate(nodes) if i not in gone]
    return order


def condense(ground, edges):
    count = len(ground)
    ground = list(ground)
    edges = {(i, i + 1): edge for i, edge in enumerate(edges)}
    to_low, to_high, inverse = ([None] * (count - 2) for _ in range(3))
    for node, low, high in halving(count):
        inv = 1.0 / (ground[node] + edges[low, node] + edges[node, high])
        a, b = edges[low, node] * inv, edges[node, high] * inv
        to_low[node - 1], to_high[node - 1], inverse[node - 1] = a, b, inv
        ground[low] = ground[low] + a * ground[node]
        ground[high] = ground[high] + b * ground[node]
        edges[low, high] = edges[low, node] * b
    return ground[0], ground[-1], edges[0, count - 1], to_low, to_high, inverse


def condense_source(source, to_low, to_high, inverse):
    source = list(source)
    for node, low, high in halving(len(source)):
        source[low] = source[low] + to_low[node - 1] * source[node]
        source[high] = source[high] + to_high[node - 1] * source[node]
    offsets = [x * inv for x, inv in zip(source[1:-1], inverse)]
    return source[0], source[-1], offsets


def expand(first, last, to_low, to_high, offsets):
    values = [first] + [None] * len(offsets) + [last]
    for node, low, high in reversed(halving(len(values))):
        inflow = to_low[node - 1] * values[low] + to_high[node - 1] * values[high]
        values[node] = inflow if offsets[node - 1] is None else offsets[node - 1] + inflow
    return values


def to_row(column):
    on_diagonal = row_iota((8, LANES)) == lane_iota((8, LANES))
    return jnp.sum(jnp.where(on_diagonal, column, 0.0), axis=0, keepdims=True)


def section_rows(terms):
    return [to_row(jnp.sum(term, axis=1, keepdims=True)) for term in terms]


def sort_panels(section, rows):
    square = (PANELS_DEV, PANELS_DEV)
    key = section * PANELS_DEV + lane_iota((1, PANELS_DEV))
    key = key.astype(F32)
    on_diagonal = row_iota(square) == lane_iota(square)
    key_column = jnp.sum(jnp.where(on_diagonal, key, 0.0), axis=1, keepdims=True)
    rank = jnp.sum(jnp.where(key < key_column, 1.0, 0.0), axis=1, keepdims=True)
    order = jnp.where(lane_iota(square).astype(F32) == rank, 1.0, 0.0).astype(jnp.bfloat16)
    return exact_dot(rows, order)


def fetch_kernel(*refs):
    sources, targets = refs[:8], refs[8:13] + refs[17:20]
    other_ref, pair_ref, bound_ref, sorted_ref = refs[13:17]
    p_ref, u_ref = targets[:2]
    cell_ref, sec_ref, geom_ref = targets[5:]
    fetches = [
        pltpu.make_async_copy(source, target, refs[20].at[i])
        for i, (source, target) in enumerate(zip(sources, targets))
    ]
    for fetch in fetches[5:] + fetches[:5]:
        fetch.start()
    slab = lax.axis_index("slab")
    even = lax.rem(slab, 2) == 0
    for fetch in fetches[5:]:
        fetch.wait()
    section = sec_ref[...] - (slab * SEC_DEV - REACH)
    rows = [geom_ref[k : k + 1, :] for k in range(3)] + [cell_ref[...].astype(F32)]
    rows = jnp.concatenate(rows + [jnp.zeros((4, PANELS_DEV), F32)], 0)
    sorted_ref[...] = sort_panels(section, rows)
    at_section = row_iota((8, PANELS_DEV))
    for at, before in enumerate((section < at_section, section <= at_section)):
        count = jnp.sum(jnp.where(before, 1.0, 0.0), axis=1, keepdims=True)
        bound_ref[at * 8 : (at + 1) * 8, :] = jnp.broadcast_to(count, (8, LANES))
    for fetch in fetches[:5]:
        fetch.wait()
    for z in range(CZ):
        first, last = z * CX, (z + 1) * CX - 1
        leading = GAMMA_HORIZ * p_ref[first : first + 1, :] - HALF_DIV * u_ref[first : first + 1, :]
        trailing = GAMMA_HORIZ * p_ref[last : last + 1, :] + HALF_DIV * u_ref[last : last + 1, :]
        other_ref[z : z + 1, :] = jnp.where(even, leading, trailing)
        pair_ref[z : z + 1, :] = jnp.where(even, trailing, leading)


A_AT, B_AT, I_AT, FACE_AT, PORT_AT = 0, 6, 12, 18, 25
MAT_LEVELS = 30


def matrix_kernel(
    p_ref, u_ref, v_ref, w_ref, flags_ref, bound_ref, sorted_ref, mat_ref, src_ref, panel_ref
):
    shape = (CX, NY)
    rows, lanes = row_iota(shape), lane_iota(shape)
    densities, kappas = [], []
    for z in range(CZ):
        p, flags = level(p_ref, z), level(flags_ref, z)
        air = jnp.where(flags == 1, 1.0, jnp.where(flags == 2, 0.5, 0.0)).astype(F32)
        water = jnp.ones_like(p)
        for _ in range(EOS_ITERS):
            square = water * water
            cube = square * water
            sixth = cube * cube
            water = water - (sixth * water - 1.0 - p) / (7.0 * sixth)
        shifted = 1.0 + p
        air_density = AIR_DENSITY * jnp.exp(jnp.log(shifted) * (1.0 / 1.4))
        densities.append(air * air_density + (1.0 - air) * water)
        kappa = KAPPA_SCALE * (air / (1.4 * shifted) + (1.0 - air) / (7.0 * shifted))
        kappas.append(kappa)

        u, v = level(u_ref, z), level(v_ref, z)

        def beside(x, axis, step):
            size = shape[axis]
            moved = pltpu.roll(x, (-step) % size, axis)
            at = rows if axis == 0 else lanes
            return jnp.where(at == (size - 1 if step > 0 else 0), 0.0, moved)

        laplacian = (
            beside(p, 0, 1) + beside(p, 0, -1) + beside(p, 1, 1) + beside(p, 1, -1) - 4.0 * p
        )
        divergence = 0.5 * (beside(u, 0, 1) - beside(u, 0, -1)) + 0.5 * (
            beside(v, 1, 1) - beside(v, 1, -1)
        )
        if z == 0:
            w_difference = level(w_ref, 1)
        elif z == CZ - 1:
            w_difference = -level(w_ref, CZ - 2)
        else:
            w_difference = level(w_ref, z + 1) - level(w_ref, z - 1)
        divergence = divergence + 0.5 * w_difference
        src_ref[z * CX : (z + 1) * CX, :] = (
            kappa * p + GAMMA_HORIZ * laplacian - DIVERGENCE_SCALE * divergence
        )
    faces = [2.0 / (densities[z] + densities[z + 1]) for z in range(CZ - 1)]
    first, last, link, to_low, to_high, inverse = condense(kappas, faces)
    stored = to_low + to_high + inverse + faces + [first, last, link, densities[0], densities[-1]]
    for at, value in enumerate(stored):
        mat_ref[at * CX : (at + 1) * CX, :] = value

    zero, one = jnp.zeros(shape, F32), jnp.ones(shape, F32)
    no_offset = [None] * (CZ - 2)
    rows = sorted_ref[...]
    cell = rows[3:4, :].astype(jnp.int32)
    onehot, row_mask = panel_masks(cell)
    from_first = expand(one, zero, to_low, to_high, no_offset)
    from_last = expand(zero, one, to_low, to_high, no_offset)
    at_first = pick(jnp.concatenate(from_first, 0), onehot, row_mask)
    at_last = pick(jnp.concatenate(from_last, 0), onehot, row_mask)
    panel_rows = [rows[k : k + 1, :] * (at_first + at_last) for k in range(3)]
    panel_rows.append(at_first / (at_first + at_last))
    panel_rows.append((cell & (CX * NY - 1)).astype(F32))
    panel_ref[...] = jnp.zeros_like(panel_ref)
    for at, row in enumerate(panel_rows):
        for half in range(2):
            panel_ref[2 * at + half : 2 * at + half + 1, :] = row[
                :, half * LANES : (half + 1) * LANES
            ]
    panel_ref[META_ROW - GEOM_ROW : META_ROW - GEOM_ROW + 1, :] = to_row(bound_ref[0:8, 0:1])


def pack_kernel(
    mat_ref, src_ref, other_ref, pair_ref, w_ref, panel_ref, bound_ref, sorted_ref,
    send_ref, offset_ref,
):
    core = lax.rem(lax.axis_index("slab"), 2)
    even = core == 0
    shape = (CX, NY)
    rows = row_iota(shape)
    received, beyond = pair_ref[1 - core], other_ref[...]
    from_left = jnp.where(even, beyond, received)
    from_right = jnp.where(even, received, beyond)
    source = []
    for z in range(CZ):
        halo = jnp.where(rows == 0, from_left[z : z + 1, :], 0.0) + jnp.where(
            rows == CX - 1, from_right[z : z + 1, :], 0.0
        )
        source.append(level(src_ref, z) + halo)
    to_low = [level(mat_ref, A_AT + j) for j in range(CZ - 2)]
    to_high = [level(mat_ref, B_AT + j) for j in range(CZ - 2)]
    inverse = [level(mat_ref, I_AT + j) for j in range(CZ - 2)]
    first, last, offsets = condense_source(source, to_low, to_high, inverse)
    for j, offset in enumerate(offsets):
        offset_ref[j * CX : (j + 1) * CX, :] = offset

    zero = jnp.zeros(shape, F32)
    constant = expand(zero, zero, to_low, to_high, offsets)
    onehot, row_mask = panel_masks(sorted_ref[3:4, :].astype(jnp.int32))
    at_panel = pick(jnp.concatenate(constant, 0), onehot, row_mask)
    terms = [0.0, 0.0, 0.0]
    for half in range(2):
        lanes = slice(half * LANES, (half + 1) * LANES)
        place = (lane_iota((8, LANES)) + half * LANES).astype(F32)
        in_section = (place >= bound_ref[0:8, :]) & (place < bound_ref[8:16, :])
        for k in range(3):
            row = sorted_ref[k : k + 1, lanes] * at_panel[:, lanes]
            terms[k] = terms[k] + jnp.where(in_section, row, 0.0)
    meta = panel_ref[META_ROW - GEOM_ROW : META_ROW - GEOM_ROW + 1, :]
    for k, row in enumerate(section_rows(terms)):
        meta = meta + pltpu.roll(row, 8 * (k + 1), 1)

    for row in range(GEOM_ROW, SEND_ROWS):
        value = meta if row == META_ROW else panel_ref[row - GEOM_ROW : row - GEOM_ROW + 1, :]
        send_ref[pl.ds(row, COLS, stride=SEND_ROWS), :] = jnp.broadcast_to(value, (COLS, LANES))
    ports = [level(mat_ref, PORT_AT + j) for j in range(3)] + [first, last]
    ports += [level(mat_ref, PORT_AT + 3), level(mat_ref, PORT_AT + 4)]
    ports += [level(w_ref, 0), level(w_ref, CZ - 1)]
    for at, value in enumerate(ports):
        for half in range(2):
            row = half * 8 + at if at < 8 else 16 + half
            for group in range(0, COLS, OWNERS):
                send_ref[pl.ds(group * SEND_ROWS + row, OWNERS, stride=SEND_ROWS), :] = value[
                    :, half * LANES : (half + 1) * LANES
                ]


def solve_columns(half, recv_ref, group_ref, ends_ref, all_ref, parts_ref):
    def value(at, x):
        row = half * 8 + at if at < 8 else 16 + half
        return recv_ref[pl.ds(x * SEND_ROWS + row, 4, stride=4 * SEND_ROWS), :]

    per = [[value(at, x) for x in range(4)] for at in range(9)]
    low_k, high_k, link, low_r, high_r, low_d, high_d, low_w, high_w = per
    join = [2.0 / (high_d[x] + low_d[x + 1]) for x in range(3)]
    for x in range(3):
        high_r[x] = high_r[x] - HALF_DIV * low_w[x + 1]
        low_r[x + 1] = low_r[x + 1] + HALF_DIV * high_w[x]
    ground, source, edges = [], [], []
    for x in range(4):
        ground += [low_k[x], high_k[x]]
        source += [low_r[x], high_r[x]]
        edges += [link[x]] + ([join[x]] if x < 3 else [])
    first, last, across, to_low, to_high, inverse = condense(ground, edges)
    first_r, last_r, offsets = condense_source(source, to_low, to_high, inverse)

    stored = [first, last, across, first_r, last_r, low_d[0], high_d[3], low_w[0], high_w[3]]
    for at, x in enumerate(stored):
        group_ref[half, at * 4 : (at + 1) * 4, :] = x
    per = [[group_ref[half, at * 4 + z : at * 4 + z + 1, :] for z in range(4)] for at in range(9)]
    low_k, high_k, link, low_r, high_r, low_d, high_d, low_w, high_w = per
    outer = [2.0 / (high_d[z] + low_d[z + 1]) for z in range(3)]
    for z in range(3):
        high_r[z] = high_r[z] - HALF_DIV * low_w[z + 1]
        low_r[z + 1] = low_r[z + 1] + HALF_DIV * high_w[z]
    ground, source, edges = [], [], []
    for z in range(4):
        ground += [low_k[z], high_k[z]]
        source += [low_r[z], high_r[z]]
        edges += [link[z]] + ([outer[z]] if z < 3 else [])
    k_a, k_b, f_ab, *factors = condense(ground, edges)
    r_a, r_b, outer_offsets = condense_source(source, *factors)
    scale = 1.0 / (k_a * k_b + f_ab * (k_a + k_b))
    p_a = ((k_b + f_ab) * r_a + f_ab * r_b) * scale
    p_b = ((k_a + f_ab) * r_b + f_ab * r_a) * scale
    nodes = expand(p_a, p_b, *factors[:2], outer_offsets)
    zero_row = jnp.zeros((1, LANES), F32)
    flux = [outer[z] * (nodes[2 * z + 2] - nodes[2 * z + 1]) for z in range(3)]
    for z in range(4):
        ends_ref[half, z : z + 1, :] = nodes[2 * z]
        ends_ref[half, 4 + z : 5 + z, :] = nodes[2 * z + 1]
        ends_ref[half, 8 + z : 9 + z, :] = flux[z - 1] if z > 0 else zero_row
        ends_ref[half, 12 + z : 13 + z, :] = flux[z] if z < 3 else zero_row

    nodes = expand(ends_ref[half, 0:4, :], ends_ref[half, 4:8, :], to_low, to_high, offsets)
    inner = [join[x] * (nodes[2 * x + 2] - nodes[2 * x + 1]) for x in range(3)]
    below = [ends_ref[half, 8:12, :]] + inner
    above = inner + [ends_ref[half, 12:16, :]]

    def put(ref, rows, at, x, what):
        ref[pl.ds(x * rows + at, 4, stride=4 * rows), :] = what

    for x in range(4):
        for at, what in enumerate([nodes[2 * x], nodes[2 * x + 1], below[x], above[x]]):
            put(all_ref, BACK_ROWS, half * 4 + at, x, what)
        for end in range(2):
            for at, part in enumerate(split_three(nodes[2 * x + end])):
                put(parts_ref, 16, half * 8 + 3 * end + at, x, part.astype(F32))


def owner_kernel(
    recv_ref, back_ref, group_ref, ends_ref, all_ref, parts_ref, place_ref, picked_ref
):
    for half in range(2):
        solve_columns(half, recv_ref, group_ref, ends_ref, all_ref, parts_ref)

    column_device = lax.axis_index("col")
    mine = lax.rem(column_device, OWNERS) * NY

    def panel(row):
        return recv_ref[pl.ds(row, COLS, stride=SEND_ROWS), :]

    inside, upper = [], []
    for half in range(2):
        place = panel(COLUMN_ROW + half).astype(jnp.int32) - mine
        inside.append((place >= 0) & (place < NY))
        upper.append(place >= LANES)
        place_ref[half * COLS : (half + 1) * COLS, :] = (place & (LANES - 1)).astype(F32)
    want = row_iota((LANES, LANES)).astype(F32).astype(jnp.bfloat16)
    for block in range(COLS):
        ends = parts_ref[block * 16 : (block + 1) * 16, :].astype(jnp.bfloat16)
        onehots = []
        for half in range(2):
            at = half * COLS + block
            place = place_ref[at : at + 1, :].astype(jnp.bfloat16)
            onehots.append(jnp.where(want == place, jnp.bfloat16(1.0), jnp.bfloat16(0.0)))
        got = jnp.dot(ends, jnp.concatenate(onehots, 1), preferred_element_type=F32)
        for half in range(2):
            at = half * COLS + block
            picked_ref[at * 16 : (at + 1) * 16, :] = got[:, half * LANES : (half + 1) * LANES]
    meta = panel(META_ROW)
    starts = [meta[:, j : j + 1] for j in range(8)] + [float(PANELS_DEV)]
    sums = [[None] * 8 for _ in range(3)]
    for half in range(2):

        def got(at):
            return picked_ref[pl.ds(half * COLS * 16 + at, COLS, stride=16), :]

        low = [got(8 * h) + got(8 * h + 1) + got(8 * h + 2) for h in range(2)]
        high = [got(8 * h + 3) + got(8 * h + 4) + got(8 * h + 5) for h in range(2)]
        low = jnp.where(upper[half], low[1], low[0])
        high = jnp.where(upper[half], high[1], high[0])
        at_panel = high + panel(SHARE_ROW + half) * (low - high)
        at_panel = jnp.where(inside[half], at_panel, 0.0)
        place = (lane_iota((COLS, LANES)) + half * LANES).astype(F32)
        reached = [place >= start for start in starts]
        terms = [panel(GEOM_ROW + 2 * k + half) * at_panel for k in range(3)]
        for j in range(8):
            in_section = reached[j] & jnp.logical_not(reached[j + 1])
            for k in range(3):
                part = jnp.where(in_section, terms[k], 0.0)
                part = part[0:8, :] + part[8:16, :]
                sums[k][j] = part if half == 0 else sums[k][j] + part
    terms = [
        jnp.concatenate([jnp.sum(x, axis=0, keepdims=True) for x in sums[k]], 0)
        for k in range(3)
    ]
    constant = jnp.sum(meta, axis=0, keepdims=True)
    lanes = lane_iota((1, LANES))
    own = lax.rem(column_device, OWNERS) == 0
    rows = section_rows(terms)
    for k in range(3):
        moved = pltpu.roll(constant, LANES - 8 * (k + 1), 1)
        rows[k] = rows[k] + jnp.where((lanes < 8) & own, moved, 0.0)
    packed = sum(pltpu.roll(row, 8 * k, 1) for k, row in enumerate(rows))
    all_ref[pl.ds(8, COLS, stride=BACK_ROWS), :] = jnp.broadcast_to(packed, (COLS, LANES))
    mine = pl.multiple_of((column_device // OWNERS) * (OWNERS * BACK_ROWS), OWNERS * BACK_ROWS)
    back_ref[...] = all_ref[pl.ds(mine, OWNERS * BACK_ROWS), :]


def load_kernel(back_ref, load_ref):
    packed = back_ref[pl.ds(8, OWNERS, stride=BACK_ROWS), :]
    load_ref[...] = jnp.sum(packed, axis=0, keepdims=True)


def final_kernel(
    back_ref, mat_ref, offset_ref, w_ref, load_ref, pair_ref, other_ref,
    pressure_ref, velocity_ref, out_ref,
):
    def end(at):
        halves = [back_ref[pl.ds(half * 4 + at, CX, stride=BACK_ROWS), :] for half in range(2)]
        return jnp.concatenate(halves, axis=1)

    to_low = [level(mat_ref, A_AT + j) for j in range(CZ - 2)]
    to_high = [level(mat_ref, B_AT + j) for j in range(CZ - 2)]
    offsets = [level(offset_ref, j) for j in range(CZ - 2)]
    pressure = expand(end(0), end(1), to_low, to_high, offsets)
    flux = [end(2)]
    for z in range(CZ - 1):
        flux.append(level(mat_ref, FACE_AT + z) * (pressure[z + 1] - pressure[z]))
    flux.append(end(3))
    for z in range(CZ):
        pressure_ref[z * CX : (z + 1) * CX, :] = pressure[z]
        velocity_ref[z * CX : (z + 1) * CX, :] = level(w_ref, z) - 0.5 * (flux[z + 1] + flux[z])

    core = lax.rem(lax.axis_index("slab"), 2)
    even = core == 0
    received, beyond = pair_ref[1 - core], other_ref[...]
    from_left = jnp.where(even, beyond, received)
    from_right = jnp.where(even, received, beyond)
    lower = (lane_iota((1, LANES)) & 7) < 4
    total = load_ref[...] + jnp.where(
        lower, pltpu.roll(from_left, LANES - 4, 1), pltpu.roll(from_right, 4, 1)
    )
    for k in range(3):
        moved = pltpu.roll(total, LANES - 8 * k - REACH, 1)
        out_ref[k : k + 1, :] = moved[:, 0:SEC_DEV]


def call(kernel, outs, scratch=(), flops=20000):
    shapes = [jax.ShapeDtypeStruct(shape, F32) for shape in outs]
    return pl.pallas_call(
        kernel,
        out_shape=shapes if len(shapes) > 1 else shapes[0],
        scratch_shapes=[pltpu.VMEM(shape, F32) for shape in scratch],
        compiler_params=pltpu.CompilerParams(vmem_limit_bytes=16 * 1024 * 1024),
        cost_estimate=pl.CostEstimate(flops=flops, bytes_accessed=500000, transcendentals=0),
    )


def exchange(x, parts, groups=None):
    rows, lanes = x.shape
    x = x.reshape(parts, 1, rows // parts * lanes)
    x = lax.all_to_all(x, "col", 0, 0, axis_index_groups=groups, tiled=True)
    return x.reshape(rows, lanes)


def per_device(p_star, u_star, v_star, w_star, flags, panel_cell, panel_section, panel_geom):
    flat = (CZ * CX, NY)
    p, u, v, w = (x.reshape(flat) for x in (p_star, u_star, v_star, w_star))
    flags = flags.reshape(flat)
    cell = panel_cell.reshape(1, PANELS_DEV)
    section = panel_section.reshape(1, PANELS_DEV)
    slabs = lax.axis_size("slab")
    cores = [[i, i + 1] for i in range(0, slabs, 2)]
    others = [(i, i + 1) for i in range(1, slabs - 1, 2)]
    others += [(j, i) for i, j in others]

    inputs = [p, u, v, w, flags, cell, section, panel_geom]
    shapes = [(CZ, NY), (CZ, NY), (16, LANES), (8, PANELS_DEV)]
    p, u, v, w, flags, to_other, to_pair, bounds, ordered = pl.pallas_call(
        fetch_kernel,
        out_shape=[jax.ShapeDtypeStruct(x.shape, x.dtype) for x in inputs[:5]]
        + [jax.ShapeDtypeStruct(shape, F32) for shape in shapes],
        in_specs=[pl.BlockSpec(memory_space=pltpu.HBM)] * 8,
        scratch_shapes=[pltpu.VMEM(x.shape, x.dtype) for x in inputs[5:]]
        + [pltpu.SemaphoreType.DMA((8,))],
        compiler_params=pltpu.CompilerParams(vmem_limit_bytes=16 * 1024 * 1024),
        cost_estimate=pl.CostEstimate(flops=20000, bytes_accessed=500000, transcendentals=0),
    )(*[pltpu.with_memory_space_constraint(x, pltpu.HBM) for x in inputs])
    from_other = lax.ppermute(to_other, "slab", others)
    from_pair = lax.all_gather(to_pair, "slab", axis_index_groups=cores)
    mat, source, panel = call(
        matrix_kernel, [(MAT_LEVELS * CX, NY), flat, (16, LANES)], flops=5000000
    )(p, u, v, w, flags, bounds, ordered)
    send, offsets = call(pack_kernel, [(COLS * SEND_ROWS, LANES), ((CZ - 2) * CX, NY)])(
        mat, source, from_other, from_pair, w, panel, bounds, ordered
    )
    recv = exchange(send, COLS)
    back = call(
        owner_kernel,
        [(OWNERS * BACK_ROWS, LANES)],
        [
            (2, 40, LANES),
            (2, 16, LANES),
            (COLS * BACK_ROWS, LANES),
            (COLS * 16, LANES),
            (2 * COLS, LANES),
            (2 * COLS * 16, LANES),
        ],
    )(recv)
    sets = [list(range(at, at + OWNERS)) for at in range(0, COLS, OWNERS)]
    back = exchange(back, OWNERS, sets)
    loads = call(load_kernel, [(1, LANES)])(back)
    loads_other = lax.ppermute(loads, "slab", others)
    loads_pair = lax.all_gather(loads, "slab", axis_index_groups=cores)
    pressure, velocity, section_loads = call(final_kernel, [flat, flat, (3, SEC_DEV)])(
        back, mat, offsets, w, loads, loads_pair, loads_other
    )
    return pressure.reshape(p_star.shape), velocity.reshape(p_star.shape), section_loads


def solution(mesh):
    in_specs = (
        P("col", "slab", None),
        P("col", "slab", None),
        P("col", "slab", None),
        P("col", "slab", None),
        P("col", "slab", None),
        P(("col", "slab")),
        P(("col", "slab")),
        P(None, ("col", "slab")),
    )
    out_specs = (P("col", "slab", None), P("col", "slab", None), P(None, "slab"))
    return jax.shard_map(
        per_device, mesh=mesh, in_specs=in_specs, out_specs=out_specs, check_vma=False
    )
```
